128 devices in a mesh: dp: 8 (over z_lo, y), ctx: 16 (over z_hi, x, core).
Axes of the slice: x: 4, y: 4, z: 4 (z_hi: 2, z_lo: 2; z = z_hi * 2 + z_lo), core: 2. Of those that a mesh axis runs over, the one named last changes fastest.
Arguments:
- tokens: float32 [8, 2048, 768], P('dp', 'ctx'), may hold values from -6 to 6
- cotangent: float32 [8, 2048, 768], P('dp', 'ctx'), may hold values from -6 to 6
- w_qkv: bfloat16 [1, 768, 2304], P(None, ('dp', 'ctx')), may hold values from -0.21875 to 0.21875
- w_out: bfloat16 [1, 768, 768], P(None, ('dp', 'ctx')), may hold values from -0.875 to 0.875
- w_fc: bfloat16 [1, 768, 3072], P(None, ('dp', 'ctx')), may hold values from -0.21875 to 0.21875
- w_proj: bfloat16 [1, 3072, 768], P(None, ('dp', 'ctx')), may hold values from -0.109375 to 0.109375
- gains: bfloat16 [1, 2, 768], P(None, None, ('dp', 'ctx')), may hold values from 0.5 to 1.5
- biases: bfloat16 [1, 6, 768], P(None, None, ('dp', 'ctx')), may hold values from -2 to 2
- fc_bias: bfloat16 [1, 3072], P(None, ('dp', 'ctx')), may hold values from -2 to 2
Outputs:
- final: float32 [8, 2048, 768], P('dp', 'ctx')
- input_grad: float32 [8, 2048, 768], P('dp', 'ctx')
- grad_qkv: float32 [1, 768, 2304], P(None, ('dp', 'ctx'))
- grad_out: float32 [1, 768, 768], P(None, ('dp', 'ctx'))
- grad_fc: float32 [1, 768, 3072], P(None, ('dp', 'ctx'))
- grad_proj: float32 [1, 3072, 768], P(None, ('dp', 'ctx'))
- grad_gains: float32 [1, 2, 768], P(None, None, ('dp', 'ctx'))
- grad_biases: float32 [1, 6, 768], P(None, None, ('dp', 'ctx'))
- grad_fc_bias: float32 [1, 3072], P(None, ('dp', 'ctx'))
The draws below stay inside these ranges and needn't reach their ends.
All inputs are finite; a program needn't handle non-finite values.
Results may differ from the reference program's by a relative error of at most 0.025.
Values may be sent and summed in bfloat16 or wider, within the bound.
A program may use at most 128 MiB of HBM per device.

```python
import jax
import jax.numpy as jnp
from jax import lax

D = 768
FF = 3072
HEAD = 64
LAYERS = 1
BLK = 128
BATCH = 8
LENGTH = 2048
N_CTX = 16


def block_scale(stream_key, extent, pieces, low, high):
    loudness = 1.0
    for dim, blocks in pieces:
        steps = jax.random.uniform(jax.random.fold_in(jax.random.fold_in(stream_key, 6), dim), (blocks,), jnp.float32, low / len(pieces), high / len(pieces))
        loudness = loudness * jnp.repeat(jnp.exp(steps), extent[dim] // blocks).reshape((-1,) + (1,) * (len(extent) - 1 - dim))
    return loudness


def normal_values(key, extent, width, reach, cuts=(), kind=jnp.bfloat16):
    entries = width * jax.random.normal(key, extent, jnp.float32)
    if cuts:
        entries = entries * block_scale(key, extent, cuts, -0.22, 0.18)
    return jnp.clip(entries, -reach, reach).astype(kind)


def setup_inputs(seed: int = 0) -> dict:
    seeds = jax.random.split(jax.random.key(seed), 10)
    return {
        "tokens": normal_values(seeds[0], (BATCH, LENGTH, D), 1.0, 6.0, ((0, 8), (1, 16)), jnp.float32),
        "cotangent": normal_values(seeds[1], (BATCH, LENGTH, D), 1.0, 6.0, ((0, 8), (1, 16)), jnp.float32),
        "w_qkv": normal_values(seeds[2], (LAYERS, D, 3 * D), D ** -0.5, 0.21875, ((1, 128),)),
        "w_out": normal_values(seeds[3], (LAYERS, D, D), (D // 16) ** -0.5, 0.875, ((1, 128),)),
        "w_fc": normal_values(seeds[4], (LAYERS, D, FF), D ** -0.5, 0.21875, ((1, 128),)),
        "w_proj": normal_values(seeds[5], (LAYERS, FF, D), FF ** -0.5, 0.109375, ((1, 128),)),
        "gains": jnp.clip(1.0 + 0.1 * jax.random.normal(seeds[6], (LAYERS, 2, D), jnp.float32), 0.5, 1.5).astype(jnp.bfloat16),
        "biases": normal_values(seeds[7], (LAYERS, 6, D), 0.3, 2.0, ((2, 128),)),
        "fc_bias": normal_values(seeds[8], (LAYERS, FF), 0.3, 2.0, ((1, 128),)),
    }


@jax.custom_vjp
def low(v):
    return lax.optimization_barrier(v.astype(jnp.bfloat16)).astype(jnp.float32)

@jax.custom_vjp
def low_back(v):
    return v

def low_keep(v):
    return (low(v), None)

def low_pass(kept, grad):
    return (grad,)

def back_keep(v):
    return (v, None)

def back_low(kept, grad):
    return (low(grad),)
low.defvjp(low_keep, low_pass)
low_back.defvjp(back_keep, back_low)
norm_eps = 1e-05
masked_score = -1e+30

def row_positions(rows, block_len, axis_len):
    part = rows // block_len
    offset = rows % block_len
    half = block_len // 2
    return jnp.where(offset < half, part * half + offset, (2 * axis_len - 1 - part) * half + offset - half).astype(jnp.int32)

def layer_norm(values, gain, offset):
    center = values - lax.optimization_barrier(jnp.mean(values, axis=-1, keepdims=True))
    spread = lax.optimization_barrier(jnp.mean(center * center, axis=-1, keepdims=True))
    return center * lax.rsqrt(spread + norm_eps) * gain + offset

def matmul_high(left, right):
    return jnp.einsum('bld,de->ble', left, right, precision=lax.Precision.HIGHEST)

def attend(query, keys, values):
    scores = jnp.einsum('qhd,khd->hqk', query, keys, precision=lax.Precision.HIGHEST) * HEAD ** (-0.5)
    scores = low_back(scores)
    position = row_positions(jnp.arange(query.shape[0], dtype=jnp.int32), BLK, N_CTX)
    allowed = position[:, None] >= position[None, :]
    scores = jnp.where(allowed[None], scores, masked_score)
    probs = jax.nn.softmax(scores, axis=-1)
    return jnp.einsum('hqk,khd->qhd', low(probs), values, precision=lax.Precision.HIGHEST)

def forward(tokens, w_qkv, w_out, w_fc, w_proj, gains, biases, fc_bias):
    state = tokens
    batch_n, seq_len = (tokens.shape[0], tokens.shape[1])
    for layer_idx in range(LAYERS):
        normed_one = low(layer_norm(state, gains[layer_idx, 0], biases[layer_idx, 0]))
        projected = matmul_high(normed_one, w_qkv[layer_idx])
        query = low(low_back(projected[..., :D] + biases[layer_idx, 1]))
        keys = low(low_back(projected[..., D:2 * D]))
        values = low(low_back(projected[..., 2 * D:] + biases[layer_idx, 2]))
        split = (batch_n, seq_len, D // HEAD, HEAD)
        attended = lax.map(lambda trio: jax.checkpoint(attend)(*trio), (query.reshape(split), keys.reshape(split), values.reshape(split)))
        attended = low(low_back(attended.reshape(batch_n, seq_len, D)))
        middle = state + low_back(matmul_high(attended, w_out[layer_idx]) + biases[layer_idx, 3])
        normed_two = low(layer_norm(middle, gains[layer_idx, 1], biases[layer_idx, 4]))
        hidden_pre = low_back(matmul_high(normed_two, w_fc[layer_idx]) + fc_bias[layer_idx])
        activated = low(jax.nn.gelu(hidden_pre, approximate=True))
        state = middle + low_back(matmul_high(activated, w_proj[layer_idx]) + biases[layer_idx, 5])
    return state

def reference(tokens, cotangent, w_qkv, w_out, w_fc, w_proj, gains, biases, fc_bias):
    params = [w_qkv, w_out, w_fc, w_proj, gains, biases, fc_bias]
    params = [item.astype(jnp.float32) for item in params]
    final, back_fn = jax.vjp(forward, tokens, *params)
    grads = back_fn(cotangent)
    return (final, grads[0], grads[1], grads[2], grads[3], grads[4], grads[5], grads[6], grads[7])
```

```python
import functools

import jax
import jax.numpy as jnp
import numpy as np
from jax import lax
from jax.experimental import pallas as pl
from jax.experimental.pallas import tpu as pltpu
from jax.sharding import PartitionSpec as P

BF = jnp.bfloat16
F32 = jnp.float32
MESH = pl.DeviceIdType.MESH
VMEM = pltpu.VMEM
ALL = slice(None)
AXES = ("x", "y", "z")
GATHER_ORDER = (("x", "y", "z"), ("y", "z", "x"), ("z", "x", "y"))
SHAPE_Q = (4, 12, 2, 4, 2, 48, 128)
SHAPE_P = (6, 2, 4, 2, 4, 48, 128)
SHAPE_V = (2, 4, 2, 4, 2, 16, 128)


def place():
    dp = lax.axis_index("dp")
    ctx = lax.axis_index("ctx")
    at = {
        "x": lax.rem(lax.div(ctx, 2), 4),
        "y": lax.rem(dp, 4),
        "z": lax.div(ctx, 8) * 2 + lax.div(dp, 4),
    }
    return at, lax.rem(ctx, 2)


def device(at, core):
    return {
        "dp": lax.rem(at["z"], 2) * 4 + at["y"],
        "ctx": lax.div(at["z"], 2) * 8 + at["x"] * 2 + core,
    }


def beside(at, axis, distance):
    moved = dict(at)
    moved[axis] = lax.rem(at[axis] + (distance + 4), 4)
    return moved


def split_z(z):
    if isinstance(z, tuple):
        return pl.ds(z[1], 1), ALL
    if isinstance(z, slice):
        return ALL, ALL
    return lax.rem(z, 2), lax.div(z, 2)


def line(value):
    return pl.ds(2 * value[1], 2) if isinstance(value, tuple) else value


def views(refs, part, sel, core, cut=None):
    ref_q, ref_p, ref_v = refs
    x, y = line(sel["x"]), line(sel["y"])
    zl, zh = split_z(sel["z"])
    first, count = (0, 3) if cut is None else ((0, 2), (2, 1))[cut]
    if part < 2:
        start = first + 3 * part + (0 if core is None else 6 * core)
        return [ref_q.at[x, pl.ds(start, count), zl, y, zh]]
    start = first + (0 if core is None else 3 * core)
    found = [ref_p.at[pl.ds(start, count), zl, y, zh, x]]
    if cut != 1:
        found.append(ref_v.at[zl, y, zh, x] if core is None else ref_v.at[zl, y, zh, x, core])
    return found


def greet(targets):
    barrier = pltpu.get_barrier_semaphore()
    for target in targets:
        pl.semaphore_signal(barrier, inc=1, device_id=target, device_id_type=MESH)
    pl.semaphore_wait(barrier, len(targets))


class Mail:
    def __init__(self, send_sem, recv_sem):
        self.send_sem, self.recv_sem, self.used, self.sent = send_sem, recv_sem, 0, []

    def send(self, sources, targets, device_id):
        keys = []
        for source, target in zip(sources, targets):
            copy = pltpu.make_async_remote_copy(
                src_ref=source,
                dst_ref=target,
                send_sem=self.send_sem.at[self.used],
                recv_sem=self.recv_sem.at[self.used],
                device_id=device_id,
                device_id_type=MESH,
            )
            copy.start()
            self.sent.append(copy)
            keys.append(self.used)
            self.used += 1
        return keys

    def receive(self, keys, arrivals, device_id):
        for key, arrival in zip(keys, arrivals):
            pltpu.make_async_remote_copy(
                src_ref=arrival,
                dst_ref=arrival,
                send_sem=self.send_sem.at[key],
                recv_sem=self.recv_sem.at[key],
                device_id=device_id,
                device_id_type=MESH,
            ).wait_recv()

    def finish(self):
        for copy in self.sent:
            copy.wait_send()


def group_and_neighbours(at, core):
    found = []
    spot = at["x"] * 2 + core
    for step in range(1, 8):
        other = lax.rem(spot + step, 8)
        found.append(device({**at, "x": lax.div(other, 2)}, lax.rem(other, 2)))
    for axis in ("y", "z"):
        for distance in (-1, 1):
            found.append(device(beside(at, axis, distance), core))
    return found


def gather_kernel(
    wq, wp, wv, place_q, place_p, all_q, all_p, all_v, in_q, in_p, own_q, own_p, send_sem, recv_sem, local_sem
):
    at, core = place()
    greet(group_and_neighbours(at, core))
    mail = Mail(send_sem, recv_sem)
    spot = at["x"] * 2 + core
    twin = device(at, 1 - core)

    waits = []
    for step in range(1, 8):
        other = lax.rem(spot + step, 8)
        source = lax.rem(spot + 8 - step, 8)
        target = device({**at, "x": lax.div(other, 2)}, lax.rem(other, 2))
        waits.append((mail.send([wq.at[other]], [in_q.at[spot]], target), [in_q.at[source]], target))
    waits.append((mail.send([wp.at[1 - core]], [in_p.at[core]], twin), [in_p.at[1 - core]], twin))
    in_q[spot] = wq[spot]
    in_p[core] = wp[core]
    for wait in waits:
        mail.receive(*wait)
    rows = jnp.dot(place_q[...], in_q[...].reshape(128, 768), preferred_element_type=F32).astype(BF)
    for tile in range(6):
        own_q[tile] = rows[:, 128 * tile : 128 * tile + 128]
    rows = jnp.dot(place_p[...], in_p[...].reshape(64, 384), preferred_element_type=F32).astype(BF)
    for tile in range(3):
        own_p[tile] = rows[:, 128 * tile : 128 * tile + 128]

    whole = (all_q, all_p, all_v)
    own = ([own_q.at[pl.ds(0, 3)]], [own_q.at[pl.ds(3, 3)]], [own_p, wv])
    local = []
    for part in range(3):
        for source, target in zip(own[part], views(whole, part, at, core)):
            copy = pltpu.make_async_copy(source, target, local_sem.at[len(local)])
            copy.start()
            local.append(copy)

    twin_keys = []

    def to_twin(part, sel):
        mine = views(whole, part, sel, core)
        twin_keys.append((mail.send(mine, mine, twin), views(whole, part, sel, 1 - core), twin))

    for phase in range(3):
        started = []
        for part in range(3):
            order = GATHER_ORDER[part]
            axis = order[phase]
            sel = dict(at)
            for done in order[:phase]:
                sel[done] = ALL
            mine = views(whole, part, sel, core)
            source = own[part] if phase == 0 else mine
            keys = []
            for distance in (1, -1):
                target = device(beside(at, axis, distance), core)
                keys.append(mail.send(source, mine, target))
            started.append((sel, keys))
        if phase == 0:
            for copy in local:
                copy.wait()
        forwards = []
        for part in range(3):
            order = GATHER_ORDER[part]
            axis = order[phase]
            sel, keys = started[part]
            pending = []
            for half, distance, key in ((0, 1, keys[0]), (1, -1, keys[1])):
                target = device(beside(at, axis, distance), core)
                arrived = beside(sel, axis, -distance)
                mail.receive(key, views(whole, part, arrived, core), target)
                far = beside(sel, axis, 2)
                if phase == 0:
                    moving = views(whole, part, arrived, core, cut=half)
                    coming = views(whole, part, far, core, cut=half)
                else:
                    arrived = {**arrived, order[0]: ("half", half)}
                    far = {**far, order[0]: ("half", half)}
                    moving = views(whole, part, arrived, core)
                    coming = views(whole, part, far, core)
                pending.append((mail.send(moving, moving, target), coming, target))
            if phase > 0:
                to_twin(part, beside(sel, axis, 1))
                to_twin(part, beside(sel, axis, -1))
            forwards.append(pending)
        for part in range(3):
            axis = GATHER_ORDER[part][phase]
            sel, _ = started[part]
            for wait in forwards[part]:
                mail.receive(*wait)
            to_twin(part, {**sel, axis: ALL} if phase == 0 else beside(sel, axis, 2))
    for wait in twin_keys:
        mail.receive(*wait)
    mail.finish()


def place_rows(groups, rows, padded):
    found = np.zeros((groups * rows, groups * padded), np.float32)
    for group in range(groups):
        for row in range(rows):
            found[group * rows + row, group * padded + row] = 1
    return found


def gather_weights(w_qkv, w_out, w_fc, w_proj, gains, biases, fc_bias):
    joint = jnp.concatenate([w_qkv[0], w_out[0], w_fc[0]], axis=1).reshape(6, 8, 768)
    wq = jnp.pad(jnp.transpose(joint, (1, 0, 2)), ((0, 0), (0, 10), (0, 0)))
    wp = jnp.pad(jnp.transpose(w_proj[0].reshape(24, 2, 384), (1, 0, 2)), ((0, 0), (0, 8), (0, 0)))
    small = jnp.pad(jnp.concatenate([gains[0], biases[0]], axis=0), ((0, 0), (0, 122)))
    wv = jnp.concatenate([small, jnp.pad(fc_bias, ((0, 0), (0, 104))), jnp.zeros((7, 128), BF)], axis=0)
    spaces = [pl.BlockSpec(memory_space=VMEM)] * 5
    return pl.pallas_call(
        gather_kernel,
        out_shape=[jax.ShapeDtypeStruct(shape, BF) for shape in (SHAPE_Q, SHAPE_P, SHAPE_V)],
        in_specs=spaces,
        out_specs=[pl.BlockSpec(memory_space=pl.ANY)] * 3,
        scratch_shapes=[
            VMEM((8, 16, 768), BF),
            VMEM((2, 32, 384), BF),
            VMEM((6, 48, 128), BF),
            VMEM((3, 48, 128), BF),
            pltpu.SemaphoreType.DMA((96,)),
            pltpu.SemaphoreType.DMA((96,)),
            pltpu.SemaphoreType.DMA((4,)),
        ],
        compiler_params=pltpu.CompilerParams(
            collective_id=0, has_side_effects=True, vmem_limit_bytes=16 * 1024 * 1024
        ),
        name="gather_weights",
    )(
        wq,
        wp,
        wv,
        jnp.asarray(place_rows(8, 6, 16), BF),
        jnp.asarray(place_rows(2, 24, 32), BF),
    )
REDUCE_ORDER = tuple(order[::-1] for order in GATHER_ORDER)


def added(target, *terms):
    if len(target.shape) == 2:
        total = target[...].astype(F32)
        for term in terms:
            total = total + term[...].astype(F32)
        target[...] = total.astype(BF)
        return
    count = target.shape[0]

    def step(i, carry):
        total = target[i].astype(F32)
        for term in terms:
            total = total + term[i].astype(F32)
        target[i] = total.astype(BF)
        return carry

    lax.fori_loop(0, count, step, 0)


def block_shapes(part, gone, cut, half_axis):
    extent = {axis: 1 if axis in gone else 4 for axis in AXES}
    if half_axis is not None:
        extent[half_axis] = 2
    count = 3 if cut is None else (2, 1)[cut]
    if extent["z"] == 1:
        z_dims = ()
    else:
        z_dims = (extent["z"] // 2, 2)
    lead = lambda name: () if extent[name] == 1 else (extent[name],)
    zl = z_dims[:1]
    zh = z_dims[1:]
    if part < 2:
        return [lead("x") + (count,) + zl + lead("y") + zh + (48, 128)]
    found = [(count,) + zl + lead("y") + zh + lead("x") + (48, 128)]
    if cut != 1:
        found.append(zl + lead("y") + zh + lead("x") + (16, 128))
    return found


def reduce_buffers():
    found = []
    for phase in range(3):
        for part in range(3):
            order = REDUCE_ORDER[part]
            gone = order[: phase + 1]
            half_axis = order[2] if phase < 2 else None
            for half in range(2):
                cut = half if phase == 2 else None
                shapes = block_shapes(part, gone, cut, half_axis)
                for _ in range(3):
                    found.append(shapes)
    return found


def reduce_kernel(*refs):
    shapes = reduce_buffers()
    grads = refs[:3]
    spread_q, spread_p = refs[3:5]
    out_q, out_p, out_v = refs[5:8]
    acc = refs[8:11]
    flat_at = 11
    buffers = []
    for group in shapes:
        buffers.append(refs[flat_at : flat_at + len(group)])
        flat_at += len(group)
    last_q, last_p, in_q, in_p, send_sem, recv_sem = refs[flat_at:]

    at, core = place()
    greet(group_and_neighbours(at, core))
    mail = Mail(send_sem, recv_sem)
    spot = at["x"] * 2 + core
    twin = device(at, 1 - core)
    every = {axis: ALL for axis in AXES}

    waits = []
    for part in range(3):
        arrivals = views(acc, part, every, None)
        waits.append((mail.send(views(grads, part, every, 1 - core), arrivals, twin), arrivals, twin))

    def halves(part, phase, sel, half):
        if phase == 2:
            return views(acc, part, sel, None, cut=half)
        return views(acc, part, {**sel, REDUCE_ORDER[part][2]: ("half", half)}, None)

    for phase in range(3):
        first = []
        for part in range(3):
            if phase == 0:
                mail.receive(*waits[part])
                for total, term in zip(views(acc, part, every, None), views(grads, part, every, core)):
                    added(total, term)
            axis = REDUCE_ORDER[part][phase]
            sel = dict(at)
            for later in REDUCE_ORDER[part][phase + 1 :]:
                sel[later] = ALL
            base = (phase * 3 + part) * 6
            landing = [buffers[base + 3 * half : base + 3 * half + 3] for half in range(2)]
            far, up, down = beside(sel, axis, 2), beside(sel, axis, 1), beside(sel, axis, -1)
            plus = device(beside(at, axis, 1), core)
            minus = device(beside(at, axis, -1), core)
            far_keys = [
                mail.send(halves(part, phase, far, 0), landing[0][0], plus),
                mail.send(halves(part, phase, far, 1), landing[1][0], minus),
            ]
            up_keys = mail.send(halves(part, phase, up, 1), landing[1][1], plus)
            down_keys = mail.send(halves(part, phase, down, 0), landing[0][2], minus)
            first.append((sel, landing, up, down, plus, minus, far_keys, up_keys, down_keys))
        second = []
        for part in range(3):
            sel, landing, up, down, plus, minus, far_keys, _, _ = first[part]
            mail.receive(far_keys[0], landing[0][0], plus)
            for total, term in zip(halves(part, phase, up, 0), landing[0][0]):
                added(total, term)
            plus_keys = mail.send(halves(part, phase, up, 0), landing[0][1], plus)
            mail.receive(far_keys[1], landing[1][0], minus)
            for total, term in zip(halves(part, phase, down, 1), landing[1][0]):
                added(total, term)
            minus_keys = mail.send(halves(part, phase, down, 1), landing[1][2], minus)
            second.append((plus_keys, minus_keys))
        for part in range(3):
            sel, landing, up, down, plus, minus, _, up_keys, down_keys = first[part]
            plus_keys, minus_keys = second[part]
            mail.receive(up_keys, landing[1][1], plus)
            mail.receive(minus_keys, landing[1][2], minus)
            for total, one, two in zip(halves(part, phase, sel, 1), landing[1][1], landing[1][2]):
                added(total, one, two)
            mail.receive(plus_keys, landing[0][1], plus)
            mail.receive(down_keys, landing[0][2], minus)
            for total, one, two in zip(halves(part, phase, sel, 0), landing[0][1], landing[0][2]):
                added(total, one, two)

    mine = [views(acc, part, at, None) for part in range(3)]
    rows = jnp.concatenate([mine[tile // 3][0][tile % 3] for tile in range(6)], axis=1)
    last_q[...] = jnp.dot(spread_q[...], rows, preferred_element_type=F32).astype(BF).reshape(8, 16, 768)
    rows = jnp.concatenate([mine[2][0][tile] for tile in range(3)], axis=1)
    last_p[...] = jnp.dot(spread_p[...], rows, preferred_element_type=F32).astype(BF).reshape(2, 32, 384)
    waits = []
    for step in range(1, 8):
        other = lax.rem(spot + step, 8)
        source = lax.rem(spot + 8 - step, 8)
        target = device({**at, "x": lax.div(other, 2)}, lax.rem(other, 2))
        waits.append((mail.send([last_q.at[other]], [in_q.at[spot]], target), [in_q.at[source]], target))
    waits.append((mail.send([last_p.at[1 - core]], [in_p.at[core]], twin), [in_p.at[1 - core]], twin))
    in_q[spot] = last_q[spot]
    in_p[core] = last_p[core]
    out_v[...] = mine[2][1][...].astype(F32)
    for wait in waits:
        mail.receive(*wait)
    for group in range(8):
        out_q[:, 768 * group : 768 * group + 768] = in_q[group].astype(F32)[:8]
    for half in range(2):
        out_p[:, 384 * half : 384 * half + 384] = in_p[half].astype(F32)[:24]
    mail.finish()


def reduce_grads(grad_q, grad_p, grad_v):
    scratch = [VMEM((4, 6, 2, 4, 2, 48, 128), BF), VMEM((3, 2, 4, 2, 4, 48, 128), BF), VMEM((2, 4, 2, 4, 16, 128), BF)]
    for group in reduce_buffers():
        scratch += [VMEM(shape, BF) for shape in group]
    scratch += [
        VMEM((8, 16, 768), BF),
        VMEM((2, 32, 384), BF),
        VMEM((8, 16, 768), BF),
        VMEM((2, 32, 384), BF),
        pltpu.SemaphoreType.DMA((100,)),
        pltpu.SemaphoreType.DMA((100,)),
    ]
    return pl.pallas_call(
        reduce_kernel,
        out_shape=[
            jax.ShapeDtypeStruct((8, 6144), F32),
            jax.ShapeDtypeStruct((24, 768), F32),
            jax.ShapeDtypeStruct((16, 128), F32),
        ],
        in_specs=[pl.BlockSpec(memory_space=VMEM)] * 5,
        out_specs=[pl.BlockSpec(memory_space=VMEM)] * 3,
        scratch_shapes=scratch,
        compiler_params=pltpu.CompilerParams(
            collective_id=1, has_side_effects=True, vmem_limit_bytes=56 * 1024 * 1024
        ),
        name="reduce_grads",
    )(
        grad_q,
        grad_p,
        grad_v,
        jnp.asarray(place_rows(8, 6, 16).T, BF),
        jnp.asarray(place_rows(2, 24, 32).T, BF),
    )
HEADS = 12
WIDTH = 768
HIDDEN = 3072
NORM_EPS = 1e-05
MASKED = -1e30
MEGA = 1024 * 1024


def dot(left, right):
    return jnp.dot(left, right, preferred_element_type=F32)


def dot_right_t(left, right):
    return lax.dot_general(left, right, (((1,), (1,)), ((), ())), preferred_element_type=F32)


def dot_left_t(left, right):
    return lax.dot_general(left, right, (((0,), (0,)), ((), ())), preferred_element_type=F32)


def mean_last(values):
    return jnp.mean(values, axis=-1, keepdims=True)


def normalize(values):
    center = values - mean_last(values)
    factor = lax.rsqrt(mean_last(center * center) + NORM_EPS)
    return center * factor, factor


def norm_back(d_norm, xhat, factor, gain):
    e = d_norm * gain
    return factor * (e - mean_last(e) - xhat * mean_last(e * xhat))


def owner_mask(rows, extra, columns, each):
    shape = (128, extra, columns) if extra else (128, columns)
    owner = lax.broadcasted_iota(jnp.int32, shape, 0) * each
    column = lax.broadcasted_iota(jnp.int32, shape, len(shape) - 1)
    return (column >= owner) & (column < owner + each)


def spread_matrix(columns, each):
    found = np.zeros((128, columns), np.float32)
    found[np.arange(columns) % each, np.arange(columns)] = 1
    return found


def fetch(source, target, sem):
    copy = pltpu.make_async_copy(source, target, sem)
    copy.start()
    return copy


def query_kernel(x, small, spread, spread_fc, all_q, normed, qkv_t, vectors, hidden_bias, w, sem):
    coming = fetch(all_q.at[pl.ds(0, 18)], w, sem)
    small_rows = small[...]
    wide = dot(small_rows, spread[...]).reshape(128, 16, WIDTH)
    found = jnp.sum(jnp.where(owner_mask(128, 16, WIDTH, 6), wide, 0.0), axis=0)
    vectors[...] = found
    tall = small_rows.astype(F32).reshape(128, 16, 128)
    pick = lax.broadcasted_iota(jnp.int32, (128, 16, 128), 1) == 8
    fc_rows = jnp.sum(jnp.where(pick, tall, 0.0), axis=1).astype(BF)
    wide = dot(fc_rows, spread_fc[...])
    hidden_bias[...] = jnp.sum(jnp.where(owner_mask(128, 0, HIDDEN, 24), wide, 0.0), axis=0, keepdims=True)
    xhat, _ = normalize(x[...])
    rows = (xhat * found[0:1] + found[2:3]).astype(BF)
    normed[...] = rows
    coming.wait()
    for pair in range(9):
        kind, first = pair // 3, (pair % 3) * 256
        out = dot(rows, jnp.concatenate([w[2 * pair], w[2 * pair + 1]], axis=1))
        if kind != 1:
            out = out + found[3 + kind // 2 : 4 + kind // 2, first : first + 256]
        out = out.astype(BF).astype(F32).T.astype(BF)
        for head in range(4):
            qkv_t[first // 64 + head, 64 * kind : 64 * kind + 64, :] = out[64 * head : 64 * head + 64]


def local_call(kernel, name, ins, outs, scratch=(), limit=56, in_specs=None, flops=0):
    return pl.pallas_call(
        kernel,
        out_shape=[jax.ShapeDtypeStruct(shape, kind) for shape, kind in outs],
        in_specs=in_specs or [pl.BlockSpec(memory_space=VMEM)] * len(ins),
        out_specs=[pl.BlockSpec(memory_space=VMEM)] * len(outs),
        scratch_shapes=list(scratch),
        compiler_params=pltpu.CompilerParams(vmem_limit_bytes=limit * MEGA),
        name=name,
    )(*ins)


def ctx_peers(ctx):
    return [lax.rem(ctx + step, 16) for step in range(1, 16)]


def to_heads_kernel(block, out, send_sem, recv_sem, local_sem):
    ctx = lax.axis_index("ctx")
    greet([{"ctx": peer} for peer in ctx_peers(ctx)])
    span = lambda who: out.at[:, pl.ds(pl.multiple_of(who * 128, 128), 128)]
    for step in range(1, 16):
        peer = lax.rem(ctx + step, 16)

        @pl.when(peer < HEADS)
        def _():
            pltpu.make_async_remote_copy(
                block.at[peer], span(ctx), send_sem.at[step], recv_sem.at[step],
                device_id={"ctx": peer}, device_id_type=MESH,
            ).start()

    @pl.when(ctx < HEADS)
    def _():
        copy = pltpu.make_async_copy(block.at[ctx], span(ctx), local_sem)
        copy.start()
        for step in range(1, 16):
            source = lax.rem(ctx + 16 - step, 16)
            pltpu.make_async_remote_copy(
                span(source), span(source), send_sem.at[step], recv_sem.at[step],
                device_id={"ctx": source}, device_id_type=MESH,
            ).wait_recv()
        copy.wait()

    for step in range(1, 16):
        peer = lax.rem(ctx + step, 16)

        @pl.when(peer < HEADS)
        def _():
            pltpu.make_async_remote_copy(
                block.at[peer], span(ctx), send_sem.at[step], recv_sem.at[step],
                device_id={"ctx": peer}, device_id_type=MESH,
            ).wait_send()


def from_heads_kernel(blocks, out, send_sem, recv_sem, local_sem):
    ctx = lax.axis_index("ctx")
    greet([{"ctx": peer} for peer in ctx_peers(ctx)])

    @pl.when(ctx < HEADS)
    def _():
        for step in range(1, 16):
            peer = lax.rem(ctx + step, 16)
            pltpu.make_async_remote_copy(
                blocks.at[peer], out.at[ctx], send_sem.at[step], recv_sem.at[step],
                device_id={"ctx": peer}, device_id_type=MESH,
            ).start()
        copy = pltpu.make_async_copy(blocks.at[ctx], out.at[ctx], local_sem)
        copy.start()
        copy.wait()

    for step in range(1, 16):
        source = lax.rem(ctx + 16 - step, 16)

        @pl.when(source < HEADS)
        def _():
            pltpu.make_async_remote_copy(
                out.at[source], out.at[source], send_sem.at[step], recv_sem.at[step],
                device_id={"ctx": source}, device_id_type=MESH,
            ).wait_recv()

    @pl.when(ctx < HEADS)
    def _():
        for step in range(1, 16):
            peer = lax.rem(ctx + step, 16)
            pltpu.make_async_remote_copy(
                blocks.at[peer], out.at[ctx], send_sem.at[step], recv_sem.at[step],
                device_id={"ctx": peer}, device_id_type=MESH,
            ).wait_send()


def exchange(kernel, name, collective_id, block, out_shape):
    return pl.pallas_call(
        kernel,
        out_shape=jax.ShapeDtypeStruct(out_shape, BF),
        in_specs=[pl.BlockSpec(memory_space=VMEM)],
        out_specs=pl.BlockSpec(memory_space=VMEM),
        scratch_shapes=[
            pltpu.SemaphoreType.DMA((16,)),
            pltpu.SemaphoreType.DMA((16,)),
            pltpu.SemaphoreType.DMA,
        ],
        compiler_params=pltpu.CompilerParams(
            collective_id=collective_id, has_side_effects=True, vmem_limit_bytes=16 * MEGA
        ),
        name=name,
    )(block)


def low_half(shape):
    return lax.broadcasted_iota(jnp.int32, shape, 1) < 64


def swap_halves(tile):
    return pltpu.roll(tile, 64, 1)


def position_tile(block, tile):
    if tile < 8:
        low, high = block(2 * tile), swap_halves(block(2 * tile + 1))
    else:
        low, high = swap_halves(block(31 - 2 * tile)), block(30 - 2 * tile)
    return jnp.where(low_half(low.shape), low, high)


def position_block(tile, block):
    early, late = tile(block // 2), tile((31 - block) // 2)
    if block % 2 == 0:
        return jnp.where(low_half(early.shape), early, late)
    return swap_halves(jnp.where(low_half(early.shape), late, early))


TILE = 256


def causal(scores, first):
    rows, columns = scores.shape
    key = lax.broadcasted_iota(jnp.int32, (rows, columns), 0)
    query = lax.broadcasted_iota(jnp.int32, (rows, columns), 1) + first
    return jnp.where(key <= query, scores, MASKED)


def attend_kernel(landed, ordered, natural, out_t, log_total, blocks):
    for tile in range(16):
        found = position_tile(lambda b: landed[:, 128 * b : 128 * b + 128].astype(F32), tile)
        found = jnp.concatenate([found[0:64] * 0.125, found[64:192]], axis=0)
        span = slice(128 * tile, 128 * tile + 128)
        ordered[:, span] = found.astype(BF)
        natural[span, :] = found.T.astype(BF)
    for step in range(2048 // TILE):
        first = TILE * step
        count = first + TILE
        span = slice(first, count)
        scores = dot(natural[0:count, 64:128], ordered[0:64, span])
        scores = causal(scores, first)
        best = jnp.max(scores, axis=0, keepdims=True)
        probs = jnp.exp(scores - best)
        total = jnp.sum(probs, axis=0, keepdims=True)
        out_t[:, span] = dot(ordered[128:192, 0:count], probs.astype(BF)) / total
        log_total[0:1, span] = best + jnp.log(total)
    for block in range(16):
        blocks[block] = position_block(lambda t: out_t[:, 128 * t : 128 * t + 128], block).astype(BF)


def attend_back_kernel(ordered, natural, out_t, log_total, landed, blocks, d_out, d_out_nat, d_t, d_keys, d_values):
    for tile in range(16):
        found = position_tile(lambda b: landed[:, 128 * b : 128 * b + 128].astype(F32), tile)
        span = slice(128 * tile, 128 * tile + 128)
        d_out[:, span] = found
        d_out_nat[span, :] = found.T.astype(BF)
    d_keys[...] = jnp.zeros_like(d_keys)
    d_values[...] = jnp.zeros_like(d_values)
    for step in range(2048 // TILE):
        first = TILE * step
        count = first + TILE
        span = slice(first, count)
        scores = causal(dot(natural[0:count, 64:128], ordered[0:64, span]), first)
        probs = jnp.exp(scores - log_total[0:1, span])
        d_here = d_out[:, span]
        delta = jnp.sum(d_here * out_t[:, span], axis=0, keepdims=True)
        d_probs = dot(natural[0:count, 128:192], d_here.astype(BF))
        d_scores = (probs * (d_probs - delta)).astype(BF)
        d_t[0:64, span] = dot(ordered[64:128, 0:count], d_scores) * 0.125
        d_keys[0:count, :] += dot(d_scores, natural[span, 0:64])
        d_values[0:count, :] += dot(probs.astype(BF), d_out_nat[span, :])
    for tile in range(16):
        span = slice(128 * tile, 128 * tile + 128)
        d_t[64:128, span] = d_keys[span, :].T
        d_t[128:192, span] = d_values[span, :].T
    for block in range(16):
        blocks[block] = position_block(lambda t: d_t[:, 128 * t : 128 * t + 128], block).astype(BF)


CHUNK = 4


def middle_kernel(
    x, cotangent, att_t, vectors, hidden_bias, all_q, all_p,
    final, d_middle, d_att_t, grad_q, grad_p, grad_vectors, grad_hidden,
    total, d_norm_two, w_rest, w_proj, sem_out, sem_fc, sem_proj,
):
    coming_out = fetch(all_q.at[pl.ds(18, 6)], w_rest.at[pl.ds(0, 6)], sem_out)
    coming_fc = fetch(all_q.at[pl.ds(24, 24)], w_rest.at[pl.ds(6, 24)], sem_fc)
    coming_proj = fetch(all_p, w_proj, sem_proj)
    wide = lambda ref, first, count: jnp.concatenate([ref[first + i] for i in range(count)], axis=1)
    rows_t = att_t[...]
    coming_out.wait()
    mat_out = wide(w_rest, 0, 6)
    attended = rows_t.astype(F32).T.astype(BF)
    middle = x[...] + dot(attended, mat_out) + vectors[5:6]
    xhat, factor = normalize(middle)
    normed = (xhat * vectors[1:2] + vectors[6:7]).astype(BF)
    normed_t = normed.astype(F32).T.astype(BF)
    gradient = cotangent[...]
    d_two = gradient.astype(BF)
    total[...] = jnp.zeros_like(total)
    d_norm_two[...] = jnp.zeros_like(d_norm_two)

    coming_fc.wait()
    coming_proj.wait()

    def chunk(i, carry):
        span = pl.ds(pl.multiple_of(i * CHUNK * 128, CHUNK * 128), CHUNK * 128)
        mat_fc = jnp.concatenate([w_rest[6 + i * CHUNK + j] for j in range(CHUNK)], axis=1)
        mat_proj = jnp.concatenate([w_proj[j, span] for j in range(6)], axis=1)
        pre = dot(normed, mat_fc) + hidden_bias[:, span]
        root = 0.7978845608028654
        inner = jnp.tanh(root * (pre + 0.044715 * (pre * pre * pre)))
        activated = (0.5 * pre * (1.0 + inner)).astype(BF)
        slope = 0.5 * (1.0 + inner) + 0.5 * pre * (1.0 - inner * inner) * (
            root * (1.0 + 3 * 0.044715 * (pre * pre))
        )
        total[...] += dot(activated, mat_proj)
        d_pre = (dot_right_t(d_two, mat_proj) * slope).astype(BF)
        grad_hidden[:, span] = jnp.sum(d_pre.astype(F32), axis=0, keepdims=True)
        d_norm_two[...] += dot_right_t(d_pre, mat_fc)
        grad_fc = dot(normed_t, d_pre).astype(BF)
        for j in range(CHUNK):
            grad_q[6 + i * CHUNK + j] = grad_fc[:, 128 * j : 128 * j + 128]
        grad_proj = dot_left_t(activated, d_two).astype(BF)
        for j in range(6):
            grad_p[j, span] = grad_proj[:, 128 * j : 128 * j + 128]
        return carry

    lax.fori_loop(0, 24 // CHUNK, chunk, 0)
    final[...] = middle + total[...] + vectors[7:8]
    d_norm = d_norm_two[...]
    d_mid = gradient + norm_back(d_norm, xhat, factor, vectors[1:2])
    d_middle[...] = d_mid
    d_one = d_mid.astype(BF)
    d_att_t[...] = dot_right_t(mat_out, d_one).astype(BF)
    grad_out = dot(rows_t, d_one).astype(BF)
    for j in range(6):
        grad_q[j] = grad_out[:, 128 * j : 128 * j + 128]
    sums = lambda values: jnp.sum(values, axis=0, keepdims=True)
    grad_vectors[...] = jnp.zeros_like(grad_vectors)
    grad_vectors[1:2] = sums(d_norm * xhat)
    grad_vectors[5:6] = sums(d_one.astype(F32))
    grad_vectors[6:7] = sums(d_norm)
    grad_vectors[7:8] = sums(d_two.astype(F32))


def last_kernel(
    x, normed, d_middle, d_qkv_t, vectors, grad_vectors, grad_hidden, spread, spread_fc, all_q,
    input_grad, grad_q, grad_small, d_qkv, w, sem,
):
    coming = fetch(all_q.at[pl.ds(0, 18)], w, sem)
    for head in range(HEADS):
        rows = d_qkv_t[head].astype(F32).T.astype(BF)
        for kind in range(3):
            first = WIDTH * kind + 64 * head
            d_qkv[:, first : first + 64] = rows[:, 64 * kind : 64 * kind + 64]
    normed_t = normed[...].astype(F32).T.astype(BF)
    d_norm = jnp.zeros((128, WIDTH), F32)
    coming.wait()
    for pair in range(9):
        part = d_qkv[:, 256 * pair : 256 * pair + 256]
        out = dot(normed_t, part).astype(BF)
        grad_q[2 * pair] = out[:, :128]
        grad_q[2 * pair + 1] = out[:, 128:]
        d_norm = d_norm + dot_right_t(part, jnp.concatenate([w[2 * pair], w[2 * pair + 1]], axis=1))
    xhat, factor = normalize(x[...])
    input_grad[...] = d_middle[...] + norm_back(d_norm, xhat, factor, vectors[0:1])
    sums = lambda values: jnp.sum(values, axis=0, keepdims=True)
    kinds = lambda kind: sums(d_qkv[:, WIDTH * kind : WIDTH * kind + WIDTH].astype(F32))
    row = lax.broadcasted_iota(jnp.int32, (16, WIDTH), 0)
    found = grad_vectors[...]
    for at, value in ((0, sums(d_norm * xhat)), (2, sums(d_norm)), (3, kinds(0)), (4, kinds(2))):
        found = jnp.where(row == at, value, found)
    wide = jnp.broadcast_to(found[None], (128, 16, WIDTH))
    wide = jnp.where(owner_mask(128, 16, WIDTH, 6), wide, 0.0).astype(BF).reshape(2048, WIDTH)
    small = dot_right_t(wide, spread[...]).reshape(128, 16, 128)
    wide = jnp.where(owner_mask(128, 0, HIDDEN, 24), jnp.broadcast_to(grad_hidden[...], (128, HIDDEN)), 0.0)
    hidden = dot_right_t(wide.astype(BF), spread_fc[...])
    place_at = lax.broadcasted_iota(jnp.int32, (128, 16, 128), 1) == 8
    small = jnp.where(place_at, hidden[:, None, :], small)
    grad_small[...] = small.astype(BF)


def local(tokens, cotangent, w_qkv, w_out, w_fc, w_proj, gains, biases, fc_bias):
    x = tokens[0]
    all_q, all_p, all_v = gather_weights(w_qkv, w_out, w_fc, w_proj, gains, biases, fc_bias)
    all_q = all_q.reshape(48, WIDTH, 128)
    all_p = all_p.reshape(6, HIDDEN, 128)
    small = all_v.reshape(2048, 128)
    spread = jnp.asarray(spread_matrix(WIDTH, 6), BF)
    spread_fc = jnp.asarray(spread_matrix(HIDDEN, 24), BF)
    whole = pl.BlockSpec(memory_space=VMEM)
    stay = pl.BlockSpec(memory_space=pl.ANY)
    first_w = [VMEM((18, WIDTH, 128), BF), pltpu.SemaphoreType.DMA]
    normed, qkv_t, vectors, hidden_bias = local_call(
        query_kernel,
        "query_keys_values",
        (x, small, spread, spread_fc, all_q),
        (((128, WIDTH), BF), ((HEADS, 192, 128), BF), ((16, WIDTH), F32), ((1, HIDDEN), F32)),
        scratch=first_w,
        in_specs=[whole] * 4 + [stay],
    )
    landed = exchange(to_heads_kernel, "rows_to_heads", 2, qkv_t, (192, 2048))
    ordered, natural, out_t, log_total, blocks = local_call(
        attend_kernel,
        "attend",
        (landed,),
        (((192, 2048), BF), ((2048, 192), BF), ((64, 2048), F32), ((8, 2048), F32), ((16, 64, 128), BF)),
    )
    att_t = exchange(from_heads_kernel, "heads_to_rows", 3, blocks, (HEADS, 64, 128)).reshape(WIDTH, 128)
    final, d_middle, d_att_t, grad_rest, grad_p, grad_vectors, grad_hidden = local_call(
        middle_kernel,
        "feed_forward_both_ways",
        (x, cotangent[0], att_t, vectors, hidden_bias, all_q, all_p),
        (
            ((128, WIDTH), F32),
            ((128, WIDTH), F32),
            ((WIDTH, 128), BF),
            ((30, WIDTH, 128), BF),
            ((6, HIDDEN, 128), BF),
            ((16, WIDTH), F32),
            ((1, HIDDEN), F32),
        ),
        scratch=[
            VMEM((128, WIDTH), F32),
            VMEM((128, WIDTH), F32),
            VMEM((30, WIDTH, 128), BF),
            VMEM((6, HIDDEN, 128), BF),
            pltpu.SemaphoreType.DMA,
            pltpu.SemaphoreType.DMA,
            pltpu.SemaphoreType.DMA,
        ],
        in_specs=[whole] * 5 + [stay, stay],
    )
    landed = exchange(to_heads_kernel, "gradient_to_heads", 4, d_att_t.reshape(HEADS, 64, 128), (64, 2048))
    (blocks,) = local_call(
        attend_back_kernel,
        "attend_back",
        (ordered, natural, out_t, log_total, landed),
        (((16, 192, 128), BF),),
        scratch=[
            VMEM((64, 2048), F32),
            VMEM((2048, 64), BF),
            VMEM((192, 2048), F32),
            VMEM((2048, 64), F32),
            VMEM((2048, 64), F32),
        ],
    )
    d_qkv_t = exchange(from_heads_kernel, "gradient_to_rows", 5, blocks, (HEADS, 192, 128))
    input_grad, grad_first, grad_small = local_call(
        last_kernel,
        "input_gradient",
        (x, normed, d_middle, d_qkv_t, vectors, grad_vectors, grad_hidden, spread, spread_fc, all_q),
        (((128, WIDTH), F32), ((18, WIDTH, 128), BF), ((128, 16, 128), BF)),
        scratch=[VMEM((128, 3 * WIDTH), BF)] + first_w,
        in_specs=[whole] * 9 + [stay],
    )
    grad_q = jnp.concatenate([grad_first, grad_rest], axis=0).reshape(SHAPE_Q)
    joint, proj, small = reduce_grads(grad_q, grad_p.reshape(SHAPE_P), grad_small.reshape(SHAPE_V))
    joint = joint[:6]
    return (
        final[None],
        input_grad[None],
        joint[None, :, : 3 * WIDTH],
        joint[None, :, 3 * WIDTH : 4 * WIDTH],
        joint[None, :, 4 * WIDTH :],
        proj[None],
        small[None, 0:2, :6],
        small[None, 2:8, :6],
        small[8:9, :24],
    )


def solution(mesh):
    rows = P("dp", "ctx", None)
    weight = P(None, ("dp", "ctx"), None)
    vector = P(None, None, ("dp", "ctx"))
    tail = (weight,) * 4 + (vector, vector, P(None, ("dp", "ctx")))
    return jax.shard_map(
        local, mesh=mesh, in_specs=(rows, rows) + tail, out_specs=(rows, rows) + tail, check_vma=False
    )
```

```python
import jax
import jax.numpy as jnp
import numpy as np
from jax import lax
from jax.experimental import pallas as pl
from jax.experimental.pallas import tpu as pltpu
from jax.sharding import PartitionSpec as P

BF = jnp.bfloat16
F32 = jnp.float32
MESH = pl.DeviceIdType.MESH
VMEM = pltpu.VMEM
ALL = slice(None)
AXES = ("x", "y", "z")
GATHER_ORDER = (("x", "y", "z"), ("y", "z", "x"), ("z", "x", "y"))
REDUCE_ORDER = tuple(order[::-1] for order in GATHER_ORDER)
SHAPES = ((4, 6, 2, 4, 2, 48, 128), (4, 12, 2, 4, 2, 48, 128), (2, 4, 2, 4, 2, 16, 128))
SUMS = ((4, 3, 2, 4, 2, 48, 128), (4, 6, 2, 4, 2, 48, 128), (2, 4, 2, 4, 16, 128))
ATTENTION = ((0, 0), (0, 1), (0, 2))
FORWARD = ((1, 0), (1, 1), (1, 2))
SMALL = ((2, 0),)
HEADS = 12
WIDTH = 768
HIDDEN = 3072
NORM_EPS = 1e-05
MASKED = -1e30
MEGA = 1024 * 1024
COPIES = 256


def place():
    dp = lax.axis_index("dp")
    ctx = lax.axis_index("ctx")
    at = {
        "x": lax.rem(lax.div(ctx, 2), 4),
        "y": lax.rem(dp, 4),
        "z": lax.div(ctx, 8) * 2 + lax.div(dp, 4),
    }
    return at, lax.rem(ctx, 2)


def device(at, core):
    return {
        "dp": lax.rem(at["z"], 2) * 4 + at["y"],
        "ctx": lax.div(at["z"], 2) * 8 + at["x"] * 2 + core,
    }


def beside(at, axis, distance):
    moved = dict(at)
    moved[axis] = lax.rem(at[axis] + (distance + 4), 4)
    return moved


def split_z(z):
    if isinstance(z, tuple):
        return pl.ds(z[1], 1), ALL
    if isinstance(z, slice):
        return ALL, ALL
    return lax.rem(z, 2), lax.div(z, 2)


def line(value):
    return pl.ds(2 * value[1], 2) if isinstance(value, tuple) else value


def view(refs, sub, sel, core):
    kind, tile = sub
    x, y = line(sel["x"]), line(sel["y"])
    zl, zh = split_z(sel["z"])
    if kind == 2:
        return refs[2].at[zl, y, zh, x] if core is None else refs[2].at[zl, y, zh, x, core]
    count = kind + 1
    start = count * tile + (0 if core is None else 3 * count * core)
    return refs[kind].at[x, pl.ds(start, count), zl, y, zh]


def block_shape(sub, gone, half_axis=None):
    extent = {axis: 1 if axis in gone else 4 for axis in AXES}
    if half_axis is not None:
        extent[half_axis] = 2
    lead = lambda name: () if extent[name] == 1 else (extent[name],)
    zl, zh = ((), ()) if extent["z"] == 1 else ((extent["z"] // 2,), (2,))
    if sub[0] == 2:
        return zl + lead("y") + zh + lead("x") + (16, 128)
    return lead("x") + (sub[0] + 1,) + zl + lead("y") + zh + (48, 128)


def landing_shapes():
    found = {}
    for sub in ATTENTION + FORWARD + SMALL:
        order = REDUCE_ORDER[sub[1]]
        for phase in range(3):
            gone = order[: phase + 1]
            if phase == 0 and sub[0] < 2:
                for half in range(2):
                    for use in range(3):
                        found[sub, phase, half, use] = block_shape(sub, gone, order[2])
            else:
                for use in range(3):
                    found[sub, phase, use] = block_shape(sub, gone)
    return found


def added(target, *terms):
    if len(target.shape) == 2:
        total = target[...].astype(F32)
        for term in terms:
            total = total + term[...].astype(F32)
        target[...] = total.astype(BF)
        return

    def step(i, carry):
        total = target[i].astype(F32)
        for term in terms:
            total = total + term[i].astype(F32)
        target[i] = total.astype(BF)
        return carry

    lax.fori_loop(0, target.shape[0], step, 0)


class Mail:
    def __init__(self, send_sem, recv_sem, anyone):
        self.send_sem, self.recv_sem, self.anyone = send_sem, recv_sem, anyone
        self.used, self.sent = 0, []

    def send(self, source, target, device_id):
        key = self.used
        copy = pltpu.make_async_remote_copy(
            src_ref=source,
            dst_ref=target,
            send_sem=self.send_sem.at[key],
            recv_sem=self.recv_sem.at[key],
            device_id=device_id,
            device_id_type=MESH,
        )
        copy.start()
        self.sent.append(copy)
        self.used += 1
        return key

    def receive(self, key, arrival):
        pltpu.make_async_remote_copy(
            src_ref=arrival,
            dst_ref=arrival,
            send_sem=self.send_sem.at[key],
            recv_sem=self.recv_sem.at[key],
            device_id=self.anyone,
            device_id_type=MESH,
        ).wait_recv()

    def finish(self):
        for copy in self.sent:
            copy.wait_send()
        self.sent = []


class Gather:
    def __init__(self, mail, refs, subs, at, core):
        self.mail, self.refs, self.subs, self.at, self.core = mail, refs, subs, at, core
        self.twin = device(at, 1 - core)
        self.pending, self.twins = [], []

    def sel(self, sub, phase):
        found = dict(self.at)
        for done in GATHER_ORDER[sub[1]][:phase]:
            found[done] = ALL
        return found

    def mine(self, sub, sel):
        return view(self.refs, sub, sel, self.core)

    def peer(self, axis, distance):
        return device(beside(self.at, axis, distance), self.core)

    def to_twin(self, sub, sel):
        source = self.mine(sub, sel)
        self.twins.append((self.mail.send(source, source, self.twin), view(self.refs, sub, sel, 1 - self.core)))

    def collect(self):
        for wait in self.pending:
            self.mail.receive(*wait)
        self.pending = []

    def straight(self, phase):
        self.collect()
        for sub in self.subs:
            axis, sel = GATHER_ORDER[sub[1]][phase], self.sel(sub, phase)
            source = self.mine(sub, sel)
            for distance in (1, -1, 2):
                key = self.mail.send(source, source, self.peer(axis, distance))
                self.pending.append((key, self.mine(sub, beside(sel, axis, -distance))))

    def ring(self):
        self.collect()
        self.keys = []
        for sub in self.subs:
            axis, sel = GATHER_ORDER[sub[1]][2], self.sel(sub, 2)
            source = self.mine(sub, sel)
            self.keys.append([self.mail.send(source, source, self.peer(axis, d)) for d in (1, -1)])
        for sub in self.subs:
            self.to_twin(sub, self.sel(sub, 2))

    def pass_on(self):
        for sub, keys in zip(self.subs, self.keys):
            order = GATHER_ORDER[sub[1]]
            axis, sel = order[2], self.sel(sub, 2)
            for half, distance in ((0, 1), (1, -1)):
                arrived, far = beside(sel, axis, -distance), beside(sel, axis, 2)
                self.mail.receive(keys[half], self.mine(sub, arrived))
                moving = self.mine(sub, {**arrived, order[0]: ("half", half)})
                coming = self.mine(sub, {**far, order[0]: ("half", half)})
                self.pending.append((self.mail.send(moving, moving, self.peer(axis, distance)), coming))
        for sub in self.subs:
            for distance in (1, -1):
                self.to_twin(sub, beside(self.sel(sub, 2), GATHER_ORDER[sub[1]][2], distance))

    def last(self):
        self.collect()
        for sub in self.subs:
            self.to_twin(sub, beside(self.sel(sub, 2), GATHER_ORDER[sub[1]][2], 2))

    def finish(self):
        for wait in self.twins:
            self.mail.receive(*wait)


class Reduce:
    def __init__(self, mail, sums, landing, subs, at, core):
        self.mail, self.sums, self.landing, self.subs, self.at, self.core = mail, sums, landing, subs, at, core
        self.kept = {}

    def sel(self, sub, phase):
        found = dict(self.at)
        for later in REDUCE_ORDER[sub[1]][phase + 1 :]:
            found[later] = ALL
        return found

    def mine(self, sub, sel, half=None):
        if half is not None:
            sel = {**sel, REDUCE_ORDER[sub[1]][2]: ("half", half)}
        return view(self.sums, sub, sel, None)

    def peer(self, axis, distance):
        return device(beside(self.at, axis, distance), self.core)

    def ring(self):
        for sub in self.subs:
            axis, sel, land = REDUCE_ORDER[sub[1]][0], self.sel(sub, 0), self.landing
            plus, minus = self.peer(axis, 1), self.peer(axis, -1)
            far, up, down = beside(sel, axis, 2), beside(sel, axis, 1), beside(sel, axis, -1)
            self.kept[sub] = [
                self.mail.send(self.mine(sub, far, 0), land[sub, 0, 0, 0], plus),
                self.mail.send(self.mine(sub, far, 1), land[sub, 0, 1, 0], minus),
                self.mail.send(self.mine(sub, up, 1), land[sub, 0, 1, 1], plus),
                self.mail.send(self.mine(sub, down, 0), land[sub, 0, 0, 2], minus),
            ]

    def pass_on(self):
        for sub in self.subs:
            axis, sel, land = REDUCE_ORDER[sub[1]][0], self.sel(sub, 0), self.landing
            keys = self.kept[sub]
            for half, distance in ((0, 1), (1, -1)):
                self.mail.receive(keys[half], land[sub, 0, half, 0])
                moving = self.mine(sub, beside(sel, axis, distance), half)
                added(moving, land[sub, 0, half, 0])
                keys.append(self.mail.send(moving, land[sub, 0, half, 1 + half], self.peer(axis, distance)))

    def collect_ring(self):
        for sub in self.subs:
            sel, land, keys = self.sel(sub, 0), self.landing, self.kept[sub]
            for half, first, second in ((1, keys[2], keys[5]), (0, keys[4], keys[3])):
                self.mail.receive(first, land[sub, 0, half, 1])
                self.mail.receive(second, land[sub, 0, half, 2])
                added(self.mine(sub, sel, half), land[sub, 0, half, 1], land[sub, 0, half, 2])

    def straight(self, phase):
        for sub in self.subs:
            axis, sel = REDUCE_ORDER[sub[1]][phase], self.sel(sub, phase)
            self.kept[sub] = [
                self.mail.send(
                    self.mine(sub, beside(sel, axis, distance)),
                    self.landing[sub, phase, use],
                    self.peer(axis, distance),
                )
                for use, distance in enumerate((1, -1, 2))
            ]

    def collect(self, phase):
        for sub in self.subs:
            terms = [self.landing[sub, phase, use] for use in range(3)]
            for key, term in zip(self.kept[sub], terms):
                self.mail.receive(key, term)
            added(self.mine(sub, self.sel(sub, phase)), *terms)


def dot(left, right):
    return jnp.dot(left, right, preferred_element_type=F32)


def dot_right_t(left, right):
    return lax.dot_general(left, right, (((1,), (1,)), ((), ())), preferred_element_type=F32)


def dot_left_t(left, right):
    return lax.dot_general(left, right, (((0,), (0,)), ((), ())), preferred_element_type=F32)


def flip(values):
    return values.astype(F32).T.astype(BF)


def mean_last(values):
    return jnp.mean(values, axis=-1, keepdims=True)


def sum_rows(values):
    return jnp.sum(values, axis=0, keepdims=True)


def normalize(values):
    center = values - mean_last(values)
    factor = lax.rsqrt(mean_last(center * center) + NORM_EPS)
    return center * factor, factor


def norm_back(d_norm, xhat, factor, gain):
    e = d_norm * gain
    return factor * (e - mean_last(e) - xhat * mean_last(e * xhat))


def owner_mask(shape, column, each):
    owner = lax.broadcasted_iota(jnp.int32, shape, 0) * each
    return (column >= owner) & (column < owner + each)


def width_mask(first):
    shape = (16, 16, WIDTH)
    return owner_mask(shape, lax.broadcasted_iota(jnp.int32, shape, 2) - 6 * first, 6)


def hidden_mask(columns):
    shape = (128, HIDDEN)
    return owner_mask(shape, jnp.broadcast_to(columns, shape), 24)


def low_half(shape):
    return lax.broadcasted_iota(jnp.int32, shape, 1) < 64


def swap_halves(tile):
    return pltpu.roll(tile, 64, 1)


def position_tile(block, tile):
    if tile < 8:
        low, high = block(2 * tile), swap_halves(block(2 * tile + 1))
    else:
        low, high = swap_halves(block(31 - 2 * tile)), block(30 - 2 * tile)
    return jnp.where(low_half(low.shape), low, high)


def position_block(tile, block):
    early, late = tile(block // 2), tile((31 - block) // 2)
    if block % 2 == 0:
        return jnp.where(low_half(early.shape), early, late)
    return swap_halves(jnp.where(low_half(early.shape), late, early))


TILE = 256
KEYS = 1024


def columns_of(tile):
    return slice(128 * tile, 128 * tile + 128)


def causal(scores, first):
    key = lax.broadcasted_iota(jnp.int32, scores.shape, 0)
    query = lax.broadcasted_iota(jnp.int32, scores.shape, 1) + first
    return jnp.where(key <= query, scores, MASKED)


def scores_of(ordered, natural, first, count):
    queries = ordered[0:64, first:count]
    return causal(dot(natural[0:count, :], jnp.concatenate([jnp.zeros_like(queries), queries], axis=0)), first)


def order_heads(landed, ordered, natural):
    for tile in range(16):
        found = position_tile(lambda b: landed[:, columns_of(b)].astype(F32), tile)
        found = jnp.concatenate([found[0:64] * 0.125, found[64:192]], axis=0)
        ordered[:, columns_of(tile)] = found.astype(BF)
        natural[columns_of(tile), :] = found[0:128].T.astype(BF)


def attend(step, ordered, natural, out_t, log_total):
    first = TILE * step
    count = first + TILE
    scores = scores_of(ordered, natural, first, count)
    best = jnp.max(scores, axis=0, keepdims=True)
    probs = jnp.exp(scores - best)
    total = sum_rows(probs)
    out_t[:, first:count] = dot(ordered[128:192, 0:count], probs.astype(BF)) / total
    log_total[0:1, first:count] = best + jnp.log(total)


def order_back(landed, ordered, d_out, values_natural):
    for tile in range(16):
        found = position_tile(lambda b: landed[:, columns_of(b)].astype(F32), tile)
        d_out[:, columns_of(tile)] = found
        both = jnp.concatenate([ordered[128:192, columns_of(tile)].astype(F32), found], axis=0)
        values_natural[columns_of(tile), :] = both.T.astype(BF)


def attend_back(step, ordered, natural, values_natural, out_t, log_total, d_out, d_t, d_keys):
    first = TILE * step
    count = first + TILE
    queries = ordered[0:64, first:count]
    queries = jnp.concatenate([jnp.zeros_like(queries), queries], axis=0)
    log_here = log_total[0:1, first:count]
    d_here = d_out[:, first:count]
    delta = sum_rows(d_here * out_t[:, first:count])
    d_low = d_here.astype(BF)
    d_low = jnp.concatenate([d_low, jnp.zeros_like(d_low)], axis=0)
    query_rows, d_rows = natural[first:count, :], values_natural[first:count, :]
    low = low_half(query_rows.shape)
    query_rows = jnp.where(low, query_rows, jnp.zeros_like(query_rows))
    d_rows = jnp.where(low, jnp.zeros_like(d_rows), d_rows)
    d_query = jnp.zeros((64, TILE), F32)
    for begin in range(0, count, KEYS):
        end = min(begin + KEYS, count)
        scores = dot(natural[begin:end, :], queries)
        if end == count:
            scores = causal(scores, first - begin)
        probs = jnp.exp(scores - log_here)
        d_scores = (probs * (dot(values_natural[begin:end, :], d_low) - delta)).astype(BF)
        d_query = d_query + dot(ordered[64:128, begin:end], d_scores)
        update = dot(d_scores, query_rows) + dot(probs.astype(BF), d_rows)
        if begin < first:
            done = min(end, first)
            d_keys[begin:done, :] += update[: done - begin]
        if end == count:
            d_keys[first:count, :] = update[first - begin :]
    d_t[0:64, first:count] = d_query * 0.125


def layer_kernel(*refs):
    shapes = landing_shapes()
    (
        x, cotangent, w_joint, w_proj, w_small, place_q, place_p, spread_q, spread_p, spread, spread_fc, columns,
        final, input_grad, out_q, out_fc, out_p, out_v,
    ) = refs[:18]
    weights, grads, sums = refs[18:21], refs[21:24], refs[24:27]
    landing = dict(zip(shapes, refs[27 : 27 + len(shapes)]))
    (
        in_joint, in_proj, last_q, last_fc, last_p, back_q, back_fc, back_p,
        normed, vectors, hidden_bias, qkv_t, landed, ordered, natural, out_t, log_total, att_blocks, att_t,
        total, d_norm_two, d_middle, d_att_t, landed_back, d_out, values_natural, d_t, d_keys, d_blocks,
        d_rows, d_qkv, grad_vectors, grad_hidden,
        send_sem, recv_sem, head_send, head_recv, local_sem,
    ) = refs[27 + len(shapes) :]
    at, core = place()
    ctx = lax.axis_index("ctx")
    spot = at["x"] * 2 + core
    is_head = ctx < HEADS
    twin = device(at, 1 - core)
    mail = Mail(send_sem, recv_sem, twin)

    known = [{"ctx": lax.rem(ctx + step, 16)} for step in range(1, 16)]
    known += [device(beside(at, "y", distance), core) for distance in (1, -1, 2)]
    known += [device(beside(at, "z", distance), core) for distance in (1, -1)]
    barrier = pltpu.get_barrier_semaphore()
    for target in known:
        pl.semaphore_signal(barrier, inc=1, device_id=target, device_id_type=MESH)
    pl.semaphore_wait(barrier, len(known))

    def group_sends(source, target):
        waits = []
        for step in range(1, 8):
            other = lax.rem(spot + step, 8)
            origin = lax.rem(spot + 8 - step, 8)
            peer = device({**at, "x": lax.div(other, 2)}, lax.rem(other, 2))
            waits.append((mail.send(source.at[other], target.at[spot], peer), target.at[origin]))
        target[spot] = source[spot]
        return waits

    def pair_sends(source, target):
        key = mail.send(source.at[1 - core], target.at[core], twin)
        target[core] = source[core]
        return [(key, target.at[1 - core])]

    def receive(waits):
        for wait in waits:
            mail.receive(*wait)

    def head_span(ref, who):
        return ref.at[:, pl.ds(pl.multiple_of(who * 128, 128), 128)]

    def head_copy(turn, step, source, target, peer):
        return pltpu.make_async_remote_copy(
            source, target, head_send.at[turn, step], head_recv.at[turn, step],
            device_id={"ctx": peer}, device_id_type=MESH,
        )

    def to_heads(turn, block, out):
        for step in range(1, 16):
            peer = lax.rem(ctx + step, 16)

            @pl.when(peer < HEADS)
            def _():
                head_copy(turn, step, block.at[peer], head_span(out, ctx), peer).start()

        @pl.when(is_head)
        def _():
            pltpu.make_async_copy(block.at[ctx], head_span(out, ctx), local_sem.at[turn]).start()

    def to_heads_received(turn, block, out):
        @pl.when(is_head)
        def _():
            for step in range(1, 16):
                source = lax.rem(ctx + 16 - step, 16)
                head_copy(turn, step, head_span(out, source), head_span(out, source), source).wait_recv()
            pltpu.make_async_copy(block.at[ctx], head_span(out, ctx), local_sem.at[turn]).wait()

    def to_heads_sent(turn, block, out):
        for step in range(1, 16):
            peer = lax.rem(ctx + step, 16)

            @pl.when(peer < HEADS)
            def _():
                head_copy(turn, step, block.at[peer], head_span(out, ctx), peer).wait_send()

    def from_heads(turn, blocks, out):
        @pl.when(is_head)
        def _():
            for step in range(1, 16):
                peer = lax.rem(ctx + step, 16)
                head_copy(turn, step, blocks.at[peer], out.at[ctx], peer).start()
            pltpu.make_async_copy(blocks.at[ctx], out.at[ctx], local_sem.at[turn]).start()

    def from_heads_received(turn, blocks, out):
        for step in range(1, 16):
            source = lax.rem(ctx + 16 - step, 16)

            @pl.when(source < HEADS)
            def _():
                head_copy(turn, step, out.at[source], out.at[source], source).wait_recv()

        @pl.when(is_head)
        def _():
            pltpu.make_async_copy(blocks.at[ctx], out.at[ctx], local_sem.at[turn]).wait()

    def from_heads_sent(turn, blocks, out):
        @pl.when(is_head)
        def _():
            for step in range(1, 16):
                peer = lax.rem(ctx + step, 16)
                head_copy(turn, step, blocks.at[peer], out.at[ctx], peer).wait_send()

    zl, zh = split_z(at["z"])
    waits = group_sends(w_joint, in_joint) + pair_sends(w_proj, in_proj)
    weights[2][zl, at["y"], zh, at["x"], core] = w_small[...]
    receive(waits)
    rows = dot(place_q[...], in_joint[...].reshape(128, WIDTH)).astype(BF)
    proj_rows = dot(place_p[...], in_proj[...].reshape(64, 384)).astype(BF)
    for tile in range(3):
        span = columns_of(tile)
        weights[0][at["x"], 3 * core + tile, zl, at["y"], zh] = rows[:, span]
        weights[1][at["x"], 6 * core + 2 * tile, zl, at["y"], zh] = rows[:, 384 + 128 * tile : 512 + 128 * tile]
        weights[1][at["x"], 6 * core + 2 * tile + 1, zl, at["y"], zh] = proj_rows[:, span]

    first = Gather(mail, weights, ATTENTION + SMALL, at, core)
    second = Gather(mail, weights, FORWARD, at, core)
    first.straight(0)
    second.straight(0)
    first.straight(1)
    second.straight(1)
    first.ring()
    xhat, _ = normalize(x[...])
    first.pass_on()
    second.ring()
    first.last()
    first.finish()

    small_rows = weights[2][...].reshape(2048, 128)
    found = jnp.zeros((16, WIDTH), F32)
    for group in range(8):
        wide = dot(small_rows[256 * group : 256 * group + 256], spread[...]).reshape(16, 16, WIDTH)
        found = found + jnp.sum(jnp.where(width_mask(16 * group), wide, 0.0), axis=0)
    vectors[...] = found
    tall = small_rows.astype(F32).reshape(128, 16, 128)
    eighth = lax.broadcasted_iota(jnp.int32, (128, 16, 128), 1) == 8
    fc_rows = jnp.sum(jnp.where(eighth, tall, 0.0), axis=1).astype(BF)
    hidden_bias[...] = sum_rows(jnp.where(hidden_mask(columns[...]), dot(fc_rows, spread_fc[...]), 0.0))
    normed_rows = (xhat * vectors[0:1] + vectors[2:3]).astype(BF)
    normed[...] = normed_rows

    def joint_tiles(start, count):
        tiles = [weights[0][t // 6, t % 6].reshape(WIDTH, 128) for t in range(start, start + count)]
        return jnp.concatenate(tiles, axis=1)

    for pair in range(9):
        kind, offset = pair // 3, (pair % 3) * 256
        out = dot(normed_rows, joint_tiles(2 * pair, 2))
        if kind != 1:
            out = out + vectors[3 + kind // 2 : 4 + kind // 2, offset : offset + 256]
        out = flip(out.astype(BF))
        for head in range(4):
            qkv_t[offset // 64 + head, 64 * kind : 64 * kind + 64, :] = out[64 * head : 64 * head + 64]
    to_heads(0, qkv_t, landed)
    second.pass_on()
    to_heads_received(0, qkv_t, landed)

    @pl.when(is_head)
    def _():
        order_heads(landed, ordered, natural)
        for step in range(4):
            attend(step, ordered, natural, out_t, log_total)

    second.last()

    @pl.when(is_head)
    def _():
        for step in range(4, 2048 // TILE):
            attend(step, ordered, natural, out_t, log_total)
        for block in range(16):
            att_blocks[block] = position_block(lambda t: out_t[:, columns_of(t)], block).astype(BF)

    from_heads(1, att_blocks, att_t)
    second.finish()
    from_heads_received(1, att_blocks, att_t)

    rows_t = att_t[...].reshape(WIDTH, 128)
    mat_out = joint_tiles(18, 6)
    middle = x[...] + dot(flip(rows_t), mat_out) + vectors[5:6]
    xhat, factor = normalize(middle)
    normed_two = (xhat * vectors[1:2] + vectors[6:7]).astype(BF)
    normed_t = flip(normed_two)
    gradient = cotangent[...]
    d_two = gradient.astype(BF)
    d_norm = jnp.zeros((128, WIDTH), F32)
    twin_waits = {}
    for chunk in range(4):
        tile = lambda half, t: weights[1][chunk, 2 * t + half].reshape(WIDTH, 128)
        mat_fc = jnp.concatenate([tile(0, t) for t in range(6)], axis=1)
        mat_proj = jnp.concatenate([tile(1, t) for t in range(6)], axis=1)
        span = slice(WIDTH * chunk, WIDTH * chunk + WIDTH)
        pre = dot(normed_two, mat_fc) + hidden_bias[:, span]
        root = 0.7978845608028654
        inner = jnp.tanh(root * (pre + 0.044715 * (pre * pre * pre)))
        activated = (0.5 * pre * (1.0 + inner)).astype(BF)
        slope = 0.5 * (1.0 + inner) + 0.5 * pre * (1.0 - inner * inner) * (
            root * (1.0 + 3 * 0.044715 * (pre * pre))
        )
        update = dot(activated, mat_proj)
        total[...] = update if chunk == 0 else total[...] + update
        d_pre = (dot_right_t(d_two, mat_proj) * slope).astype(BF)
        grad_hidden[:, span] = sum_rows(d_pre.astype(F32))
        update = dot_right_t(d_pre, mat_fc)
        d_norm_two[...] = update if chunk == 0 else d_norm_two[...] + update
        grad_fc = dot(normed_t, d_pre).astype(BF)
        grad_proj = dot_left_t(activated, d_two).astype(BF)
        for t in range(6):
            grads[1][chunk, 2 * t] = grad_fc[:, columns_of(t)].reshape(2, 4, 2, 48, 128)
            grads[1][chunk, 2 * t + 1] = grad_proj[:, columns_of(t)].reshape(2, 4, 2, 48, 128)
        key = mail.send(grads[1].at[chunk, pl.ds(6 * (1 - core), 6)], sums[1].at[chunk], twin)
        twin_waits[1, chunk] = key
    final[...] = middle + total[...] + vectors[7:8]
    d_norm = d_norm_two[...]
    d_mid = gradient + norm_back(d_norm, xhat, factor, vectors[1:2])
    d_middle[...] = d_mid
    d_one = d_mid.astype(BF)
    d_att_t[...] = dot_right_t(mat_out, d_one).astype(BF).reshape(HEADS, 64, 128)
    to_heads(2, d_att_t, landed_back)
    grad_out = dot(rows_t, d_one).astype(BF)
    for t in range(6):
        grads[0][3, t] = grad_out[:, columns_of(t)].reshape(2, 4, 2, 48, 128)
    twin_waits[0, 3] = mail.send(grads[0].at[3, pl.ds(3 * (1 - core), 3)], sums[0].at[3], twin)
    grad_vectors[...] = jnp.zeros_like(grad_vectors)
    grad_vectors[1:2] = sum_rows(d_norm * xhat)
    grad_vectors[5:6] = sum_rows(d_one.astype(F32))
    grad_vectors[6:7] = sum_rows(d_norm)
    grad_vectors[7:8] = sum_rows(d_two.astype(F32))

    def add_twin(kind, chunk):
        mail.receive(twin_waits[kind, chunk], sums[kind].at[chunk])
        count = 3 * (kind + 1)
        added(sums[kind].at[chunk], grads[kind].at[chunk, pl.ds(count * core, count)])

    back_second = Reduce(mail, sums, landing, FORWARD, at, core)
    for chunk in range(4):
        add_twin(1, chunk)
    back_second.ring()
    add_twin(0, 3)

    to_heads_received(2, d_att_t, landed_back)

    @pl.when(is_head)
    def _():
        order_back(landed_back, ordered, d_out, values_natural)
        for step in range(5):
            attend_back(step, ordered, natural, values_natural, out_t, log_total, d_out, d_t, d_keys)

    back_second.pass_on()

    @pl.when(is_head)
    def _():
        for step in range(5, 2048 // TILE):
            attend_back(step, ordered, natural, values_natural, out_t, log_total, d_out, d_t, d_keys)
        for tile in range(16):
            d_t[64:192, columns_of(tile)] = d_keys[columns_of(tile), :].T
        for block in range(16):
            d_blocks[block] = position_block(lambda t: d_t[:, columns_of(t)], block).astype(BF)

    from_heads(3, d_blocks, d_rows)
    back_second.collect_ring()
    back_second.straight(1)
    from_heads_received(3, d_blocks, d_rows)

    for head in range(HEADS):
        rows = flip(d_rows[head])
        for kind in range(3):
            offset = WIDTH * kind + 64 * head
            d_qkv[:, offset : offset + 64] = rows[:, 64 * kind : 64 * kind + 64]
    normed_t = flip(normed[...])
    for pair in range(9):
        out = dot(normed_t, d_qkv[:, 256 * pair : 256 * pair + 256]).astype(BF)
        for t in range(2):
            tile = 2 * pair + t
            grads[0][tile // 6, tile % 6] = out[:, columns_of(t)].reshape(2, 4, 2, 48, 128)
        if pair % 3 == 2:
            chunk = pair // 3
            source = grads[0].at[chunk, pl.ds(3 * (1 - core), 3)]
            twin_waits[0, chunk] = mail.send(source, sums[0].at[chunk], twin)
    back_second.collect(1)
    back_second.straight(2)
    d_norm = jnp.zeros((128, WIDTH), F32)
    for pair in range(9):
        d_norm = d_norm + dot_right_t(d_qkv[:, 256 * pair : 256 * pair + 256], joint_tiles(2 * pair, 2))
    back_first = Reduce(mail, sums, landing, ATTENTION, at, core)
    for chunk in range(3):
        add_twin(0, chunk)
    back_first.ring()
    xhat, factor = normalize(x[...])
    input_grad[...] = d_middle[...] + norm_back(d_norm, xhat, factor, vectors[0:1])
    kinds = lambda kind: sum_rows(d_qkv[:, WIDTH * kind : WIDTH * kind + WIDTH].astype(F32))
    row = lax.broadcasted_iota(jnp.int32, (16, WIDTH), 0)
    found = grad_vectors[...]
    for which, value in ((0, sum_rows(d_norm * xhat)), (2, sum_rows(d_norm)), (3, kinds(0)), (4, kinds(2))):
        found = jnp.where(row == which, value, found)
    small = []
    for group in range(8):
        wide = jnp.where(width_mask(16 * group), jnp.broadcast_to(found[None], (16, 16, WIDTH)), 0.0)
        small.append(dot_right_t(wide.astype(BF).reshape(256, WIDTH), spread[...]).reshape(16, 16, 128))
    small = jnp.concatenate(small, axis=0)
    wide = jnp.where(hidden_mask(columns[...]), jnp.broadcast_to(grad_hidden[...], (128, HIDDEN)), 0.0)
    hidden = dot_right_t(wide.astype(BF), spread_fc[...])
    eighth = lax.broadcasted_iota(jnp.int32, (128, 16, 128), 1) == 8
    small = jnp.where(eighth, hidden[:, None, :], small)
    grads[2][...] = small.astype(BF).reshape(SHAPES[2])
    every = {axis: ALL for axis in AXES}
    key = mail.send(view(grads, (2, 0), every, 1 - core), sums[2], twin)

    back_second.collect(2)
    mine = [view(sums, sub, at, None) for sub in FORWARD]
    rows = jnp.concatenate([mine[t][0] for t in range(3)], axis=1)
    last_fc[...] = dot(spread_q[...], rows).astype(BF).reshape(8, 16, 384)
    rows = jnp.concatenate([mine[t][1] for t in range(3)], axis=1)
    last_p[...] = dot(spread_p[...], rows).astype(BF).reshape(2, 32, 384)
    waits = group_sends(last_fc, back_fc) + pair_sends(last_p, back_p)
    mail.receive(key, sums[2])
    added(sums[2], view(grads, (2, 0), every, core))
    back_small = Reduce(mail, sums, landing, SMALL, at, core)
    back_small.straight(0)

    back_first.pass_on()
    back_small.collect(0)
    back_small.straight(1)
    back_first.collect_ring()
    back_first.straight(1)
    back_small.collect(1)
    back_small.straight(2)
    receive(waits)
    for group in range(8):
        out_fc[:, 384 * group : 384 * group + 384] = back_fc[group].astype(F32)[:8]
    for half in range(2):
        out_p[:, 384 * half : 384 * half + 384] = back_p[half].astype(F32)[:24]
    back_first.collect(1)
    back_first.straight(2)
    back_small.collect(2)
    out_v[...] = view(sums, (2, 0), at, None)[...].astype(F32)
    back_first.collect(2)
    rows = jnp.concatenate([view(sums, sub, at, None)[0] for sub in ATTENTION], axis=1)
    last_q[...] = dot(spread_q[...], rows).astype(BF).reshape(8, 16, 384)
    receive(group_sends(last_q, back_q))
    for group in range(8):
        out_q[:, 384 * group : 384 * group + 384] = back_q[group].astype(F32)[:8]

    mail.finish()
    to_heads_sent(0, qkv_t, landed)
    from_heads_sent(1, att_blocks, att_t)
    to_heads_sent(2, d_att_t, landed_back)
    from_heads_sent(3, d_blocks, d_rows)


def place_rows(groups, rows, padded):
    found = np.zeros((groups * rows, groups * padded), np.float32)
    for group in range(groups):
        for row in range(rows):
            found[group * rows + row, group * padded + row] = 1
    return found


def spread_matrix(entries, each):
    found = np.zeros((128, len(entries)), np.float32)
    found[entries % each, np.arange(len(entries))] = 1
    return found


def hidden_order():
    x, group, row = np.meshgrid(np.arange(4), np.arange(16), np.arange(48), indexing="ij")
    return (192 * group + 48 * x + row).reshape(-1)


def local(tokens, cotangent, w_qkv, w_out, w_fc, w_proj, gains, biases, fc_bias):
    first = jnp.concatenate([w_qkv[0], w_out[0]], axis=1).reshape(6, 8, 384)
    hidden = jnp.transpose(w_fc[0].reshape(6, 16, 4, 48), (0, 2, 1, 3)).reshape(6, 8, 384)
    joint = jnp.transpose(jnp.concatenate([first, hidden], axis=2), (1, 0, 2))
    joint = jnp.pad(joint, ((0, 0), (0, 10), (0, 0)))
    proj = jnp.pad(jnp.transpose(w_proj[0].reshape(24, 2, 384), (1, 0, 2)), ((0, 0), (0, 8), (0, 0)))
    small = jnp.pad(jnp.concatenate([gains[0], biases[0]], axis=0), ((0, 0), (0, 122)))
    small = jnp.concatenate([small, jnp.pad(fc_bias, ((0, 0), (0, 104))), jnp.zeros((7, 128), BF)], axis=0)
    order = hidden_order()
    scratch = [VMEM(shape, BF) for shape in SHAPES + SHAPES + SUMS + tuple(landing_shapes().values())]
    scratch += [
        VMEM((8, 16, WIDTH), BF),
        VMEM((2, 32, 384), BF),
        VMEM((8, 16, 384), BF),
        VMEM((8, 16, 384), BF),
        VMEM((2, 32, 384), BF),
        VMEM((8, 16, 384), BF),
        VMEM((8, 16, 384), BF),
        VMEM((2, 32, 384), BF),
        VMEM((128, WIDTH), BF),
        VMEM((16, WIDTH), F32),
        VMEM((1, HIDDEN), F32),
        VMEM((HEADS, 192, 128), BF),
        VMEM((192, 2048), BF),
        VMEM((192, 2048), BF),
        VMEM((2048, 128), BF),
        VMEM((64, 2048), F32),
        VMEM((8, 2048), F32),
        VMEM((16, 64, 128), BF),
        VMEM((HEADS, 64, 128), BF),
        VMEM((128, WIDTH), F32),
        VMEM((128, WIDTH), F32),
        VMEM((128, WIDTH), F32),
        VMEM((HEADS, 64, 128), BF),
        VMEM((64, 2048), BF),
        VMEM((64, 2048), F32),
        VMEM((2048, 128), BF),
        VMEM((192, 2048), F32),
        VMEM((2048, 128), F32),
        VMEM((16, 192, 128), BF),
        VMEM((HEADS, 192, 128), BF),
        VMEM((128, 3 * WIDTH), BF),
        VMEM((16, WIDTH), F32),
        VMEM((1, HIDDEN), F32),
        pltpu.SemaphoreType.DMA((COPIES,)),
        pltpu.SemaphoreType.DMA((COPIES,)),
        pltpu.SemaphoreType.DMA((4, 16)),
        pltpu.SemaphoreType.DMA((4, 16)),
        pltpu.SemaphoreType.DMA((4,)),
    ]
    outs = ((128, WIDTH), (128, WIDTH), (8, HIDDEN), (8, HIDDEN), (24, WIDTH), (16, 128))
    final, input_grad, out_q, out_fc, out_p, out_v = pl.pallas_call(
        layer_kernel,
        out_shape=[jax.ShapeDtypeStruct(shape, F32) for shape in outs],
        in_specs=[pl.BlockSpec(memory_space=VMEM)] * 12,
        out_specs=[pl.BlockSpec(memory_space=VMEM)] * 6,
        scratch_shapes=scratch,
        compiler_params=pltpu.CompilerParams(
            collective_id=0, has_side_effects=True, vmem_limit_bytes=VMEM_LIMIT * MEGA
        ),
        name="layer",
    )(
        tokens[0],
        cotangent[0],
        joint,
        proj,
        small,
        jnp.asarray(place_rows(8, 6, 16), BF),
        jnp.asarray(place_rows(2, 24, 32), BF),
        jnp.asarray(place_rows(8, 6, 16).T, BF),
        jnp.asarray(place_rows(2, 24, 32).T, BF),
        jnp.asarray(spread_matrix(np.arange(WIDTH), 6), BF),
        jnp.asarray(spread_matrix(order, 24), BF),
        jnp.asarray(order.reshape(1, HIDDEN), jnp.int32),
    )
    grad_fc = jnp.transpose(out_fc[:6].reshape(6, 4, 16, 48), (0, 2, 1, 3)).reshape(1, 6, HIDDEN)
    return (
        final[None],
        input_grad[None],
        out_q[None, :6, : 3 * WIDTH],
        out_q[None, :6, 3 * WIDTH :],
        grad_fc,
        out_p[None],
        out_v[None, 0:2, :6],
        out_v[None, 2:8, :6],
        out_v[8:9, :24],
    )


VMEM_LIMIT = 63


def solution(mesh):
    rows = P("dp", "ctx", None)
    weight = P(None, ("dp", "ctx"), None)
    vector = P(None, None, ("dp", "ctx"))
    tail = (weight,) * 4 + (vector, vector, P(None, ("dp", "ctx")))
    return jax.shard_map(
        local, mesh=mesh, in_specs=(rows, rows) + tail, out_specs=(rows, rows) + tail, check_vma=False
    )
```

```python
import jax
import jax.numpy as jnp
import numpy as np
from jax import lax
from jax.experimental import pallas as pl
from jax.experimental.pallas import tpu as pltpu
from jax.sharding import PartitionSpec as P

BF = jnp.bfloat16
F32 = jnp.float32
MESH = pl.DeviceIdType.MESH
VMEM = pltpu.VMEM
ALL = slice(None)
AXES = ("x", "y", "z")
GATHER_ORDER = (("x", "y", "z"), ("y", "z", "x"), ("z", "x", "y"))
REDUCE_ORDER = tuple(order[::-1] for order in GATHER_ORDER)
SHAPES = ((4, 6, 2, 4, 2, 48, 128), (4, 12, 2, 4, 2, 48, 128), (2, 4, 2, 4, 2, 16, 128))
SUMS = ((4, 3, 2, 4, 2, 48, 128), (4, 6, 2, 4, 2, 48, 128), (2, 4, 2, 4, 16, 128))
ATTENTION = ((0, 0), (0, 1), (0, 2))
FORWARD = ((1, 0), (1, 1), (1, 2))
SMALL = ((2, 0),)
HEADS = 12
WIDTH = 768
HIDDEN = 3072
NORM_EPS = 1e-05
MASKED = -1e30
MEGA = 1024 * 1024
COPIES = 256


def place():
    dp = lax.axis_index("dp")
    ctx = lax.axis_index("ctx")
    at = {
        "x": lax.rem(lax.div(ctx, 2), 4),
        "y": lax.rem(dp, 4),
        "z": lax.div(ctx, 8) * 2 + lax.div(dp, 4),
    }
    return at, lax.rem(ctx, 2)


def device(at, core):
    return {
        "dp": lax.rem(at["z"], 2) * 4 + at["y"],
        "ctx": lax.div(at["z"], 2) * 8 + at["x"] * 2 + core,
    }


def head_at(ctx, z_lo):
    z_hi, x, core = lax.div(ctx, 8), lax.rem(lax.div(ctx, 2), 4), lax.rem(ctx, 2)
    head = (1 - core) * (4 * z_hi + x) + core * (8 + 2 * z_hi + x - 2 * z_lo)
    return (core == 0) | (lax.div(x, 2) == z_lo), head


def beside(at, axis, distance):
    moved = dict(at)
    moved[axis] = lax.rem(at[axis] + (distance + 4), 4)
    return moved


def split_z(z):
    if isinstance(z, tuple):
        return pl.ds(z[1], 1), ALL
    if isinstance(z, slice):
        return ALL, ALL
    return lax.rem(z, 2), lax.div(z, 2)


def line(value):
    return pl.ds(2 * value[1], 2) if isinstance(value, tuple) else value


def view(refs, sub, sel, core):
    kind, tile = sub
    x, y = line(sel["x"]), line(sel["y"])
    zl, zh = split_z(sel["z"])
    if kind == 2:
        return refs[2].at[zl, y, zh, x] if core is None else refs[2].at[zl, y, zh, x, core]
    count = kind + 1
    start = count * tile + (0 if core is None else 3 * count * core)
    return refs[kind].at[x, pl.ds(start, count), zl, y, zh]


def block_shape(sub, gone, half_axis=None):
    extent = {axis: 1 if axis in gone else 4 for axis in AXES}
    if half_axis is not None:
        extent[half_axis] = 2
    lead = lambda name: () if extent[name] == 1 else (extent[name],)
    zl, zh = ((), ()) if extent["z"] == 1 else ((extent["z"] // 2,), (2,))
    if sub[0] == 2:
        return zl + lead("y") + zh + lead("x") + (16, 128)
    return lead("x") + (sub[0] + 1,) + zl + lead("y") + zh + (48, 128)


def landing_shapes():
    found = {}
    for sub in ATTENTION + FORWARD + SMALL:
        order = REDUCE_ORDER[sub[1]]
        for phase in range(3):
            gone = order[: phase + 1]
            if phase == 0 and sub[0] < 2:
                for half in range(2):
                    for use in range(3):
                        found[sub, phase, half, use] = block_shape(sub, gone, order[2])
            else:
                for use in range(3):
                    found[sub, phase, use] = block_shape(sub, gone)
    return found


def added(target, *terms):
    if len(target.shape) == 2:
        total = target[...].astype(F32)
        for term in terms:
            total = total + term[...].astype(F32)
        target[...] = total.astype(BF)
        return

    def step(i, carry):
        total = target[i].astype(F32)
        for term in terms:
            total = total + term[i].astype(F32)
        target[i] = total.astype(BF)
        return carry

    lax.fori_loop(0, target.shape[0], step, 0)


class Mail:
    def __init__(self, send_sem, recv_sem, anyone):
        self.send_sem, self.recv_sem, self.anyone = send_sem, recv_sem, anyone
        self.used, self.sent = 0, []

    def send(self, source, target, device_id):
        key = self.used
        copy = pltpu.make_async_remote_copy(
            src_ref=source,
            dst_ref=target,
            send_sem=self.send_sem.at[key],
            recv_sem=self.recv_sem.at[key],
            device_id=device_id,
            device_id_type=MESH,
        )
        copy.start()
        self.sent.append(copy)
        self.used += 1
        return key

    def receive(self, key, arrival):
        pltpu.make_async_remote_copy(
            src_ref=arrival,
            dst_ref=arrival,
            send_sem=self.send_sem.at[key],
            recv_sem=self.recv_sem.at[key],
            device_id=self.anyone,
            device_id_type=MESH,
        ).wait_recv()

    def finish(self):
        for copy in self.sent:
            copy.wait_send()
        self.sent = []


class Gather:
    def __init__(self, mail, refs, subs, at, core):
        self.mail, self.refs, self.subs, self.at, self.core = mail, refs, subs, at, core
        self.twin = device(at, 1 - core)
        self.pending, self.twins = [], []

    def sel(self, sub, phase):
        found = dict(self.at)
        for done in GATHER_ORDER[sub[1]][:phase]:
            found[done] = ALL
        return found

    def mine(self, sub, sel):
        return view(self.refs, sub, sel, self.core)

    def peer(self, axis, distance):
        return device(beside(self.at, axis, distance), self.core)

    def to_twin(self, sub, sel):
        source = self.mine(sub, sel)
        self.twins.append((self.mail.send(source, source, self.twin), view(self.refs, sub, sel, 1 - self.core)))

    def collect(self):
        for wait in self.pending:
            self.mail.receive(*wait)
        self.pending = []

    def straight(self, phase):
        self.collect()
        for sub in self.subs:
            axis, sel = GATHER_ORDER[sub[1]][phase], self.sel(sub, phase)
            source = self.mine(sub, sel)
            for distance in (1, -1, 2):
                key = self.mail.send(source, source, self.peer(axis, distance))
                self.pending.append((key, self.mine(sub, beside(sel, axis, -distance))))

    def ring(self):
        self.collect()
        self.keys = []
        for sub in self.subs:
            axis, sel = GATHER_ORDER[sub[1]][2], self.sel(sub, 2)
            source = self.mine(sub, sel)
            self.keys.append([self.mail.send(source, source, self.peer(axis, d)) for d in (1, -1)])
        for sub in self.subs:
            self.to_twin(sub, self.sel(sub, 2))

    def pass_on(self):
        for sub, keys in zip(self.subs, self.keys):
            order = GATHER_ORDER[sub[1]]
            axis, sel = order[2], self.sel(sub, 2)
            for half, distance in ((0, 1), (1, -1)):
                arrived, far = beside(sel, axis, -distance), beside(sel, axis, 2)
                self.mail.receive(keys[half], self.mine(sub, arrived))
                moving = self.mine(sub, {**arrived, order[0]: ("half", half)})
                coming = self.mine(sub, {**far, order[0]: ("half", half)})
                self.pending.append((self.mail.send(moving, moving, self.peer(axis, distance)), coming))
        for sub in self.subs:
            for distance in (1, -1):
                self.to_twin(sub, beside(self.sel(sub, 2), GATHER_ORDER[sub[1]][2], distance))

    def last(self):
        self.collect()
        for sub in self.subs:
            self.to_twin(sub, beside(self.sel(sub, 2), GATHER_ORDER[sub[1]][2], 2))

    def finish(self):
        for wait in self.twins:
            self.mail.receive(*wait)


class Reduce:
    def __init__(self, mail, sums, landing, subs, at, core):
        self.mail, self.sums, self.landing, self.subs, self.at, self.core = mail, sums, landing, subs, at, core
        self.kept = {}

    def sel(self, sub, phase):
        found = dict(self.at)
        for later in REDUCE_ORDER[sub[1]][phase + 1 :]:
            found[later] = ALL
        return found

    def mine(self, sub, sel, half=None):
        if half is not None:
            sel = {**sel, REDUCE_ORDER[sub[1]][2]: ("half", half)}
        return view(self.sums, sub, sel, None)

    def peer(self, axis, distance):
        return device(beside(self.at, axis, distance), self.core)

    def ring(self):
        for sub in self.subs:
            axis, sel, land = REDUCE_ORDER[sub[1]][0], self.sel(sub, 0), self.landing
            plus, minus = self.peer(axis, 1), self.peer(axis, -1)
            far, up, down = beside(sel, axis, 2), beside(sel, axis, 1), beside(sel, axis, -1)
            self.kept[sub] = [
                self.mail.send(self.mine(sub, far, 0), land[sub, 0, 0, 0], plus),
                self.mail.send(self.mine(sub, far, 1), land[sub, 0, 1, 0], minus),
                self.mail.send(self.mine(sub, up, 1), land[sub, 0, 1, 1], plus),
                self.mail.send(self.mine(sub, down, 0), land[sub, 0, 0, 2], minus),
            ]

    def pass_on(self):
        for sub in self.subs:
            axis, sel, land = REDUCE_ORDER[sub[1]][0], self.sel(sub, 0), self.landing
            keys = self.kept[sub]
            for half, distance in ((0, 1), (1, -1)):
                self.mail.receive(keys[half], land[sub, 0, half, 0])
                moving = self.mine(sub, beside(sel, axis, distance), half)
                added(moving, land[sub, 0, half, 0])
                keys.append(self.mail.send(moving, land[sub, 0, half, 1 + half], self.peer(axis, distance)))

    def collect_ring(self):
        for sub in self.subs:
            sel, land, keys = self.sel(sub, 0), self.landing, self.kept[sub]
            for half, first, second in ((1, keys[2], keys[5]), (0, keys[4], keys[3])):
                self.mail.receive(first, land[sub, 0, half, 1])
                self.mail.receive(second, land[sub, 0, half, 2])
                added(self.mine(sub, sel, half), land[sub, 0, half, 1], land[sub, 0, half, 2])

    def straight(self, phase):
        for sub in self.subs:
            axis, sel = REDUCE_ORDER[sub[1]][phase], self.sel(sub, phase)
            self.kept[sub] = [
                self.mail.send(
                    self.mine(sub, beside(sel, axis, distance)),
                    self.landing[sub, phase, use],
                    self.peer(axis, distance),
                )
                for use, distance in enumerate((1, -1, 2))
            ]

    def collect(self, phase):
        for sub in self.subs:
            terms = [self.landing[sub, phase, use] for use in range(3)]
            for key, term in zip(self.kept[sub], terms):
                self.mail.receive(key, term)
            added(self.mine(sub, self.sel(sub, phase)), *terms)


def dot(left, right):
    return jnp.dot(left, right, preferred_element_type=F32)


def dot_right_t(left, right):
    return lax.dot_general(left, right, (((1,), (1,)), ((), ())), preferred_element_type=F32)


def dot_left_t(left, right):
    return lax.dot_general(left, right, (((0,), (0,)), ((), ())), preferred_element_type=F32)


def flip(values):
    return values.astype(F32).T.astype(BF)


def mean_last(values):
    return jnp.mean(values, axis=-1, keepdims=True)


def sum_rows(values):
    return jnp.sum(values, axis=0, keepdims=True)


def normalize(values):
    center = values - mean_last(values)
    factor = lax.rsqrt(mean_last(center * center) + NORM_EPS)
    return center * factor, factor


def norm_back(d_norm, xhat, factor, gain):
    e = d_norm * gain
    return factor * (e - mean_last(e) - xhat * mean_last(e * xhat))


def owner_mask(shape, column, each):
    owner = lax.broadcasted_iota(jnp.int32, shape, 0) * each
    return (column >= owner) & (column < owner + each)


def width_mask(first):
    shape = (16, 16, WIDTH)
    return owner_mask(shape, lax.broadcasted_iota(jnp.int32, shape, 2) - 6 * first, 6)


def hidden_mask(columns):
    shape = (128, HIDDEN)
    return owner_mask(shape, jnp.broadcast_to(columns, shape), 24)


def low_half(shape):
    return lax.broadcasted_iota(jnp.int32, shape, 1) < 64


def swap_halves(tile):
    return pltpu.roll(tile, 64, 1)


def position_tile(block, tile):
    if tile < 8:
        low, high = block(2 * tile), swap_halves(block(2 * tile + 1))
    else:
        low, high = swap_halves(block(31 - 2 * tile)), block(30 - 2 * tile)
    return jnp.where(low_half(low.shape), low, high)


def position_block(tile, block):
    early, late = tile(block // 2), tile((31 - block) // 2)
    if block % 2 == 0:
        return jnp.where(low_half(early.shape), early, late)
    return swap_halves(jnp.where(low_half(early.shape), late, early))


TILE = 256
KEYS = 1024


def columns_of(tile):
    return slice(128 * tile, 128 * tile + 128)


def causal(scores, first):
    key = lax.broadcasted_iota(jnp.int32, scores.shape, 0)
    query = lax.broadcasted_iota(jnp.int32, scores.shape, 1) + first
    return jnp.where(key <= query, scores, MASKED)


def scores_of(ordered, natural, first, count):
    queries = ordered[0:64, first:count]
    return causal(dot(natural[0:count, :], jnp.concatenate([jnp.zeros_like(queries), queries], axis=0)), first)


def order_heads(landed, ordered, natural):
    for tile in range(16):
        found = position_tile(lambda b: landed[:, columns_of(b)].astype(F32), tile)
        found = jnp.concatenate([found[0:64] * 0.125, found[64:192]], axis=0)
        ordered[:, columns_of(tile)] = found.astype(BF)
        natural[columns_of(tile), :] = found[0:128].T.astype(BF)


def attend(step, ordered, natural, out_t, log_total):
    first = TILE * step
    count = first + TILE
    scores = scores_of(ordered, natural, first, count)
    best = jnp.max(scores, axis=0, keepdims=True)
    probs = jnp.exp(scores - best)
    total = sum_rows(probs)
    out_t[:, first:count] = dot(ordered[128:192, 0:count], probs.astype(BF)) / total
    log_total[0:1, first:count] = best + jnp.log(total)


def order_back(landed, ordered, d_out, values_natural):
    for tile in range(16):
        found = position_tile(lambda b: landed[:, columns_of(b)].astype(F32), tile)
        d_out[:, columns_of(tile)] = found.astype(BF)
        both = jnp.concatenate([ordered[128:192, columns_of(tile)].astype(F32), found], axis=0)
        values_natural[columns_of(tile), :] = both.T.astype(BF)


def attend_back(step, ordered, natural, values_natural, out_t, log_total, d_out, d_t, d_keys):
    first = TILE * step
    count = first + TILE
    queries = ordered[0:64, first:count]
    queries = jnp.concatenate([jnp.zeros_like(queries), queries], axis=0)
    log_here = log_total[0:1, first:count]
    d_low = d_out[:, first:count]
    delta = sum_rows(d_low.astype(F32) * out_t[:, first:count])
    d_low = jnp.concatenate([d_low, jnp.zeros_like(d_low)], axis=0)
    query_rows, d_rows = natural[first:count, :], values_natural[first:count, :]
    low = low_half(query_rows.shape)
    query_rows = jnp.where(low, query_rows, jnp.zeros_like(query_rows))
    d_rows = jnp.where(low, jnp.zeros_like(d_rows), d_rows)
    d_query = jnp.zeros((64, TILE), F32)
    for begin in range(0, count, KEYS):
        end = min(begin + KEYS, count)
        scores = dot(natural[begin:end, :], queries)
        if end == count:
            scores = causal(scores, first - begin)
        probs = jnp.exp(scores - log_here)
        d_scores = (probs * (dot(values_natural[begin:end, :], d_low) - delta)).astype(BF)
        d_query = d_query + dot(ordered[64:128, begin:end], d_scores)
        update = dot(d_scores, query_rows) + dot(probs.astype(BF), d_rows)
        if begin < first:
            done = min(end, first)
            d_keys[begin:done, :] += update[: done - begin]
        if end == count:
            d_keys[first:count, :] = update[first - begin :]
    d_t[0:64, first:count] = (d_query * 0.125).astype(BF)


def hidden_order():
    x, group, row = np.meshgrid(np.arange(4), np.arange(16), np.arange(48), indexing="ij")
    return (192 * group + 48 * x + row).reshape(-1)


def reorder(source, order, store):
    for tile in range(len(order) // 128):
        wanted = order[columns_of(tile)]
        lanes = lax.broadcasted_iota(jnp.int32, (8, 128), 1)
        found = jnp.zeros((8, 128), F32)
        begin = 0
        while begin < 128:
            end = begin + 1
            while end < 128 and wanted[end] == wanted[end - 1] + 1 and wanted[end] % 128:
                end += 1
            at = int(wanted[begin])
            piece = source[0:8, columns_of(at // 128)]
            shift = (begin - at) % 128
            if shift:
                piece = pltpu.roll(piece, shift, 1)
            found = jnp.where((lanes >= begin) & (lanes < end), piece, found)
            begin = end
        store(tile, found)


def results_kernel(
    final, input_grad, joint, hidden, proj, small,
    to_final, to_input, to_qkv, to_out, to_fc, to_proj, to_gains, to_biases, to_fc_bias,
    joint_here, hidden_here, small_here, qkv, out, fc, gains, biases, fc_bias, in_sem, out_sem,
):
    straight = [
        pltpu.make_async_copy(source, target, out_sem.at[i])
        for i, (source, target) in enumerate(((final, to_final), (input_grad, to_input), (proj, to_proj)))
    ]
    loads = [
        pltpu.make_async_copy(source, target, in_sem.at[i])
        for i, (source, target) in enumerate(((joint, joint_here), (hidden, hidden_here), (small, small_here)))
    ]
    for copy in loads + straight:
        copy.start()
    for copy in loads:
        copy.wait()
    for row in range(6):
        qkv[row] = joint_here[row : row + 1, 0 : 3 * WIDTH]
        out[row] = joint_here[row : row + 1, 3 * WIDTH : HIDDEN]
        fc[row] = hidden_here[row : row + 1, :]
        biases[row] = small_here[2 + row : 3 + row, 0:6]
    gains[...] = small_here[0:2, 0:6]
    fc_bias[...] = small_here[8:9, 0:24]
    pairs = ((qkv, to_qkv), (out, to_out), (fc, to_fc), (gains, to_gains), (biases, to_biases), (fc_bias, to_fc_bias))
    last = [pltpu.make_async_copy(source, target, out_sem.at[3 + i]) for i, (source, target) in enumerate(pairs)]
    for copy in last:
        copy.start()
    for copy in straight + last:
        copy.wait()


def layer_kernel(*refs):
    shapes = landing_shapes()
    ins, outs, refs = refs[:12], refs[12:18], refs[18:]
    loaded, refs = refs[:12], refs[12:]
    x, cotangent, raw_qkv, raw_out, raw_fc, raw_proj, raw_gains, raw_biases, raw_fc_bias, placing, spreads, columns = loaded
    final, input_grad, out_q, out_fc, out_p, out_v = refs[:6]
    weights, grads, sums = refs[6:9], refs[9:12], refs[12:15]
    refs = refs[15:]
    landing = dict(zip(shapes, refs[: len(shapes)]))
    (
        pad_joint, pad_fc, pad_proj, pad_small, w_joint, w_proj, in_sem, out_sem,
        in_joint, in_proj, last_q, last_fc, last_p, back_q, back_fc, back_p,
        normed, vectors, hidden_bias, qkv_t, landed, ordered, natural, out_t, log_total, att_blocks, att_t,
        d_middle, d_att_t, landed_back, d_out, values_natural, d_t, d_keys, d_blocks,
        d_rows, d_qkv, grad_vectors, grad_hidden,
        send_sem, recv_sem, head_send, head_recv, local_sem,
    ) = refs[len(shapes) :]
    loads = [pltpu.make_async_copy(ins[i], loaded[i], in_sem.at[i]) for i in range(12)]
    for i in (2, 3, 4, 5, 6, 7, 8, 9, 0, 10, 11, 1):
        loads[i].start()
    stores = [
        pltpu.make_async_copy(source, outs[i], out_sem.at[i])
        for i, source in enumerate((final, input_grad, out_q, out_fc, out_p, out_v))
    ]
    place_q, place_p = placing.at[:, 0:128], placing.at[:, 128:192]
    spread, spread_fc = spreads.at[:, 0:WIDTH], spreads.at[:, WIDTH:]
    at, core = place()
    ctx = lax.axis_index("ctx")
    spot = at["x"] * 2 + core
    is_head, my_head = head_at(ctx, lax.rem(at["z"], 2))
    twin = device(at, 1 - core)
    mail = Mail(send_sem, recv_sem, twin)

    known = [{"ctx": lax.rem(ctx + step, 16)} for step in range(1, 16)]
    known += [device(beside(at, "y", distance), core) for distance in (1, -1, 2)]
    known += [device(beside(at, "z", distance), core) for distance in (1, -1)]
    barrier = pltpu.get_barrier_semaphore()
    for target in known:
        pl.semaphore_signal(barrier, inc=1, device_id=target, device_id_type=MESH)

    pad_joint[...] = jnp.zeros_like(pad_joint)
    pad_fc[...] = jnp.zeros_like(pad_fc)
    pad_proj[...] = jnp.zeros_like(pad_proj)
    pad_small[...] = jnp.zeros_like(pad_small)
    for i in range(2, 10):
        loads[i].wait()
    pad_joint[0:6, 0 : 3 * WIDTH] = raw_qkv[0].astype(F32)
    pad_joint[0:6, 3 * WIDTH : HIDDEN] = raw_out[0].astype(F32)
    pad_fc[0:6, :] = raw_fc[0].astype(F32)
    reorder(pad_fc, hidden_order(), lambda t, value: pad_joint.__setitem__(
        (slice(0, 8), slice(HIDDEN + 128 * t, HIDDEN + 128 * t + 128)), value))
    for group in range(8):
        for half in range(2):
            first = HIDDEN * half + 384 * group
            w_joint[group, :, 384 * half : 384 * half + 384] = pad_joint[:, first : first + 384].astype(BF)
    pad_proj[0:24, :] = raw_proj[0].astype(F32)
    for half in range(2):
        w_proj[half] = pad_proj[:, 384 * half : 384 * half + 384].astype(BF)
    pad_small[0:2, 0:6] = raw_gains[0].astype(F32)
    pad_small[2:8, 0:6] = raw_biases[0].astype(F32)
    pad_small[8:9, 0:24] = raw_fc_bias[...].astype(F32)
    pl.semaphore_wait(barrier, len(known))

    def group_sends(source, target):
        waits = []
        for step in range(1, 8):
            other = lax.rem(spot + step, 8)
            origin = lax.rem(spot + 8 - step, 8)
            peer = device({**at, "x": lax.div(other, 2)}, lax.rem(other, 2))
            waits.append((mail.send(source.at[other], target.at[spot], peer), target.at[origin]))
        target[spot] = source[spot]
        return waits

    def pair_sends(source, target):
        key = mail.send(source.at[1 - core], target.at[core], twin)
        target[core] = source[core]
        return [(key, target.at[1 - core])]

    def receive(waits):
        for wait in waits:
            mail.receive(*wait)

    def head_span(ref, who):
        return ref.at[:, pl.ds(pl.multiple_of(who * 128, 128), 128)]

    def head_copy(turn, step, source, target, peer):
        return pltpu.make_async_remote_copy(
            source, target, head_send.at[turn, step], head_recv.at[turn, step],
            device_id={"ctx": peer}, device_id_type=MESH,
        )

    z_lo = lax.rem(at["z"], 2)

    def to_heads(turn, block, out):
        for step in range(1, 16):
            peer = lax.rem(ctx + step, 16)
            has, head = head_at(peer, z_lo)

            @pl.when(has)
            def _():
                head_copy(turn, step, block.at[head], head_span(out, ctx), peer).start()

        @pl.when(is_head)
        def _():
            pltpu.make_async_copy(block.at[my_head], head_span(out, ctx), local_sem.at[turn]).start()

    def to_heads_received(turn, block, out):
        @pl.when(is_head)
        def _():
            for step in range(1, 16):
                source = lax.rem(ctx + 16 - step, 16)
                head_copy(turn, step, head_span(out, source), head_span(out, source), source).wait_recv()
            pltpu.make_async_copy(block.at[my_head], head_span(out, ctx), local_sem.at[turn]).wait()

    def to_heads_sent(turn, block, out):
        for step in range(1, 16):
            peer = lax.rem(ctx + step, 16)
            has, head = head_at(peer, z_lo)

            @pl.when(has)
            def _():
                head_copy(turn, step, block.at[head], head_span(out, ctx), peer).wait_send()

    def from_heads(turn, blocks, out):
        @pl.when(is_head)
        def _():
            for step in range(1, 16):
                peer = lax.rem(ctx + step, 16)
                head_copy(turn, step, blocks.at[peer], out.at[my_head], peer).start()
            pltpu.make_async_copy(blocks.at[ctx], out.at[my_head], local_sem.at[turn]).start()

    def from_heads_received(turn, blocks, out):
        for step in range(1, 16):
            source = lax.rem(ctx + 16 - step, 16)
            has, head = head_at(source, z_lo)

            @pl.when(has)
            def _():
                head_copy(turn, step, out.at[head], out.at[head], source).wait_recv()

        @pl.when(is_head)
        def _():
            pltpu.make_async_copy(blocks.at[ctx], out.at[my_head], local_sem.at[turn]).wait()

    def from_heads_sent(turn, blocks, out):
        @pl.when(is_head)
        def _():
            for step in range(1, 16):
                peer = lax.rem(ctx + step, 16)
                head_copy(turn, step, blocks.at[peer], out.at[my_head], peer).wait_send()

    zl, zh = split_z(at["z"])
    waits = group_sends(w_joint, in_joint) + pair_sends(w_proj, in_proj)
    weights[2][zl, at["y"], zh, at["x"], core] = pad_small[...].astype(BF)
    receive(waits)
    rows = dot(place_q[...], in_joint[...].reshape(128, WIDTH)).astype(BF)
    proj_rows = dot(place_p[...], in_proj[...].reshape(64, 384)).astype(BF)
    for tile in range(3):
        span = columns_of(tile)
        weights[0][at["x"], 3 * core + tile, zl, at["y"], zh] = rows[:, span]
        weights[1][at["x"], 6 * core + 2 * tile, zl, at["y"], zh] = rows[:, 384 + 128 * tile : 512 + 128 * tile]
        weights[1][at["x"], 6 * core + 2 * tile + 1, zl, at["y"], zh] = proj_rows[:, span]

    first = Gather(mail, weights, ATTENTION + SMALL, at, core)
    second = Gather(mail, weights, FORWARD, at, core)
    first.straight(0)
    second.straight(0)
    first.straight(1)
    first.ring()
    loads[0].wait()
    xhat, _ = normalize(x[0])
    first.pass_on()
    second.straight(1)
    first.last()
    first.finish()

    loads[10].wait()
    loads[11].wait()
    small_rows = weights[2][...].reshape(2048, 128)
    found = jnp.zeros((16, WIDTH), F32)
    for group in range(8):
        wide = dot(small_rows[256 * group : 256 * group + 256], spread[...]).reshape(16, 16, WIDTH)
        found = found + jnp.sum(jnp.where(width_mask(16 * group), wide, 0.0), axis=0)
    vectors[...] = found
    tall = small_rows.astype(F32).reshape(128, 16, 128)
    eighth = lax.broadcasted_iota(jnp.int32, (128, 16, 128), 1) == 8
    fc_rows = jnp.sum(jnp.where(eighth, tall, 0.0), axis=1).astype(BF)
    hidden_bias[...] = sum_rows(jnp.where(hidden_mask(columns[...]), dot(fc_rows, spread_fc[...]), 0.0))
    normed_rows = (xhat * vectors[0:1] + vectors[2:3]).astype(BF)
    normed[...] = normed_rows

    def joint_tiles(start, count):
        tiles = [weights[0][t // 6, t % 6].reshape(WIDTH, 128) for t in range(start, start + count)]
        return jnp.concatenate(tiles, axis=1)

    for pair in range(9):
        kind, offset = pair // 3, (pair % 3) * 256
        out = dot(normed_rows, joint_tiles(2 * pair, 2))
        if kind != 1:
            out = out + vectors[3 + kind // 2 : 4 + kind // 2, offset : offset + 256]
        out = flip(out.astype(BF))
        for head in range(4):
            qkv_t[offset // 64 + head, 64 * kind : 64 * kind + 64, :] = out[64 * head : 64 * head + 64]
    to_heads(0, qkv_t, landed)
    second.ring()
    to_heads_received(0, qkv_t, landed)

    @pl.when(is_head)
    def _():
        order_heads(landed, ordered, natural)
        for step in range(4):
            attend(step, ordered, natural, out_t, log_total)

    second.pass_on()

    @pl.when(is_head)
    def _():
        for step in range(4, 2048 // TILE):
            attend(step, ordered, natural, out_t, log_total)
        for block in range(16):
            att_blocks[block] = position_block(lambda t: out_t[:, columns_of(t)], block).astype(BF)

    from_heads(1, att_blocks, att_t)
    second.last()
    second.finish()
    from_heads_received(1, att_blocks, att_t)

    rows_t = att_t[...].reshape(WIDTH, 128)
    mat_out = joint_tiles(18, 6)
    middle = x[0] + dot(flip(rows_t), mat_out) + vectors[5:6]
    xhat, factor = normalize(middle)
    normed_two = (xhat * vectors[1:2] + vectors[6:7]).astype(BF)
    normed_t = flip(normed_two)
    loads[1].wait()
    gradient = cotangent[0]
    d_two = gradient.astype(BF)
    d_norm = jnp.zeros((128, WIDTH), F32)
    twin_waits = {}
    for chunk in range(4):
        tile = lambda half, t: weights[1][chunk, 2 * t + half].reshape(WIDTH, 128)
        mat_fc = jnp.concatenate([tile(0, t) for t in range(6)], axis=1)
        mat_proj = jnp.concatenate([tile(1, t) for t in range(6)], axis=1)
        span = slice(WIDTH * chunk, WIDTH * chunk + WIDTH)
        pre = dot(normed_two, mat_fc) + hidden_bias[:, span]
        root = 0.7978845608028654
        inner = jnp.tanh(root * (pre + 0.044715 * (pre * pre * pre)))
        activated = (0.5 * pre * (1.0 + inner)).astype(BF)
        slope = 0.5 * (1.0 + inner) + 0.5 * pre * (1.0 - inner * inner) * (
            root * (1.0 + 3 * 0.044715 * (pre * pre))
        )
        update = dot(activated, mat_proj)
        final[...] = update if chunk == 0 else final[...] + update
        d_pre = (dot_right_t(d_two, mat_proj) * slope).astype(BF)
        grad_hidden[:, span] = sum_rows(d_pre.astype(F32))
        update = dot_right_t(d_pre, mat_fc)
        input_grad[...] = update if chunk == 0 else input_grad[...] + update
        grad_fc = dot(normed_t, d_pre).astype(BF)
        grad_proj = dot_left_t(activated, d_two).astype(BF)
        for t in range(6):
            grads[1][chunk, 2 * t] = grad_fc[:, columns_of(t)].reshape(2, 4, 2, 48, 128)
            grads[1][chunk, 2 * t + 1] = grad_proj[:, columns_of(t)].reshape(2, 4, 2, 48, 128)
        key = mail.send(grads[1].at[chunk, pl.ds(6 * (1 - core), 6)], sums[1].at[chunk], twin)
        twin_waits[1, chunk] = key
    final[...] = middle + final[...] + vectors[7:8]
    stores[0].start()
    d_norm = input_grad[...]
    d_mid = gradient + norm_back(d_norm, xhat, factor, vectors[1:2])
    d_middle[...] = d_mid
    d_one = d_mid.astype(BF)
    d_att_t[...] = dot_right_t(mat_out, d_one).astype(BF).reshape(HEADS, 64, 128)
    to_heads(2, d_att_t, landed_back)
    grad_out = dot(rows_t, d_one).astype(BF)
    for t in range(6):
        grads[0][3, t] = grad_out[:, columns_of(t)].reshape(2, 4, 2, 48, 128)
    twin_waits[0, 3] = mail.send(grads[0].at[3, pl.ds(3 * (1 - core), 3)], sums[0].at[3], twin)
    grad_vectors[...] = jnp.zeros_like(grad_vectors)
    grad_vectors[1:2] = sum_rows(d_norm * xhat)
    grad_vectors[5:6] = sum_rows(d_one.astype(F32))
    grad_vectors[6:7] = sum_rows(d_norm)
    grad_vectors[7:8] = sum_rows(d_two.astype(F32))

    def add_twin(kind, chunk):
        mail.receive(twin_waits[kind, chunk], sums[kind].at[chunk])
        count = 3 * (kind + 1)
        added(sums[kind].at[chunk], grads[kind].at[chunk, pl.ds(count * core, count)])

    back_second = Reduce(mail, sums, landing, FORWARD, at, core)
    for chunk in range(4):
        add_twin(1, chunk)
    back_second.ring()
    add_twin(0, 3)

    to_heads_received(2, d_att_t, landed_back)

    @pl.when(is_head)
    def _():
        order_back(landed_back, ordered, d_out, values_natural)
        for step in range(5):
            attend_back(step, ordered, natural, values_natural, out_t, log_total, d_out, d_t, d_keys)

    back_second.pass_on()

    @pl.when(is_head)
    def _():
        for step in range(5, 2048 // TILE):
            attend_back(step, ordered, natural, values_natural, out_t, log_total, d_out, d_t, d_keys)
        for tile in range(16):
            d_t[64:192, columns_of(tile)] = d_keys[columns_of(tile), :].T.astype(BF)
        for block in range(16):
            d_blocks[block] = position_block(lambda t: d_t[:, columns_of(t)].astype(F32), block).astype(BF)

    from_heads(3, d_blocks, d_rows)
    back_second.collect_ring()
    back_second.straight(1)
    from_heads_received(3, d_blocks, d_rows)

    for head in range(HEADS):
        rows = flip(d_rows[head])
        for kind in range(3):
            offset = WIDTH * kind + 64 * head
            d_qkv[:, offset : offset + 64] = rows[:, 64 * kind : 64 * kind + 64]
    normed_t = flip(normed[...])
    for pair in range(9):
        out = dot(normed_t, d_qkv[:, 256 * pair : 256 * pair + 256]).astype(BF)
        for t in range(2):
            tile = 2 * pair + t
            grads[0][tile // 6, tile % 6] = out[:, columns_of(t)].reshape(2, 4, 2, 48, 128)
        if pair % 3 == 2:
            chunk = pair // 3
            source = grads[0].at[chunk, pl.ds(3 * (1 - core), 3)]
            twin_waits[0, chunk] = mail.send(source, sums[0].at[chunk], twin)
    back_second.collect(1)
    back_second.straight(2)
    d_norm = jnp.zeros((128, WIDTH), F32)
    for pair in range(9):
        d_norm = d_norm + dot_right_t(d_qkv[:, 256 * pair : 256 * pair + 256], joint_tiles(2 * pair, 2))
    back_first = Reduce(mail, sums, landing, ATTENTION, at, core)
    for chunk in range(3):
        add_twin(0, chunk)
    back_first.ring()
    xhat, factor = normalize(x[0])
    input_grad[...] = d_middle[...] + norm_back(d_norm, xhat, factor, vectors[0:1])
    stores[1].start()
    kinds = lambda kind: sum_rows(d_qkv[:, WIDTH * kind : WIDTH * kind + WIDTH].astype(F32))
    row = lax.broadcasted_iota(jnp.int32, (16, WIDTH), 0)
    found = grad_vectors[...]
    for which, value in ((0, sum_rows(d_norm * xhat)), (2, sum_rows(d_norm)), (3, kinds(0)), (4, kinds(2))):
        found = jnp.where(row == which, value, found)
    small = []
    for group in range(8):
        wide = jnp.where(width_mask(16 * group), jnp.broadcast_to(found[None], (16, 16, WIDTH)), 0.0)
        small.append(dot_right_t(wide.astype(BF).reshape(256, WIDTH), spread[...]).reshape(16, 16, 128))
    small = jnp.concatenate(small, axis=0)
    wide = jnp.where(hidden_mask(columns[...]), jnp.broadcast_to(grad_hidden[...], (128, HIDDEN)), 0.0)
    hidden = dot_right_t(wide.astype(BF), spread_fc[...])
    eighth = lax.broadcasted_iota(jnp.int32, (128, 16, 128), 1) == 8
    small = jnp.where(eighth, hidden[:, None, :], small)
    grads[2][...] = small.astype(BF).reshape(SHAPES[2])
    every = {axis: ALL for axis in AXES}
    key = mail.send(view(grads, (2, 0), every, 1 - core), sums[2], twin)

    back_second.collect(2)
    mine = [view(sums, sub, at, None) for sub in FORWARD]
    rows = jnp.concatenate([mine[t][0] for t in range(3)], axis=1)
    last_fc[...] = dot_left_t(place_q[...], rows).astype(BF).reshape(8, 16, 384)
    rows = jnp.concatenate([mine[t][1] for t in range(3)], axis=1)
    last_p[...] = dot_left_t(place_p[...], rows).astype(BF).reshape(2, 32, 384)
    waits = group_sends(last_fc, back_fc) + pair_sends(last_p, back_p)
    mail.receive(key, sums[2])
    added(sums[2], view(grads, (2, 0), every, core))
    back_small = Reduce(mail, sums, landing, SMALL, at, core)
    back_small.straight(0)

    back_first.pass_on()
    back_small.collect(0)
    back_small.straight(1)
    back_first.collect_ring()
    back_first.straight(1)
    back_small.collect(1)
    back_small.straight(2)
    receive(waits)
    for group in range(8):
        pad_fc[:, 384 * group : 384 * group + 384] = back_fc[group].astype(F32)[:8]
    reorder(pad_fc, np.argsort(hidden_order()), lambda t, value: out_fc.__setitem__((ALL, columns_of(t)), value))
    stores[3].start()
    for half in range(2):
        out_p[:, 384 * half : 384 * half + 384] = back_p[half].astype(F32)[:24]
    stores[4].start()
    back_first.collect(1)
    back_first.straight(2)
    back_small.collect(2)
    out_v[...] = view(sums, (2, 0), at, None)[...].astype(F32)
    stores[5].start()
    back_first.collect(2)
    rows = jnp.concatenate([view(sums, sub, at, None)[0] for sub in ATTENTION], axis=1)
    last_q[...] = dot_left_t(place_q[...], rows).astype(BF).reshape(8, 16, 384)
    receive(group_sends(last_q, back_q))
    for group in range(8):
        out_q[:, 384 * group : 384 * group + 384] = back_q[group].astype(F32)[:8]
    stores[2].start()

    mail.finish()
    to_heads_sent(0, qkv_t, landed)
    from_heads_sent(1, att_blocks, att_t)
    to_heads_sent(2, d_att_t, landed_back)
    from_heads_sent(3, d_blocks, d_rows)
    for store in stores:
        store.wait()


def place_rows(groups, rows, padded):
    found = np.zeros((groups * rows, groups * padded), np.float32)
    for group in range(groups):
        for row in range(rows):
            found[group * rows + row, group * padded + row] = 1
    return found


def spread_matrix(entries, each):
    found = np.zeros((128, len(entries)), np.float32)
    found[entries % each, np.arange(len(entries))] = 1
    return found


def local(tokens, cotangent, w_qkv, w_out, w_fc, w_proj, gains, biases, fc_bias):
    order = hidden_order()
    placing = np.concatenate([place_rows(8, 6, 16), place_rows(2, 24, 32)], axis=1)
    spreads = np.concatenate([spread_matrix(np.arange(WIDTH), 6), spread_matrix(order, 24)], axis=1)
    given = (tokens, cotangent, w_qkv, w_out, w_fc, w_proj, gains, biases, fc_bias)
    given += (jnp.asarray(placing, BF), jnp.asarray(spreads, BF), jnp.asarray(order.reshape(1, HIDDEN), jnp.int32))
    results = ((128, WIDTH), (128, WIDTH), (8, HIDDEN), (8, HIDDEN), (24, WIDTH), (16, 128))
    scratch = [VMEM(item.shape, item.dtype) for item in given]
    scratch += [VMEM(shape, F32) for shape in results]
    scratch += [VMEM(shape, BF) for shape in SHAPES + SHAPES + SUMS + tuple(landing_shapes().values())]
    scratch += [
        VMEM((16, 2 * HIDDEN), F32),
        VMEM((8, HIDDEN), F32),
        VMEM((32, WIDTH), F32),
        VMEM((16, 128), F32),
        VMEM((8, 16, WIDTH), BF),
        VMEM((2, 32, 384), BF),
        pltpu.SemaphoreType.DMA((12,)),
        pltpu.SemaphoreType.DMA((6,)),
        VMEM((8, 16, WIDTH), BF),
        VMEM((2, 32, 384), BF),
        VMEM((8, 16, 384), BF),
        VMEM((8, 16, 384), BF),
        VMEM((2, 32, 384), BF),
        VMEM((8, 16, 384), BF),
        VMEM((8, 16, 384), BF),
        VMEM((2, 32, 384), BF),
        VMEM((128, WIDTH), BF),
        VMEM((16, WIDTH), F32),
        VMEM((1, HIDDEN), F32),
        VMEM((HEADS, 192, 128), BF),
        VMEM((192, 2048), BF),
        VMEM((192, 2048), BF),
        VMEM((2048, 128), BF),
        VMEM((64, 2048), F32),
        VMEM((8, 2048), F32),
        VMEM((16, 64, 128), BF),
        VMEM((HEADS, 64, 128), BF),
        VMEM((128, WIDTH), F32),
        VMEM((HEADS, 64, 128), BF),
        VMEM((64, 2048), BF),
        VMEM((64, 2048), BF),
        VMEM((2048, 128), BF),
        VMEM((192, 2048), BF),
        VMEM((2048, 128), F32),
        VMEM((16, 192, 128), BF),
        VMEM((HEADS, 192, 128), BF),
        VMEM((128, 3 * WIDTH), BF),
        VMEM((16, WIDTH), F32),
        VMEM((1, HIDDEN), F32),
        pltpu.SemaphoreType.DMA((COPIES,)),
        pltpu.SemaphoreType.DMA((COPIES,)),
        pltpu.SemaphoreType.DMA((4, 16)),
        pltpu.SemaphoreType.DMA((4, 16)),
        pltpu.SemaphoreType.DMA((4,)),
    ]
    stay = pl.BlockSpec(memory_space=pl.ANY)
    found = pl.pallas_call(
        layer_kernel,
        out_shape=[jax.ShapeDtypeStruct(shape, F32) for shape in results],
        in_specs=[stay] * 12,
        out_specs=[stay] * 6,
        scratch_shapes=scratch,
        compiler_params=pltpu.CompilerParams(
            collective_id=0, has_side_effects=True, vmem_limit_bytes=VMEM_LIMIT * MEGA
        ),
        name="layer",
    )(*given)
    shapes = (
        (128, WIDTH), (128, WIDTH), (6, 1, 3 * WIDTH), (6, 1, WIDTH), (6, 1, HIDDEN), (24, WIDTH),
        (2, 6), (6, 1, 6), (1, 24),
    )
    parts = [shapes[i] for i in (2, 3, 4, 6, 7, 8)]
    final, input_grad, qkv, out, fc, proj, d_gains, d_biases, d_fc_bias = pl.pallas_call(
        results_kernel,
        out_shape=[jax.ShapeDtypeStruct(shape, F32) for shape in shapes],
        in_specs=[stay] * 6,
        out_specs=[stay] * 9,
        scratch_shapes=[VMEM(shape, F32) for shape in [results[2], results[3], results[5]] + parts]
        + [pltpu.SemaphoreType.DMA((3,)), pltpu.SemaphoreType.DMA((9,))],
        compiler_params=pltpu.CompilerParams(vmem_limit_bytes=VMEM_LIMIT * MEGA),
        name="results",
    )(*found)
    rows_first = lambda value: jnp.transpose(value, (1, 0, 2))
    return (
        final[None],
        input_grad[None],
        rows_first(qkv),
        rows_first(out),
        rows_first(fc),
        proj[None],
        d_gains[None],
        rows_first(d_biases),
        d_fc_bias,
    )


VMEM_LIMIT = 63


def solution(mesh):
    rows = P("dp", "ctx", None)
    weight = P(None, ("dp", "ctx"), None)
    vector = P(None, None, ("dp", "ctx"))
    tail = (weight,) * 4 + (vector, vector, P(None, ("dp", "ctx")))
    return jax.shard_map(
        local, mesh=mesh, in_specs=(rows, rows) + tail, out_specs=(rows, rows) + tail, check_vma=False
    )
```

```python
import jax
import jax.numpy as jnp
import numpy as np
from jax import lax
from jax.experimental import pallas as pl
from jax.experimental.pallas import tpu as pltpu
from jax.sharding import PartitionSpec as P

BF = jnp.bfloat16
F32 = jnp.float32
MESH = pl.DeviceIdType.MESH
VMEM = pltpu.VMEM
ALL = slice(None)
AXES = ("x", "y", "z")
GATHER_ORDER = (("x", "y", "z"), ("y", "z", "x"), ("z", "x", "y"))
REDUCE_ORDER = tuple(order[::-1] for order in GATHER_ORDER)
SHAPES = ((4, 6, 2, 4, 2, 48, 128), (4, 12, 2, 4, 2, 48, 128), (2, 4, 2, 4, 2, 16, 128))
SUMS = ((4, 3, 2, 4, 2, 48, 128), (4, 6, 2, 4, 2, 48, 128), (2, 4, 2, 4, 16, 128))
ATTENTION = ((0, 0), (0, 1), (0, 2))
FORWARD = ((1, 0), (1, 1), (1, 2))
SMALL = ((2, 0),)
HEADS = 12
WIDTH = 768
HIDDEN = 3072
NORM_EPS = 1e-05
MASKED = -1e30
MEGA = 1024 * 1024
COPIES = 211
IN_FLIGHT = 48


def place():
    dp = lax.axis_index("dp")
    ctx = lax.axis_index("ctx")
    at = {
        "x": lax.rem(lax.div(ctx, 2), 4),
        "y": lax.rem(dp, 4),
        "z": lax.div(ctx, 8) * 2 + lax.div(dp, 4),
    }
    return at, lax.rem(ctx, 2)


def device(at, core):
    return {
        "dp": lax.rem(at["z"], 2) * 4 + at["y"],
        "ctx": lax.div(at["z"], 2) * 8 + at["x"] * 2 + core,
    }


def head_at(ctx, z_lo):
    z_hi, x, core = lax.div(ctx, 8), lax.rem(lax.div(ctx, 2), 4), lax.rem(ctx, 2)
    head = (1 - core) * (4 * z_hi + x) + core * (8 + 2 * z_hi + x - 2 * z_lo)
    return (core == 0) | (lax.div(x, 2) == z_lo), head


def beside(at, axis, distance):
    moved = dict(at)
    moved[axis] = lax.rem(at[axis] + (distance + 4), 4)
    return moved


def split_z(z):
    if isinstance(z, tuple):
        return pl.ds(z[1], 1), ALL
    if isinstance(z, slice):
        return ALL, ALL
    return lax.rem(z, 2), lax.div(z, 2)


def line(value):
    return pl.ds(2 * value[1], 2) if isinstance(value, tuple) else value


def view(refs, sub, sel, core):
    kind, tile = sub
    x, y = line(sel["x"]), line(sel["y"])
    zl, zh = split_z(sel["z"])
    if kind == 2:
        return refs[2].at[zl, y, zh, x] if core is None else refs[2].at[zl, y, zh, x, core]
    count = kind + 1
    start = count * tile + (0 if core is None else 3 * count * core)
    return refs[kind].at[x, pl.ds(start, count), zl, y, zh]


def block_shape(sub, gone, half_axis=None):
    extent = {axis: 1 if axis in gone else 4 for axis in AXES}
    if half_axis is not None:
        extent[half_axis] = 2
    lead = lambda name: () if extent[name] == 1 else (extent[name],)
    zl, zh = ((), ()) if extent["z"] == 1 else ((extent["z"] // 2,), (2,))
    if sub[0] == 2:
        return zl + lead("y") + zh + lead("x") + (16, 128)
    return lead("x") + (sub[0] + 1,) + zl + lead("y") + zh + (48, 128)


def landing_shapes():
    found = {}
    for sub in ATTENTION + FORWARD + SMALL:
        order = REDUCE_ORDER[sub[1]]
        for phase in range(3):
            gone = order[: phase + 1]
            if phase == 0 and sub[0] < 2:
                for half in range(2):
                    for use in range(3):
                        found[sub, phase, half, use] = block_shape(sub, gone, order[2])
            else:
                for use in range(3):
                    found[sub, phase, use] = block_shape(sub, gone)
    return found


def added(target, *terms):
    if len(target.shape) == 2:
        total = target[...].astype(F32)
        for term in terms:
            total = total + term[...].astype(F32)
        target[...] = total.astype(BF)
        return

    def step(i, carry):
        total = target[i].astype(F32)
        for term in terms:
            total = total + term[i].astype(F32)
        target[i] = total.astype(BF)
        return carry

    lax.fori_loop(0, target.shape[0], step, 0)


class Mail:
    def __init__(self, send_sem, recv_sem, anyone):
        self.send_sem, self.recv_sem, self.anyone = send_sem, recv_sem, anyone
        self.used, self.sent = 0, []

    def send(self, source, target, device_id):
        key = self.used
        if key >= IN_FLIGHT:
            self.sent[key - IN_FLIGHT].wait_send()
        copy = pltpu.make_async_remote_copy(
            src_ref=source,
            dst_ref=target,
            send_sem=self.send_sem.at[key % IN_FLIGHT],
            recv_sem=self.recv_sem.at[key],
            device_id=device_id,
            device_id_type=MESH,
        )
        copy.start()
        self.sent.append(copy)
        self.used += 1
        return key

    def receive(self, key, arrival):
        pltpu.make_async_remote_copy(
            src_ref=arrival,
            dst_ref=arrival,
            send_sem=self.send_sem.at[key % IN_FLIGHT],
            recv_sem=self.recv_sem.at[key],
            device_id=self.anyone,
            device_id_type=MESH,
        ).wait_recv()

    def finish(self):
        for copy in self.sent[-IN_FLIGHT:]:
            copy.wait_send()
        assert self.used == COPIES, self.used


class Gather:
    def __init__(self, mail, refs, subs, at, core):
        self.mail, self.refs, self.subs, self.at, self.core = mail, refs, subs, at, core
        self.twin = device(at, 1 - core)
        self.pending, self.twins = [], []

    def sel(self, sub, phase):
        found = dict(self.at)
        for done in GATHER_ORDER[sub[1]][:phase]:
            found[done] = ALL
        return found

    def mine(self, sub, sel):
        return view(self.refs, sub, sel, self.core)

    def peer(self, axis, distance):
        return device(beside(self.at, axis, distance), self.core)

    def to_twin(self, sub, sel):
        source = self.mine(sub, sel)
        self.twins.append((self.mail.send(source, source, self.twin), view(self.refs, sub, sel, 1 - self.core)))

    def collect(self):
        for wait in self.pending:
            self.mail.receive(*wait)
        self.pending = []

    def straight(self, phase):
        self.collect()
        for sub in self.subs:
            axis, sel = GATHER_ORDER[sub[1]][phase], self.sel(sub, phase)
            source = self.mine(sub, sel)
            for distance in (1, -1, 2):
                key = self.mail.send(source, source, self.peer(axis, distance))
                self.pending.append((key, self.mine(sub, beside(sel, axis, -distance))))

    def ring(self):
        self.collect()
        self.keys = []
        for sub in self.subs:
            axis, sel = GATHER_ORDER[sub[1]][2], self.sel(sub, 2)
            source = self.mine(sub, sel)
            self.keys.append([self.mail.send(source, source, self.peer(axis, d)) for d in (1, -1)])
        for sub in self.subs:
            self.to_twin(sub, self.sel(sub, 2))

    def pass_on(self):
        for sub, keys in zip(self.subs, self.keys):
            order = GATHER_ORDER[sub[1]]
            axis, sel = order[2], self.sel(sub, 2)
            for half, distance in ((0, 1), (1, -1)):
                arrived, far = beside(sel, axis, -distance), beside(sel, axis, 2)
                self.mail.receive(keys[half], self.mine(sub, arrived))
                moving = self.mine(sub, {**arrived, order[0]: ("half", half)})
                coming = self.mine(sub, {**far, order[0]: ("half", half)})
                self.pending.append((self.mail.send(moving, moving, self.peer(axis, distance)), coming))
        for sub in self.subs:
            for distance in (1, -1):
                self.to_twin(sub, beside(self.sel(sub, 2), GATHER_ORDER[sub[1]][2], distance))

    def last(self):
        self.collect()
        for sub in self.subs:
            self.to_twin(sub, beside(self.sel(sub, 2), GATHER_ORDER[sub[1]][2], 2))

    def finish(self):
        for wait in self.twins:
            self.mail.receive(*wait)


class Reduce:
    def __init__(self, mail, sums, landing, subs, at, core):
        self.mail, self.sums, self.landing, self.subs, self.at, self.core = mail, sums, landing, subs, at, core
        self.kept = {}

    def sel(self, sub, phase):
        found = dict(self.at)
        for later in REDUCE_ORDER[sub[1]][phase + 1 :]:
            found[later] = ALL
        return found

    def mine(self, sub, sel, half=None):
        if half is not None:
            sel = {**sel, REDUCE_ORDER[sub[1]][2]: ("half", half)}
        return view(self.sums, sub, sel, None)

    def peer(self, axis, distance):
        return device(beside(self.at, axis, distance), self.core)

    def ring(self):
        for sub in self.subs:
            axis, sel, land = REDUCE_ORDER[sub[1]][0], self.sel(sub, 0), self.landing
            plus, minus = self.peer(axis, 1), self.peer(axis, -1)
            far, up, down = beside(sel, axis, 2), beside(sel, axis, 1), beside(sel, axis, -1)
            self.kept[sub] = [
                self.mail.send(self.mine(sub, far, 0), land[sub, 0, 0, 0], plus),
                self.mail.send(self.mine(sub, far, 1), land[sub, 0, 1, 0], minus),
                self.mail.send(self.mine(sub, up, 1), land[sub, 0, 1, 1], plus),
                self.mail.send(self.mine(sub, down, 0), land[sub, 0, 0, 2], minus),
            ]

    def pass_on(self):
        for sub in self.subs:
            axis, sel, land = REDUCE_ORDER[sub[1]][0], self.sel(sub, 0), self.landing
            keys = self.kept[sub]
            for half, distance in ((0, 1), (1, -1)):
                self.mail.receive(keys[half], land[sub, 0, half, 0])
                moving = self.mine(sub, beside(sel, axis, distance), half)
                added(moving, land[sub, 0, half, 0])
                keys.append(self.mail.send(moving, land[sub, 0, half, 1 + half], self.peer(axis, distance)))

    def collect_ring(self):
        for sub in self.subs:
            sel, land, keys = self.sel(sub, 0), self.landing, self.kept[sub]
            for half, first, second in ((1, keys[2], keys[5]), (0, keys[4], keys[3])):
                self.mail.receive(first, land[sub, 0, half, 1])
                self.mail.receive(second, land[sub, 0, half, 2])
                added(self.mine(sub, sel, half), land[sub, 0, half, 1], land[sub, 0, half, 2])

    def straight(self, phase):
        for sub in self.subs:
            axis, sel = REDUCE_ORDER[sub[1]][phase], self.sel(sub, phase)
            self.kept[sub] = [
                self.mail.send(
                    self.mine(sub, beside(sel, axis, distance)),
                    self.landing[sub, phase, use],
                    self.peer(axis, distance),
                )
                for use, distance in enumerate((1, -1, 2))
            ]

    def collect(self, phase):
        for sub in self.subs:
            terms = [self.landing[sub, phase, use] for use in range(3)]
            for key, term in zip(self.kept[sub], terms):
                self.mail.receive(key, term)
            added(self.mine(sub, self.sel(sub, phase)), *terms)


def dot(left, right):
    return jnp.dot(left, right, preferred_element_type=F32)


def dot_right_t(left, right):
    return lax.dot_general(left, right, (((1,), (1,)), ((), ())), preferred_element_type=F32)


def dot_left_t(left, right):
    return lax.dot_general(left, right, (((0,), (0,)), ((), ())), preferred_element_type=F32)


def flip(values):
    return values.astype(F32).T.astype(BF)


def mean_last(values):
    return jnp.mean(values, axis=-1, keepdims=True)


def sum_rows(values):
    return jnp.sum(values, axis=0, keepdims=True)


def normalize(values):
    center = values - mean_last(values)
    factor = lax.rsqrt(mean_last(center * center) + NORM_EPS)
    return center * factor, factor


def norm_back(d_norm, xhat, factor, gain):
    e = d_norm * gain
    return factor * (e - mean_last(e) - xhat * mean_last(e * xhat))


def owner_mask(shape, column, each):
    owner = lax.broadcasted_iota(jnp.int32, shape, 0) * each
    return (column >= owner) & (column < owner + each)


def width_mask(first):
    shape = (16, 16, WIDTH)
    return owner_mask(shape, lax.broadcasted_iota(jnp.int32, shape, 2) - 6 * first, 6)


def hidden_mask(columns):
    shape = (128, HIDDEN)
    return owner_mask(shape, jnp.broadcast_to(columns, shape), 24)


def low_half(shape):
    return lax.broadcasted_iota(jnp.int32, shape, 1) < 64


def swap_halves(tile):
    return pltpu.roll(tile, 64, 1)


def position_tile(block, tile):
    if tile < 8:
        low, high = block(2 * tile), swap_halves(block(2 * tile + 1))
    else:
        low, high = swap_halves(block(31 - 2 * tile)), block(30 - 2 * tile)
    return jnp.where(low_half(low.shape), low, high)


def position_block(tile, block):
    early, late = tile(block // 2), tile((31 - block) // 2)
    if block % 2 == 0:
        return jnp.where(low_half(early.shape), early, late)
    return swap_halves(jnp.where(low_half(early.shape), late, early))


TILE = 256
KEYS = 1024


def columns_of(tile):
    return slice(128 * tile, 128 * tile + 128)


def causal(scores):
    key = lax.broadcasted_iota(jnp.int32, scores.shape, 0)
    query = lax.broadcasted_iota(jnp.int32, scores.shape, 1)
    return jnp.where(key <= query, scores, MASKED)


def query_columns(ordered, first):
    queries = ordered[0:64, first : first + TILE]
    return jnp.concatenate([jnp.zeros_like(queries), queries], axis=0)


def order_heads(landed, ordered, natural):
    for tile in range(16):
        found = position_tile(lambda b: landed[:, columns_of(b)].astype(F32), tile)
        found = jnp.concatenate([found[0:64] * 0.125, found[64:192]], axis=0)
        ordered[:, columns_of(tile)] = found.astype(BF)
        natural[columns_of(tile), :] = found[0:128].T.astype(BF)


def attend(step, ordered, natural, out_t, log_total):
    first = TILE * step
    count = first + TILE
    queries = query_columns(ordered, first)
    spans = [slice(first, count)] + ([slice(0, first)] if first else [])
    scores = [dot(natural[span, :], queries) for span in spans]
    scores[0] = causal(scores[0])
    best = jnp.max(scores[0], axis=0, keepdims=True)
    for part in scores[1:]:
        best = jnp.maximum(best, jnp.max(part, axis=0, keepdims=True))
    total = jnp.zeros((1, TILE), F32)
    out = jnp.zeros((64, TILE), F32)
    for span, part in zip(spans, scores):
        probs = jnp.exp(part - best)
        total = total + sum_rows(probs)
        out = out + dot(ordered[128:192, span], probs.astype(BF))
    out_t[:, first:count] = out / total
    log_total[0:1, first:count] = best + jnp.log(total)


def order_back(landed, ordered, d_out, values_natural):
    for tile in range(16):
        found = position_tile(lambda b: landed[:, columns_of(b)].astype(F32), tile)
        d_out[:, columns_of(tile)] = found.astype(BF)
        both = jnp.concatenate([ordered[128:192, columns_of(tile)].astype(F32), found], axis=0)
        values_natural[columns_of(tile), :] = both.T.astype(BF)


def attend_back(step, ordered, natural, values_natural, out_t, log_total, d_out, d_t, d_keys):
    first = TILE * step
    count = first + TILE
    queries = query_columns(ordered, first)
    log_here = log_total[0:1, first:count]
    d_low = d_out[:, first:count]
    delta = sum_rows(d_low.astype(F32) * out_t[:, first:count])
    d_low = jnp.concatenate([d_low, jnp.zeros_like(d_low)], axis=0)
    query_rows, d_rows = natural[first:count, :], values_natural[first:count, :]
    low = low_half(query_rows.shape)
    query_rows = jnp.where(low, query_rows, jnp.zeros_like(query_rows))
    d_rows = jnp.where(low, jnp.zeros_like(d_rows), d_rows)
    d_query = jnp.zeros((64, TILE), F32)
    for begin in [*range(0, first, KEYS), first]:
        end = count if begin == first else min(begin + KEYS, first)
        scores = dot(natural[begin:end, :], queries)
        if begin == first:
            scores = causal(scores)
        probs = jnp.exp(scores - log_here)
        d_scores = (probs * (dot(values_natural[begin:end, :], d_low) - delta)).astype(BF)
        d_query = d_query + dot(ordered[64:128, begin:end], d_scores)
        update = dot(d_scores, query_rows) + dot(probs.astype(BF), d_rows)
        if begin == first:
            d_keys[begin:end, :] = update
        else:
            d_keys[begin:end, :] += update
    d_t[0:64, first:count] = (d_query * 0.125).astype(BF)


def hidden_order():
    x, group, row = np.meshgrid(np.arange(4), np.arange(16), np.arange(48), indexing="ij")
    return (192 * group + 48 * x + row).reshape(-1)


def reorder(source, order, store):
    for tile in range(len(order) // 128):
        wanted = order[columns_of(tile)]
        lanes = lax.broadcasted_iota(jnp.int32, (8, 128), 1)
        found = jnp.zeros((8, 128), F32)
        begin = 0
        while begin < 128:
            end = begin + 1
            while end < 128 and wanted[end] == wanted[end - 1] + 1 and wanted[end] % 128:
                end += 1
            at = int(wanted[begin])
            piece = source[0:8, columns_of(at // 128)]
            shift = (begin - at) % 128
            if shift:
                piece = pltpu.roll(piece, shift, 1)
            found = jnp.where((lanes >= begin) & (lanes < end), piece, found)
            begin = end
        store(tile, found)


def results_kernel(
    final, input_grad, joint, hidden, proj, small,
    to_final, to_input, to_qkv, to_out, to_fc, to_proj, to_gains, to_biases, to_fc_bias,
    final_here, input_here, joint_here, hidden_here, proj_here, small_here,
    qkv, out, fc, gains, biases, fc_bias, in_sem, out_sem,
):
    pairs = (
        (joint, joint_here), (hidden, hidden_here), (small, small_here),
        (final, final_here), (input_grad, input_here), (proj, proj_here),
    )
    loads = [pltpu.make_async_copy(source, target, in_sem.at[i]) for i, (source, target) in enumerate(pairs)]
    pairs = (
        (final_here, to_final), (input_here, to_input), (proj_here, to_proj),
        (qkv, to_qkv), (out, to_out), (fc, to_fc), (gains, to_gains), (biases, to_biases), (fc_bias, to_fc_bias),
    )
    stores = [pltpu.make_async_copy(source, target, out_sem.at[i]) for i, (source, target) in enumerate(pairs)]
    for copy in loads:
        copy.start()
    for copy in loads[:3]:
        copy.wait()
    for row in range(6):
        qkv[row] = joint_here[row : row + 1, 0 : 3 * WIDTH]
        out[row] = joint_here[row : row + 1, 3 * WIDTH : HIDDEN]
        fc[row] = hidden_here[row : row + 1, :]
        biases[row] = small_here[2 + row : 3 + row, 0:6]
    gains[...] = small_here[0:2, 0:6]
    fc_bias[...] = small_here[8:9, 0:24]
    for copy in stores[3:]:
        copy.start()
    for load, store in zip(loads[3:], stores[:3]):
        load.wait()
        store.start()
    for copy in stores:
        copy.wait()


def layer_kernel(*refs):
    shapes = landing_shapes()
    ins, outs, refs = refs[:12], refs[12:18], refs[18:]
    loaded, refs = refs[:12], refs[12:]
    x, cotangent, raw_qkv, raw_out, raw_fc, raw_proj, raw_gains, raw_biases, raw_fc_bias, placing, spreads, columns = loaded
    final, input_grad, out_q, out_fc, out_p, out_v = refs[:6]
    weights, grads, sums = refs[6:9], refs[9:12], refs[12:15]
    refs = refs[15:]
    landing = dict(zip(shapes, refs[: len(shapes)]))
    (
        pad_joint, pad_fc, pad_proj, pad_small, w_joint, w_proj, in_sem, out_sem,
        in_joint, in_proj, last_q, last_fc, last_p, back_q, back_fc, back_p,
        normed, vectors, hidden_bias, qkv_t, landed, ordered, natural, out_t, log_total, att_blocks, att_t,
        d_middle, d_att_t, landed_back, d_out, values_natural, d_t, d_keys, d_blocks,
        d_rows, d_qkv, grad_vectors, grad_hidden,
        send_sem, recv_sem, head_send, head_recv, local_sem,
    ) = refs[len(shapes) :]
    loads = [pltpu.make_async_copy(ins[i], loaded[i], in_sem.at[i]) for i in range(12)]
    for i in (2, 3, 4, 5, 6, 7, 8, 9, 0, 10, 11, 1):
        loads[i].start()
    stores = [
        pltpu.make_async_copy(source, outs[i], out_sem.at[i])
        for i, source in enumerate((final, input_grad, out_q, out_fc, out_p, out_v))
    ]
    place_q, place_p = placing.at[:, 0:128], placing.at[:, 128:192]
    spread, spread_fc = spreads.at[:, 0:WIDTH], spreads.at[:, WIDTH:]
    at, core = place()
    ctx = lax.axis_index("ctx")
    spot = at["x"] * 2 + core
    is_head, my_head = head_at(ctx, lax.rem(at["z"], 2))
    twin = device(at, 1 - core)
    mail = Mail(send_sem, recv_sem, twin)

    known = [{"ctx": lax.rem(ctx + step, 16)} for step in range(1, 16)]
    known += [device(beside(at, "y", distance), core) for distance in (1, -1, 2)]
    known += [device(beside(at, "z", distance), core) for distance in (1, -1)]
    barrier = pltpu.get_barrier_semaphore()
    for target in known:
        pl.semaphore_signal(barrier, inc=1, device_id=target, device_id_type=MESH)

    pad_joint[...] = jnp.zeros_like(pad_joint)
    pad_fc[...] = jnp.zeros_like(pad_fc)
    pad_proj[...] = jnp.zeros_like(pad_proj)
    pad_small[...] = jnp.zeros_like(pad_small)
    for i in range(2, 10):
        loads[i].wait()
    pad_joint[0:6, 0 : 3 * WIDTH] = raw_qkv[0].astype(F32)
    pad_joint[0:6, 3 * WIDTH : HIDDEN] = raw_out[0].astype(F32)
    pad_fc[0:6, :] = raw_fc[0].astype(F32)
    reorder(pad_fc, hidden_order(), lambda t, value: pad_joint.__setitem__(
        (slice(0, 8), slice(HIDDEN + 128 * t, HIDDEN + 128 * t + 128)), value))
    for group in range(8):
        for half in range(2):
            first = HIDDEN * half + 384 * group
            w_joint[group, :, 384 * half : 384 * half + 384] = pad_joint[:, first : first + 384].astype(BF)
    pad_proj[0:24, :] = raw_proj[0].astype(F32)
    for half in range(2):
        w_proj[half] = pad_proj[:, 384 * half : 384 * half + 384].astype(BF)
    pad_small[0:2, 0:6] = raw_gains[0].astype(F32)
    pad_small[2:8, 0:6] = raw_biases[0].astype(F32)
    pad_small[8:9, 0:24] = raw_fc_bias[...].astype(F32)
    pl.semaphore_wait(barrier, len(known))

    def group_sends(source, target):
        waits = []
        for step in range(1, 8):
            other = lax.rem(spot + step, 8)
            origin = lax.rem(spot + 8 - step, 8)
            peer = device({**at, "x": lax.div(other, 2)}, lax.rem(other, 2))
            waits.append((mail.send(source.at[other], target.at[spot], peer), target.at[origin]))
        target[spot] = source[spot]
        return waits

    def pair_sends(source, target):
        key = mail.send(source.at[1 - core], target.at[core], twin)
        target[core] = source[core]
        return [(key, target.at[1 - core])]

    def receive(waits):
        for wait in waits:
            mail.receive(*wait)

    def head_span(ref, who):
        return ref.at[:, pl.ds(pl.multiple_of(who * 128, 128), 128)]

    def head_copy(turn, step, source, target, peer):
        return pltpu.make_async_remote_copy(
            source, target, head_send.at[turn % 2, step], head_recv.at[turn % 2, step],
            device_id={"ctx": peer}, device_id_type=MESH,
        )

    z_lo = lax.rem(at["z"], 2)

    def to_heads(turn, block, out):
        for step in range(1, 16):
            peer = lax.rem(ctx + step, 16)
            has, head = head_at(peer, z_lo)

            @pl.when(has)
            def _():
                head_copy(turn, step, block.at[head], head_span(out, ctx), peer).start()

        @pl.when(is_head)
        def _():
            pltpu.make_async_copy(block.at[my_head], head_span(out, ctx), local_sem.at[turn]).start()

    def to_heads_received(turn, block, out):
        @pl.when(is_head)
        def _():
            for step in range(1, 16):
                source = lax.rem(ctx + 16 - step, 16)
                head_copy(turn, step, head_span(out, source), head_span(out, source), source).wait_recv()
            pltpu.make_async_copy(block.at[my_head], head_span(out, ctx), local_sem.at[turn]).wait()

    def to_heads_sent(turn, block, out):
        for step in range(1, 16):
            peer = lax.rem(ctx + step, 16)
            has, head = head_at(peer, z_lo)

            @pl.when(has)
            def _():
                head_copy(turn, step, block.at[head], head_span(out, ctx), peer).wait_send()

    def from_heads(turn, blocks, out):
        @pl.when(is_head)
        def _():
            for step in range(1, 16):
                peer = lax.rem(ctx + step, 16)
                head_copy(turn, step, blocks.at[peer], out.at[my_head], peer).start()
            pltpu.make_async_copy(blocks.at[ctx], out.at[my_head], local_sem.at[turn]).start()

    def from_heads_received(turn, blocks, out):
        for step in range(1, 16):
            source = lax.rem(ctx + 16 - step, 16)
            has, head = head_at(source, z_lo)

            @pl.when(has)
            def _():
                head_copy(turn, step, out.at[head], out.at[head], source).wait_recv()

        @pl.when(is_head)
        def _():
            pltpu.make_async_copy(blocks.at[ctx], out.at[my_head], local_sem.at[turn]).wait()

    def from_heads_sent(turn, blocks, out):
        @pl.when(is_head)
        def _():
            for step in range(1, 16):
                peer = lax.rem(ctx + step, 16)
                head_copy(turn, step, blocks.at[peer], out.at[my_head], peer).wait_send()

    zl, zh = split_z(at["z"])
    waits = group_sends(w_joint, in_joint) + pair_sends(w_proj, in_proj)
    weights[2][zl, at["y"], zh, at["x"], core] = pad_small[...].astype(BF)
    receive(waits)
    rows = dot(place_q[...], in_joint[...].reshape(128, WIDTH)).astype(BF)
    proj_rows = dot(place_p[...], in_proj[...].reshape(64, 384)).astype(BF)
    for tile in range(3):
        span = columns_of(tile)
        weights[0][at["x"], 3 * core + tile, zl, at["y"], zh] = rows[:, span]
        weights[1][at["x"], 6 * core + 2 * tile, zl, at["y"], zh] = rows[:, 384 + 128 * tile : 512 + 128 * tile]
        weights[1][at["x"], 6 * core + 2 * tile + 1, zl, at["y"], zh] = proj_rows[:, span]

    first = Gather(mail, weights, ATTENTION + SMALL, at, core)
    second = Gather(mail, weights, FORWARD, at, core)
    first.straight(0)
    second.straight(0)
    first.straight(1)
    first.ring()
    loads[0].wait()
    xhat, _ = normalize(x[0])
    first.pass_on()
    second.straight(1)
    first.last()
    first.finish()

    loads[10].wait()
    loads[11].wait()
    small_rows = weights[2][...].reshape(2048, 128)
    found = jnp.zeros((16, WIDTH), F32)
    for group in range(8):
        wide = dot(small_rows[256 * group : 256 * group + 256], spread[...]).reshape(16, 16, WIDTH)
        found = found + jnp.sum(jnp.where(width_mask(16 * group), wide, 0.0), axis=0)
    vectors[...] = found
    tall = small_rows.astype(F32).reshape(128, 16, 128)
    eighth = lax.broadcasted_iota(jnp.int32, (128, 16, 128), 1) == 8
    fc_rows = jnp.sum(jnp.where(eighth, tall, 0.0), axis=1).astype(BF)
    hidden_bias[...] = sum_rows(jnp.where(hidden_mask(columns[...]), dot(fc_rows, spread_fc[...]), 0.0))
    normed_rows = (xhat * vectors[0:1] + vectors[2:3]).astype(BF)
    normed[...] = normed_rows

    def joint_tiles(start, count):
        tiles = [weights[0][t // 6, t % 6].reshape(WIDTH, 128) for t in range(start, start + count)]
        return jnp.concatenate(tiles, axis=1)

    for pair in range(9):
        kind, offset = pair // 3, (pair % 3) * 256
        out = dot(normed_rows, joint_tiles(2 * pair, 2))
        if kind != 1:
            out = out + vectors[3 + kind // 2 : 4 + kind // 2, offset : offset + 256]
        out = flip(out.astype(BF))
        for head in range(4):
            qkv_t[offset // 64 + head, 64 * kind : 64 * kind + 64, :] = out[64 * head : 64 * head + 64]
    to_heads(0, qkv_t, landed)
    second.ring()
    to_heads_received(0, qkv_t, landed)

    @pl.when(is_head)
    def _():
        order_heads(landed, ordered, natural)
        for step in range(4):
            attend(step, ordered, natural, out_t, log_total)

    second.pass_on()

    @pl.when(is_head)
    def _():
        for step in range(4, 2048 // TILE):
            attend(step, ordered, natural, out_t, log_total)
        for block in range(16):
            att_blocks[block] = position_block(lambda t: out_t[:, columns_of(t)], block).astype(BF)

    from_heads(1, att_blocks, att_t)
    second.last()
    second.finish()
    from_heads_received(1, att_blocks, att_t)

    rows_t = att_t[...].reshape(WIDTH, 128)
    mat_out = joint_tiles(18, 6)
    middle = x[0] + dot(flip(rows_t), mat_out) + vectors[5:6]
    xhat, factor = normalize(middle)
    normed_two = (xhat * vectors[1:2] + vectors[6:7]).astype(BF)
    normed_t = flip(normed_two)
    loads[1].wait()
    gradient = cotangent[0]
    d_two = gradient.astype(BF)
    d_norm = jnp.zeros((128, WIDTH), F32)
    twin_waits = {}
    for chunk in range(4):
        tile = lambda half, t: weights[1][chunk, 2 * t + half].reshape(WIDTH, 128)
        mat_fc = jnp.concatenate([tile(0, t) for t in range(6)], axis=1)
        mat_proj = jnp.concatenate([tile(1, t) for t in range(6)], axis=1)
        span = slice(WIDTH * chunk, WIDTH * chunk + WIDTH)
        pre = dot(normed_two, mat_fc) + hidden_bias[:, span]
        root = 0.7978845608028654
        inner = jnp.tanh(root * (pre + 0.044715 * (pre * pre * pre)))
        activated = (0.5 * pre * (1.0 + inner)).astype(BF)
        slope = 0.5 * (1.0 + inner) + 0.5 * pre * (1.0 - inner * inner) * (
            root * (1.0 + 3 * 0.044715 * (pre * pre))
        )
        update = dot(activated, mat_proj)
        final[...] = update if chunk == 0 else final[...] + update
        d_pre = (dot_right_t(d_two, mat_proj) * slope).astype(BF)
        grad_hidden[:, span] = sum_rows(d_pre.astype(F32))
        update = dot_right_t(d_pre, mat_fc)
        input_grad[...] = update if chunk == 0 else input_grad[...] + update
        grad_fc = dot(normed_t, d_pre).astype(BF)
        grad_proj = dot_left_t(activated, d_two).astype(BF)
        for t in range(6):
            grads[1][chunk, 2 * t] = grad_fc[:, columns_of(t)].reshape(2, 4, 2, 48, 128)
            grads[1][chunk, 2 * t + 1] = grad_proj[:, columns_of(t)].reshape(2, 4, 2, 48, 128)
        key = mail.send(grads[1].at[chunk, pl.ds(6 * (1 - core), 6)], sums[1].at[chunk], twin)
        twin_waits[1, chunk] = key
    final[...] = middle + final[...] + vectors[7:8]
    stores[0].start()
    d_norm = input_grad[...]
    d_mid = gradient + norm_back(d_norm, xhat, factor, vectors[1:2])
    d_middle[...] = d_mid
    d_one = d_mid.astype(BF)
    d_att_t[...] = dot_right_t(mat_out, d_one).astype(BF).reshape(HEADS, 64, 128)
    to_heads_sent(0, qkv_t, landed)
    to_heads(2, d_att_t, landed_back)
    grad_out = dot(rows_t, d_one).astype(BF)
    for t in range(6):
        grads[0][3, t] = grad_out[:, columns_of(t)].reshape(2, 4, 2, 48, 128)
    twin_waits[0, 3] = mail.send(grads[0].at[3, pl.ds(3 * (1 - core), 3)], sums[0].at[3], twin)
    grad_vectors[...] = jnp.zeros_like(grad_vectors)
    grad_vectors[1:2] = sum_rows(d_norm * xhat)
    grad_vectors[5:6] = sum_rows(d_one.astype(F32))
    grad_vectors[6:7] = sum_rows(d_norm)
    grad_vectors[7:8] = sum_rows(d_two.astype(F32))

    def add_twin(kind, chunk):
        mail.receive(twin_waits[kind, chunk], sums[kind].at[chunk])
        count = 3 * (kind + 1)
        added(sums[kind].at[chunk], grads[kind].at[chunk, pl.ds(count * core, count)])

    back_second = Reduce(mail, sums, landing, FORWARD, at, core)
    for chunk in range(4):
        add_twin(1, chunk)
    back_second.ring()
    add_twin(0, 3)

    to_heads_received(2, d_att_t, landed_back)

    @pl.when(is_head)
    def _():
        order_back(landed_back, ordered, d_out, values_natural)
        for step in range(5):
            attend_back(step, ordered, natural, values_natural, out_t, log_total, d_out, d_t, d_keys)

    back_second.pass_on()

    @pl.when(is_head)
    def _():
        for step in range(5, 2048 // TILE):
            attend_back(step, ordered, natural, values_natural, out_t, log_total, d_out, d_t, d_keys)
        for tile in range(16):
            d_t[64:192, columns_of(tile)] = d_keys[columns_of(tile), :].T.astype(BF)
        for block in range(16):
            d_blocks[block] = position_block(lambda t: d_t[:, columns_of(t)].astype(F32), block).astype(BF)

    from_heads_sent(1, att_blocks, att_t)
    from_heads(3, d_blocks, d_rows)
    back_second.collect_ring()
    back_second.straight(1)
    from_heads_received(3, d_blocks, d_rows)

    for head in range(HEADS):
        rows = flip(d_rows[head])
        for kind in range(3):
            offset = WIDTH * kind + 64 * head
            d_qkv[:, offset : offset + 64] = rows[:, 64 * kind : 64 * kind + 64]
    normed_t = flip(normed[...])
    for pair in range(9):
        out = dot(normed_t, d_qkv[:, 256 * pair : 256 * pair + 256]).astype(BF)
        for t in range(2):
            tile = 2 * pair + t
            grads[0][tile // 6, tile % 6] = out[:, columns_of(t)].reshape(2, 4, 2, 48, 128)
        if pair % 3 == 2:
            chunk = pair // 3
            source = grads[0].at[chunk, pl.ds(3 * (1 - core), 3)]
            twin_waits[0, chunk] = mail.send(source, sums[0].at[chunk], twin)
    back_second.collect(1)
    back_second.straight(2)
    d_norm = jnp.zeros((128, WIDTH), F32)
    for pair in range(9):
        d_norm = d_norm + dot_right_t(d_qkv[:, 256 * pair : 256 * pair + 256], joint_tiles(2 * pair, 2))
    back_first = Reduce(mail, sums, landing, ATTENTION, at, core)
    for chunk in range(3):
        add_twin(0, chunk)
    back_first.ring()
    xhat, factor = normalize(x[0])
    input_grad[...] = d_middle[...] + norm_back(d_norm, xhat, factor, vectors[0:1])
    stores[1].start()
    kinds = lambda kind: sum_rows(d_qkv[:, WIDTH * kind : WIDTH * kind + WIDTH].astype(F32))
    row = lax.broadcasted_iota(jnp.int32, (16, WIDTH), 0)
    found = grad_vectors[...]
    for which, value in ((0, sum_rows(d_norm * xhat)), (2, sum_rows(d_norm)), (3, kinds(0)), (4, kinds(2))):
        found = jnp.where(row == which, value, found)
    small = []
    for group in range(8):
        wide = jnp.where(width_mask(16 * group), jnp.broadcast_to(found[None], (16, 16, WIDTH)), 0.0)
        small.append(dot_right_t(wide.astype(BF).reshape(256, WIDTH), spread[...]).reshape(16, 16, 128))
    small = jnp.concatenate(small, axis=0)
    wide = jnp.where(hidden_mask(columns[...]), jnp.broadcast_to(grad_hidden[...], (128, HIDDEN)), 0.0)
    hidden = dot_right_t(wide.astype(BF), spread_fc[...])
    eighth = lax.broadcasted_iota(jnp.int32, (128, 16, 128), 1) == 8
    small = jnp.where(eighth, hidden[:, None, :], small)
    grads[2][...] = small.astype(BF).reshape(SHAPES[2])
    every = {axis: ALL for axis in AXES}
    key = mail.send(view(grads, (2, 0), every, 1 - core), sums[2], twin)

    back_second.collect(2)
    mine = [view(sums, sub, at, None) for sub in FORWARD]
    rows = jnp.concatenate([mine[t][0] for t in range(3)], axis=1)
    last_fc[...] = dot_left_t(place_q[...], rows).astype(BF).reshape(8, 16, 384)
    rows = jnp.concatenate([mine[t][1] for t in range(3)], axis=1)
    last_p[...] = dot_left_t(place_p[...], rows).astype(BF).reshape(2, 32, 384)
    waits = group_sends(last_fc, back_fc) + pair_sends(last_p, back_p)
    mail.receive(key, sums[2])
    added(sums[2], view(grads, (2, 0), every, core))
    back_small = Reduce(mail, sums, landing, SMALL, at, core)
    back_small.straight(0)

    back_first.pass_on()
    back_small.collect(0)
    back_small.straight(1)
    back_first.collect_ring()
    back_first.straight(1)
    back_small.collect(1)
    back_small.straight(2)
    receive(waits)
    for group in range(8):
        pad_fc[:, 384 * group : 384 * group + 384] = back_fc[group].astype(F32)[:8]
    reorder(pad_fc, np.argsort(hidden_order()), lambda t, value: out_fc.__setitem__((ALL, columns_of(t)), value))
    stores[3].start()
    for half in range(2):
        out_p[:, 384 * half : 384 * half + 384] = back_p[half].astype(F32)[:24]
    stores[4].start()
    back_first.collect(1)
    back_first.straight(2)
    back_small.collect(2)
    out_v[...] = view(sums, (2, 0), at, None)[...].astype(F32)
    stores[5].start()
    back_first.collect(2)
    rows = jnp.concatenate([view(sums, sub, at, None)[0] for sub in ATTENTION], axis=1)
    last_q[...] = dot_left_t(place_q[...], rows).astype(BF).reshape(8, 16, 384)
    receive(group_sends(last_q, back_q))
    for group in range(8):
        out_q[:, 384 * group : 384 * group + 384] = back_q[group].astype(F32)[:8]
    stores[2].start()

    mail.finish()
    to_heads_sent(2, d_att_t, landed_back)
    from_heads_sent(3, d_blocks, d_rows)
    for store in stores:
        store.wait()


def place_rows(groups, rows, padded):
    found = np.zeros((groups * rows, groups * padded), np.float32)
    for group in range(groups):
        for row in range(rows):
            found[group * rows + row, group * padded + row] = 1
    return found


def spread_matrix(entries, each):
    found = np.zeros((128, len(entries)), np.float32)
    found[entries % each, np.arange(len(entries))] = 1
    return found


def local(tokens, cotangent, w_qkv, w_out, w_fc, w_proj, gains, biases, fc_bias):
    order = hidden_order()
    placing = np.concatenate([place_rows(8, 6, 16), place_rows(2, 24, 32)], axis=1)
    spreads = np.concatenate([spread_matrix(np.arange(WIDTH), 6), spread_matrix(order, 24)], axis=1)
    given = (tokens, cotangent, w_qkv, w_out, w_fc, w_proj, gains, biases, fc_bias)
    given += (jnp.asarray(placing, BF), jnp.asarray(spreads, BF), jnp.asarray(order.reshape(1, HIDDEN), jnp.int32))
    results = ((128, WIDTH), (128, WIDTH), (8, HIDDEN), (8, HIDDEN), (24, WIDTH), (16, 128))
    scratch = [VMEM(item.shape, item.dtype) for item in given]
    scratch += [VMEM(shape, F32) for shape in results]
    scratch += [VMEM(shape, BF) for shape in SHAPES + SHAPES + SUMS + tuple(landing_shapes().values())]
    scratch += [
        VMEM((16, 2 * HIDDEN), F32),
        VMEM((8, HIDDEN), F32),
        VMEM((32, WIDTH), F32),
        VMEM((16, 128), F32),
        VMEM((8, 16, WIDTH), BF),
        VMEM((2, 32, 384), BF),
        pltpu.SemaphoreType.DMA((12,)),
        pltpu.SemaphoreType.DMA((6,)),
        VMEM((8, 16, WIDTH), BF),
        VMEM((2, 32, 384), BF),
        VMEM((8, 16, 384), BF),
        VMEM((8, 16, 384), BF),
        VMEM((2, 32, 384), BF),
        VMEM((8, 16, 384), BF),
        VMEM((8, 16, 384), BF),
        VMEM((2, 32, 384), BF),
        VMEM((128, WIDTH), BF),
        VMEM((16, WIDTH), F32),
        VMEM((1, HIDDEN), F32),
        VMEM((HEADS, 192, 128), BF),
        VMEM((192, 2048), BF),
        VMEM((192, 2048), BF),
        VMEM((2048, 128), BF),
        VMEM((64, 2048), F32),
        VMEM((8, 2048), F32),
        VMEM((16, 64, 128), BF),
        VMEM((HEADS, 64, 128), BF),
        VMEM((128, WIDTH), F32),
        VMEM((HEADS, 64, 128), BF),
        VMEM((64, 2048), BF),
        VMEM((64, 2048), BF),
        VMEM((2048, 128), BF),
        VMEM((192, 2048), BF),
        VMEM((2048, 128), F32),
        VMEM((16, 192, 128), BF),
        VMEM((HEADS, 192, 128), BF),
        VMEM((128, 3 * WIDTH), BF),
        VMEM((16, WIDTH), F32),
        VMEM((1, HIDDEN), F32),
        pltpu.SemaphoreType.DMA((IN_FLIGHT,)),
        pltpu.SemaphoreType.DMA((COPIES,)),
        pltpu.SemaphoreType.DMA((2, 16)),
        pltpu.SemaphoreType.DMA((2, 16)),
        pltpu.SemaphoreType.DMA((4,)),
    ]
    stay = pl.BlockSpec(memory_space=pl.ANY)
    found = pl.pallas_call(
        layer_kernel,
        out_shape=[jax.ShapeDtypeStruct(shape, F32) for shape in results],
        in_specs=[stay] * 12,
        out_specs=[stay] * 6,
        scratch_shapes=scratch,
        compiler_params=pltpu.CompilerParams(
            collective_id=0, has_side_effects=True, vmem_limit_bytes=VMEM_LIMIT * MEGA
        ),
        name="layer",
    )(*given)
    shapes = (
        (128, WIDTH), (128, WIDTH), (6, 1, 3 * WIDTH), (6, 1, WIDTH), (6, 1, HIDDEN), (24, WIDTH),
        (2, 6), (6, 1, 6), (1, 24),
    )
    parts = [shapes[i] for i in (2, 3, 4, 6, 7, 8)]
    final, input_grad, qkv, out, fc, proj, d_gains, d_biases, d_fc_bias = pl.pallas_call(
        results_kernel,
        out_shape=[jax.ShapeDtypeStruct(shape, F32) for shape in shapes],
        in_specs=[stay] * 6,
        out_specs=[stay] * 9,
        scratch_shapes=[VMEM(shape, F32) for shape in list(results) + parts]
        + [pltpu.SemaphoreType.DMA((6,)), pltpu.SemaphoreType.DMA((9,))],
        compiler_params=pltpu.CompilerParams(vmem_limit_bytes=VMEM_LIMIT * MEGA),
        name="results",
    )(*found)
    rows_first = lambda value: jnp.transpose(value, (1, 0, 2))
    return (
        final[None],
        input_grad[None],
        rows_first(qkv),
        rows_first(out),
        rows_first(fc),
        proj[None],
        d_gains[None],
        rows_first(d_biases),
        d_fc_bias,
    )


VMEM_LIMIT = 63


def solution(mesh):
    rows = P("dp", "ctx", None)
    weight = P(None, ("dp", "ctx"), None)
    vector = P(None, None, ("dp", "ctx"))
    tail = (weight,) * 4 + (vector, vector, P(None, ("dp", "ctx")))
    return jax.shard_map(
        local, mesh=mesh, in_specs=(rows, rows) + tail, out_specs=(rows, rows) + tail, check_vma=False
    )
```

```python
import jax
import jax.numpy as jnp
import numpy as np
from jax import lax
from jax.experimental import pallas as pl
from jax.experimental.pallas import tpu as pltpu
from jax.sharding import PartitionSpec as P

BF = jnp.bfloat16
F32 = jnp.float32
MESH = pl.DeviceIdType.MESH
VMEM = pltpu.VMEM
ALL = slice(None)
AXES = ("x", "y", "z")
GATHER_ORDER = (("x", "y", "z"), ("y", "z", "x"), ("z", "x", "y"))
REDUCE_ORDER = tuple(order[::-1] for order in GATHER_ORDER)
SHAPES = ((4, 6, 2, 4, 2, 48, 128), (4, 12, 2, 4, 2, 48, 128), (2, 4, 2, 4, 2, 16, 128))
SUMS = ((4, 3, 2, 4, 2, 48, 128), (4, 6, 2, 4, 2, 48, 128), (2, 4, 2, 4, 16, 128))
ATTENTION = ((0, 0), (0, 1), (0, 2))
FORWARD = ((1, 0), (1, 1), (1, 2))
SMALL = ((2, 0),)
HEADS = 12
WIDTH = 768
HIDDEN = 3072
NORM_EPS = 1e-05
MASKED = -1e30
MEGA = 1024 * 1024
COPIES = 211
IN_FLIGHT = 48


def place():
    dp = lax.axis_index("dp")
    ctx = lax.axis_index("ctx")
    at = {
        "x": lax.rem(lax.div(ctx, 2), 4),
        "y": lax.rem(dp, 4),
        "z": lax.div(ctx, 8) * 2 + lax.div(dp, 4),
    }
    return at, lax.rem(ctx, 2)


def device(at, core):
    return {
        "dp": lax.rem(at["z"], 2) * 4 + at["y"],
        "ctx": lax.div(at["z"], 2) * 8 + at["x"] * 2 + core,
    }


def head_at(ctx, z_lo):
    z_hi, x, core = lax.div(ctx, 8), lax.rem(lax.div(ctx, 2), 4), lax.rem(ctx, 2)
    head = (1 - core) * (4 * z_hi + x) + core * (8 + 2 * z_hi + x - 2 * z_lo)
    return (core == 0) | (lax.div(x, 2) == z_lo), head


def beside(at, axis, distance):
    moved = dict(at)
    moved[axis] = lax.rem(at[axis] + (distance + 4), 4)
    return moved


def split_z(z):
    if isinstance(z, tuple):
        return pl.ds(z[1], 1), ALL
    if isinstance(z, slice):
        return ALL, ALL
    return lax.rem(z, 2), lax.div(z, 2)


def line(value):
    return pl.ds(2 * value[1], 2) if isinstance(value, tuple) else value


def view(refs, sub, sel, core):
    kind, tile = sub
    x, y = line(sel["x"]), line(sel["y"])
    zl, zh = split_z(sel["z"])
    if kind == 2:
        return refs[2].at[zl, y, zh, x] if core is None else refs[2].at[zl, y, zh, x, core]
    count = kind + 1
    start = count * tile + (0 if core is None else 3 * count * core)
    return refs[kind].at[x, pl.ds(start, count), zl, y, zh]


def block_shape(sub, gone, half_axis=None):
    extent = {axis: 1 if axis in gone else 4 for axis in AXES}
    if half_axis is not None:
        extent[half_axis] = 2
    lead = lambda name: () if extent[name] == 1 else (extent[name],)
    zl, zh = ((), ()) if extent["z"] == 1 else ((extent["z"] // 2,), (2,))
    if sub[0] == 2:
        return zl + lead("y") + zh + lead("x") + (16, 128)
    return lead("x") + (sub[0] + 1,) + zl + lead("y") + zh + (48, 128)


def landing_shapes():
    found = {}
    for sub in ATTENTION + FORWARD + SMALL:
        order = REDUCE_ORDER[sub[1]]
        for phase in range(3):
            gone = order[: phase + 1]
            if phase == 0 and sub[0] < 2:
                for half in range(2):
                    for use in range(3):
                        found[sub, phase, half, use] = block_shape(sub, gone, order[2])
            else:
                for use in range(3):
                    found[sub, phase, use] = block_shape(sub, gone)
    return found


def added(target, *terms):
    if len(target.shape) == 2:
        total = target[...].astype(F32)
        for term in terms:
            total = total + term[...].astype(F32)
        target[...] = total.astype(BF)
        return

    def step(i, carry):
        if len(terms) == 1:
            target[i] = target[i] + terms[0][i]
            return carry
        total = target[i].astype(F32)
        for term in terms:
            total = total + term[i].astype(F32)
        target[i] = total.astype(BF)
        return carry

    lax.fori_loop(0, target.shape[0], step, 0)


class Mail:
    def __init__(self, send_sem, recv_sem, anyone):
        self.send_sem, self.recv_sem, self.anyone = send_sem, recv_sem, anyone
        self.used, self.sent = 0, []

    def send(self, source, target, device_id):
        key = self.used
        if key >= IN_FLIGHT:
            self.sent[key - IN_FLIGHT].wait_send()
        copy = pltpu.make_async_remote_copy(
            src_ref=source,
            dst_ref=target,
            send_sem=self.send_sem.at[key % IN_FLIGHT],
            recv_sem=self.recv_sem.at[key],
            device_id=device_id,
            device_id_type=MESH,
        )
        copy.start()
        self.sent.append(copy)
        self.used += 1
        return key

    def receive(self, key, arrival):
        pltpu.make_async_remote_copy(
            src_ref=arrival,
            dst_ref=arrival,
            send_sem=self.send_sem.at[key % IN_FLIGHT],
            recv_sem=self.recv_sem.at[key],
            device_id=self.anyone,
            device_id_type=MESH,
        ).wait_recv()

    def finish(self):
        for copy in self.sent[-IN_FLIGHT:]:
            copy.wait_send()
        assert self.used == COPIES, self.used


class Gather:
    def __init__(self, mail, refs, subs, at, core):
        self.mail, self.refs, self.subs, self.at, self.core = mail, refs, subs, at, core
        self.twin = device(at, 1 - core)
        self.pending, self.twins = [], []

    def sel(self, sub, phase):
        found = dict(self.at)
        for done in GATHER_ORDER[sub[1]][:phase]:
            found[done] = ALL
        return found

    def mine(self, sub, sel):
        return view(self.refs, sub, sel, self.core)

    def peer(self, axis, distance):
        return device(beside(self.at, axis, distance), self.core)

    def to_twin(self, sub, sel):
        source = self.mine(sub, sel)
        self.twins.append((self.mail.send(source, source, self.twin), view(self.refs, sub, sel, 1 - self.core)))

    def collect(self):
        for wait in self.pending:
            self.mail.receive(*wait)
        self.pending = []

    def straight(self, phase):
        self.collect()
        for sub in self.subs:
            axis, sel = GATHER_ORDER[sub[1]][phase], self.sel(sub, phase)
            source = self.mine(sub, sel)
            for distance in (1, -1, 2):
                key = self.mail.send(source, source, self.peer(axis, distance))
                self.pending.append((key, self.mine(sub, beside(sel, axis, -distance))))

    def ring(self):
        self.collect()
        self.keys = []
        for sub in self.subs:
            axis, sel = GATHER_ORDER[sub[1]][2], self.sel(sub, 2)
            source = self.mine(sub, sel)
            self.keys.append([self.mail.send(source, source, self.peer(axis, d)) for d in (1, -1)])
        for sub in self.subs:
            self.to_twin(sub, self.sel(sub, 2))

    def pass_on(self):
        for sub, keys in zip(self.subs, self.keys):
            order = GATHER_ORDER[sub[1]]
            axis, sel = order[2], self.sel(sub, 2)
            for half, distance in ((0, 1), (1, -1)):
                arrived, far = beside(sel, axis, -distance), beside(sel, axis, 2)
                self.mail.receive(keys[half], self.mine(sub, arrived))
                moving = self.mine(sub, {**arrived, order[0]: ("half", half)})
                coming = self.mine(sub, {**far, order[0]: ("half", half)})
                self.pending.append((self.mail.send(moving, moving, self.peer(axis, distance)), coming))
        for sub in self.subs:
            for distance in (1, -1):
                self.to_twin(sub, beside(self.sel(sub, 2), GATHER_ORDER[sub[1]][2], distance))

    def last(self):
        self.collect()
        for sub in self.subs:
            self.to_twin(sub, beside(self.sel(sub, 2), GATHER_ORDER[sub[1]][2], 2))

    def finish(self):
        for wait in self.twins:
            self.mail.receive(*wait)


class Reduce:
    def __init__(self, mail, sums, landing, subs, at, core):
        self.mail, self.sums, self.landing, self.subs, self.at, self.core = mail, sums, landing, subs, at, core
        self.kept = {}

    def sel(self, sub, phase):
        found = dict(self.at)
        for later in REDUCE_ORDER[sub[1]][phase + 1 :]:
            found[later] = ALL
        return found

    def mine(self, sub, sel, half=None):
        if half is not None:
            sel = {**sel, REDUCE_ORDER[sub[1]][2]: ("half", half)}
        return view(self.sums, sub, sel, None)

    def peer(self, axis, distance):
        return device(beside(self.at, axis, distance), self.core)

    def ring(self):
        for sub in self.subs:
            axis, sel, land = REDUCE_ORDER[sub[1]][0], self.sel(sub, 0), self.landing
            plus, minus = self.peer(axis, 1), self.peer(axis, -1)
            far, up, down = beside(sel, axis, 2), beside(sel, axis, 1), beside(sel, axis, -1)
            self.kept[sub] = [
                self.mail.send(self.mine(sub, far, 0), land[sub, 0, 0, 0], plus),
                self.mail.send(self.mine(sub, far, 1), land[sub, 0, 1, 0], minus),
                self.mail.send(self.mine(sub, up, 1), land[sub, 0, 1, 1], plus),
                self.mail.send(self.mine(sub, down, 0), land[sub, 0, 0, 2], minus),
            ]

    def pass_on(self):
        for sub in self.subs:
            axis, sel, land = REDUCE_ORDER[sub[1]][0], self.sel(sub, 0), self.landing
            keys = self.kept[sub]
            for half, distance in ((0, 1), (1, -1)):
                self.mail.receive(keys[half], land[sub, 0, half, 0])
                moving = self.mine(sub, beside(sel, axis, distance), half)
                added(moving, land[sub, 0, half, 0])
                keys.append(self.mail.send(moving, land[sub, 0, half, 1 + half], self.peer(axis, distance)))

    def collect_ring(self):
        for sub in self.subs:
            sel, land, keys = self.sel(sub, 0), self.landing, self.kept[sub]
            for half, first, second in ((1, keys[2], keys[5]), (0, keys[4], keys[3])):
                self.mail.receive(first, land[sub, 0, half, 1])
                self.mail.receive(second, land[sub, 0, half, 2])
                added(self.mine(sub, sel, half), land[sub, 0, half, 1], land[sub, 0, half, 2])

    def straight(self, phase):
        for sub in self.subs:
            axis, sel = REDUCE_ORDER[sub[1]][phase], self.sel(sub, phase)
            self.kept[sub] = [
                self.mail.send(
                    self.mine(sub, beside(sel, axis, distance)),
                    self.landing[sub, phase, use],
                    self.peer(axis, distance),
                )
                for use, distance in enumerate((1, -1, 2))
            ]

    def collect(self, phase):
        for sub in self.subs:
            terms = [self.landing[sub, phase, use] for use in range(3)]
            for key, term in zip(self.kept[sub], terms):
                self.mail.receive(key, term)
            added(self.mine(sub, self.sel(sub, phase)), *terms)


def dot(left, right):
    return jnp.dot(left, right, preferred_element_type=F32)


def dot_right_t(left, right):
    return lax.dot_general(left, right, (((1,), (1,)), ((), ())), preferred_element_type=F32)


def dot_left_t(left, right):
    return lax.dot_general(left, right, (((0,), (0,)), ((), ())), preferred_element_type=F32)


def flip(values):
    return values.astype(F32).T.astype(BF)


def mean_last(values):
    return jnp.mean(values, axis=-1, keepdims=True)


def sum_rows(values):
    return jnp.sum(values, axis=0, keepdims=True)


def normalize(values):
    center = values - mean_last(values)
    factor = lax.rsqrt(mean_last(center * center) + NORM_EPS)
    return center * factor, factor


def norm_back(d_norm, xhat, factor, gain):
    e = d_norm * gain
    return factor * (e - mean_last(e) - xhat * mean_last(e * xhat))


def owner_mask(shape, column, each):
    owner = lax.broadcasted_iota(jnp.int32, shape, 0) * each
    return (column >= owner) & (column < owner + each)


def width_mask(first):
    shape = (16, 16, WIDTH)
    return owner_mask(shape, lax.broadcasted_iota(jnp.int32, shape, 2) - 6 * first, 6)


def hidden_mask(columns):
    shape = (128, HIDDEN)
    return owner_mask(shape, jnp.broadcast_to(columns, shape), 24)


def low_half(shape):
    return lax.broadcasted_iota(jnp.int32, shape, 1) < 64


def swap_halves(tile):
    return pltpu.roll(tile, 64, 1)


def position_tile(block, tile):
    if tile < 8:
        low, high = block(2 * tile), swap_halves(block(2 * tile + 1))
    else:
        low, high = swap_halves(block(31 - 2 * tile)), block(30 - 2 * tile)
    return jnp.where(low_half(low.shape), low, high)


def position_block(tile, block):
    early, late = tile(block // 2), tile((31 - block) // 2)
    if block % 2 == 0:
        return jnp.where(low_half(early.shape), early, late)
    return swap_halves(jnp.where(low_half(early.shape), late, early))


TILE = 256
KEYS = 1024


def columns_of(tile):
    return slice(128 * tile, 128 * tile + 128)


def causal(scores):
    key = lax.broadcasted_iota(jnp.int32, scores.shape, 0)
    query = lax.broadcasted_iota(jnp.int32, scores.shape, 1)
    return jnp.where(key <= query, scores, MASKED)


def query_columns(ordered, first):
    queries = ordered[0:64, first : first + TILE]
    return jnp.concatenate([jnp.zeros_like(queries), queries], axis=0)


def order_heads(landed, ordered, natural):
    for tile in range(16):
        found = position_tile(lambda b: landed[:, columns_of(b)].astype(F32), tile)
        found = jnp.concatenate([found[0:64] * 0.125, found[64:192]], axis=0)
        ordered[:, columns_of(tile)] = found.astype(BF)
        natural[columns_of(tile), :] = found[0:128].T.astype(BF)


def attend(step, ordered, natural, out_t, log_total):
    first = TILE * step
    count = first + TILE
    queries = query_columns(ordered, first)
    spans = [slice(first, count)] + ([slice(0, first)] if first else [])
    scores = [dot(natural[span, :], queries) for span in spans]
    scores[0] = causal(scores[0])
    best = jnp.max(scores[0], axis=0, keepdims=True)
    for part in scores[1:]:
        best = jnp.maximum(best, jnp.max(part, axis=0, keepdims=True))
    total = jnp.zeros((1, TILE), F32)
    out = jnp.zeros((64, TILE), F32)
    for span, part in zip(spans, scores):
        probs = jnp.exp(part - best)
        total = total + sum_rows(probs)
        out = out + dot(ordered[128:192, span], probs.astype(BF))
    out_t[:, first:count] = out / total
    log_total[0:1, first:count] = best + jnp.log(total)


def order_back(landed, ordered, d_out, values_natural):
    for tile in range(16):
        found = position_tile(lambda b: landed[:, columns_of(b)].astype(F32), tile)
        d_out[:, columns_of(tile)] = found.astype(BF)
        both = jnp.concatenate([ordered[128:192, columns_of(tile)].astype(F32), found], axis=0)
        values_natural[columns_of(tile), :] = both.T.astype(BF)


def attend_back(step, ordered, natural, values_natural, out_t, log_total, d_out, d_t, d_keys):
    first = TILE * step
    count = first + TILE
    queries = query_columns(ordered, first)
    log_here = log_total[0:1, first:count]
    d_low = d_out[:, first:count]
    delta = sum_rows(d_low.astype(F32) * out_t[:, first:count])
    d_low = jnp.concatenate([d_low, jnp.zeros_like(d_low)], axis=0)
    query_rows, d_rows = natural[first:count, :], values_natural[first:count, :]
    low = low_half(query_rows.shape)
    query_rows = jnp.where(low, query_rows, jnp.zeros_like(query_rows))
    d_rows = jnp.where(low, jnp.zeros_like(d_rows), d_rows)
    d_query = jnp.zeros((64, TILE), F32)
    for begin in [*range(0, first, KEYS), first]:
        end = count if begin == first else min(begin + KEYS, first)
        scores = dot(natural[begin:end, :], queries)
        if begin == first:
            scores = causal(scores)
        probs = jnp.exp(scores - log_here)
        d_scores = (probs * (dot(values_natural[begin:end, :], d_low) - delta)).astype(BF)
        d_query = d_query + dot(ordered[64:128, begin:end], d_scores)
        update = dot(d_scores, query_rows) + dot(probs.astype(BF), d_rows)
        if begin == first:
            d_keys[begin:end, :] = update
        else:
            d_keys[begin:end, :] += update
    d_t[0:64, first:count] = (d_query * 0.125).astype(BF)


def hidden_order():
    x, group, row = np.meshgrid(np.arange(4), np.arange(16), np.arange(48), indexing="ij")
    return (192 * group + 48 * x + row).reshape(-1)


def reorder(source, order, store):
    for tile in range(len(order) // 128):
        wanted = order[columns_of(tile)]
        lanes = lax.broadcasted_iota(jnp.int32, (8, 128), 1)
        found = jnp.zeros((8, 128), F32)
        begin = 0
        while begin < 128:
            end = begin + 1
            while end < 128 and wanted[end] == wanted[end - 1] + 1 and wanted[end] % 128:
                end += 1
            at = int(wanted[begin])
            piece = source[0:8, columns_of(at // 128)]
            shift = (begin - at) % 128
            if shift:
                piece = pltpu.roll(piece, shift, 1)
            found = jnp.where((lanes >= begin) & (lanes < end), piece, found)
            begin = end
        store(tile, found)


def results_kernel(
    final, input_grad, joint, hidden, proj, small,
    to_final, to_input, to_qkv, to_out, to_fc, to_proj, to_gains, to_biases, to_fc_bias,
    final_here, input_here, joint_here, hidden_here, proj_here, small_here,
    qkv, out, fc, gains, biases, fc_bias, in_sem, out_sem,
):
    pairs = (
        (joint, joint_here), (hidden, hidden_here), (small, small_here),
        (final, final_here), (input_grad, input_here), (proj, proj_here),
    )
    loads = [pltpu.make_async_copy(source, target, in_sem.at[i]) for i, (source, target) in enumerate(pairs)]
    pairs = (
        (final_here, to_final), (input_here, to_input), (proj_here, to_proj),
        (qkv, to_qkv), (out, to_out), (fc, to_fc), (gains, to_gains), (biases, to_biases), (fc_bias, to_fc_bias),
    )
    stores = [pltpu.make_async_copy(source, target, out_sem.at[i]) for i, (source, target) in enumerate(pairs)]
    for copy in loads:
        copy.start()
    for copy in loads[:3]:
        copy.wait()
    for row in range(6):
        qkv[row] = joint_here[row : row + 1, 0 : 3 * WIDTH]
        out[row] = joint_here[row : row + 1, 3 * WIDTH : HIDDEN]
        fc[row] = hidden_here[row : row + 1, :]
        biases[row] = small_here[2 + row : 3 + row, 0:6]
    gains[...] = small_here[0:2, 0:6]
    fc_bias[...] = small_here[8:9, 0:24]
    for copy in stores[3:]:
        copy.start()
    for load, store in zip(loads[3:], stores[:3]):
        load.wait()
        store.start()
    for copy in stores:
        copy.wait()


def layer_kernel(*refs):
    shapes = landing_shapes()
    ins, outs, refs = refs[:12], refs[12:18], refs[18:]
    loaded, refs = refs[:12], refs[12:]
    x, cotangent, raw_qkv, raw_out, raw_fc, raw_proj, raw_gains, raw_biases, raw_fc_bias, placing, spreads, columns = loaded
    final, input_grad, out_q, out_fc, out_p, out_v = refs[:6]
    weights, grads, sums = refs[6:9], refs[9:12], refs[12:15]
    refs = refs[15:]
    landing = dict(zip(shapes, refs[: len(shapes)]))
    (
        pad_joint, pad_fc, pad_proj, pad_small, w_joint, w_proj, in_sem, out_sem,
        in_joint, in_proj, last_q, last_fc, last_p, back_q, back_fc, back_p,
        normed, vectors, hidden_bias, qkv_t, landed, ordered, natural, out_t, log_total, att_blocks, att_t,
        d_middle, d_att_t, landed_back, d_out, values_natural, d_t, d_keys, d_blocks,
        d_rows, d_qkv, grad_vectors, grad_hidden,
        send_sem, recv_sem, head_send, head_recv, local_sem,
    ) = refs[len(shapes) :]
    loads = [pltpu.make_async_copy(ins[i], loaded[i], in_sem.at[i]) for i in range(12)]
    for i in (2, 3, 4, 5, 6, 7, 8, 9, 0, 10, 11, 1):
        loads[i].start()
    stores = [
        pltpu.make_async_copy(source, outs[i], out_sem.at[i])
        for i, source in enumerate((final, input_grad, out_q, out_fc, out_p, out_v))
    ]
    place_q, place_p = placing.at[:, 0:128], placing.at[:, 128:192]
    spread, spread_fc = spreads.at[:, 0:WIDTH], spreads.at[:, WIDTH:]
    at, core = place()
    ctx = lax.axis_index("ctx")
    spot = at["x"] * 2 + core
    is_head, my_head = head_at(ctx, lax.rem(at["z"], 2))
    twin = device(at, 1 - core)
    mail = Mail(send_sem, recv_sem, twin)

    known = [{"ctx": lax.rem(ctx + step, 16)} for step in range(1, 16)]
    known += [device(beside(at, "y", distance), core) for distance in (1, -1, 2)]
    known += [device(beside(at, "z", distance), core) for distance in (1, -1)]
    barrier = pltpu.get_barrier_semaphore()
    for target in known:
        pl.semaphore_signal(barrier, inc=1, device_id=target, device_id_type=MESH)

    pad_joint[...] = jnp.zeros_like(pad_joint)
    pad_fc[...] = jnp.zeros_like(pad_fc)
    pad_proj[...] = jnp.zeros_like(pad_proj)
    pad_small[...] = jnp.zeros_like(pad_small)
    for i in range(2, 10):
        loads[i].wait()
    pad_joint[0:6, 0 : 3 * WIDTH] = raw_qkv[0].astype(F32)
    pad_joint[0:6, 3 * WIDTH : HIDDEN] = raw_out[0].astype(F32)
    pad_fc[0:6, :] = raw_fc[0].astype(F32)
    reorder(pad_fc, hidden_order(), lambda t, value: pad_joint.__setitem__(
        (slice(0, 8), slice(HIDDEN + 128 * t, HIDDEN + 128 * t + 128)), value))
    for group in range(8):
        for half in range(2):
            first = HIDDEN * half + 384 * group
            w_joint[group, :, 384 * half : 384 * half + 384] = pad_joint[:, first : first + 384].astype(BF)
    pad_proj[0:24, :] = raw_proj[0].astype(F32)
    for half in range(2):
        w_proj[half] = pad_proj[:, 384 * half : 384 * half + 384].astype(BF)
    pad_small[0:2, 0:6] = raw_gains[0].astype(F32)
    pad_small[2:8, 0:6] = raw_biases[0].astype(F32)
    pad_small[8:9, 0:24] = raw_fc_bias[...].astype(F32)
    pl.semaphore_wait(barrier, len(known))

    def group_sends(source, target):
        waits = []
        for step in range(1, 8):
            other = lax.rem(spot + step, 8)
            origin = lax.rem(spot + 8 - step, 8)
            peer = device({**at, "x": lax.div(other, 2)}, lax.rem(other, 2))
            waits.append((mail.send(source.at[other], target.at[spot], peer), target.at[origin]))
        target[spot] = source[spot]
        return waits

    def pair_sends(source, target):
        key = mail.send(source.at[1 - core], target.at[core], twin)
        target[core] = source[core]
        return [(key, target.at[1 - core])]

    def receive(waits):
        for wait in waits:
            mail.receive(*wait)

    def head_span(ref, who):
        return ref.at[:, pl.ds(pl.multiple_of(who * 128, 128), 128)]

    def head_copy(turn, step, source, target, peer):
        return pltpu.make_async_remote_copy(
            source, target, head_send.at[turn % 2, step], head_recv.at[turn % 2, step],
            device_id={"ctx": peer}, device_id_type=MESH,
        )

    z_lo = lax.rem(at["z"], 2)

    def to_heads(turn, block, out):
        for step in range(1, 16):
            peer = lax.rem(ctx + step, 16)
            has, head = head_at(peer, z_lo)

            @pl.when(has)
            def _():
                head_copy(turn, step, block.at[head], head_span(out, ctx), peer).start()

        @pl.when(is_head)
        def _():
            pltpu.make_async_copy(block.at[my_head], head_span(out, ctx), local_sem.at[turn]).start()

    def to_heads_received(turn, block, out):
        @pl.when(is_head)
        def _():
            for step in range(1, 16):
                source = lax.rem(ctx + 16 - step, 16)
                head_copy(turn, step, head_span(out, source), head_span(out, source), source).wait_recv()
            pltpu.make_async_copy(block.at[my_head], head_span(out, ctx), local_sem.at[turn]).wait()

    def to_heads_sent(turn, block, out):
        for step in range(1, 16):
            peer = lax.rem(ctx + step, 16)
            has, head = head_at(peer, z_lo)

            @pl.when(has)
            def _():
                head_copy(turn, step, block.at[head], head_span(out, ctx), peer).wait_send()

    def from_heads(turn, blocks, out):
        @pl.when(is_head)
        def _():
            for step in range(1, 16):
                peer = lax.rem(ctx + step, 16)
                head_copy(turn, step, blocks.at[peer], out.at[my_head], peer).start()
            pltpu.make_async_copy(blocks.at[ctx], out.at[my_head], local_sem.at[turn]).start()

    def from_heads_received(turn, blocks, out):
        for step in range(1, 16):
            source = lax.rem(ctx + 16 - step, 16)
            has, head = head_at(source, z_lo)

            @pl.when(has)
            def _():
                head_copy(turn, step, out.at[head], out.at[head], source).wait_recv()

        @pl.when(is_head)
        def _():
            pltpu.make_async_copy(blocks.at[ctx], out.at[my_head], local_sem.at[turn]).wait()

    def from_heads_sent(turn, blocks, out):
        @pl.when(is_head)
        def _():
            for step in range(1, 16):
                peer = lax.rem(ctx + step, 16)
                head_copy(turn, step, blocks.at[peer], out.at[my_head], peer).wait_send()

    zl, zh = split_z(at["z"])
    waits = group_sends(w_joint, in_joint) + pair_sends(w_proj, in_proj)
    weights[2][zl, at["y"], zh, at["x"], core] = pad_small[...].astype(BF)
    receive(waits)
    rows = dot(place_q[...], in_joint[...].reshape(128, WIDTH)).astype(BF)
    proj_rows = dot(place_p[...], in_proj[...].reshape(64, 384)).astype(BF)
    for tile in range(3):
        span = columns_of(tile)
        weights[0][at["x"], 3 * core + tile, zl, at["y"], zh] = rows[:, span]
        weights[1][at["x"], 6 * core + 2 * tile, zl, at["y"], zh] = rows[:, 384 + 128 * tile : 512 + 128 * tile]
        weights[1][at["x"], 6 * core + 2 * tile + 1, zl, at["y"], zh] = proj_rows[:, span]

    first = Gather(mail, weights, ATTENTION + SMALL, at, core)
    second = Gather(mail, weights, FORWARD, at, core)
    first.straight(0)
    second.straight(0)
    first.straight(1)
    first.ring()
    loads[0].wait()
    xhat, _ = normalize(x[0])
    first.pass_on()
    second.straight(1)
    first.last()
    first.finish()

    loads[10].wait()
    loads[11].wait()
    small_rows = weights[2][...].reshape(2048, 128)
    found = jnp.zeros((16, WIDTH), F32)
    for group in range(8):
        wide = dot(small_rows[256 * group : 256 * group + 256], spread[...]).reshape(16, 16, WIDTH)
        found = found + jnp.sum(jnp.where(width_mask(16 * group), wide, 0.0), axis=0)
    vectors[...] = found
    tall = small_rows.astype(F32).reshape(128, 16, 128)
    eighth = lax.broadcasted_iota(jnp.int32, (128, 16, 128), 1) == 8
    fc_rows = jnp.sum(jnp.where(eighth, tall, 0.0), axis=1).astype(BF)
    hidden_bias[...] = sum_rows(jnp.where(hidden_mask(columns[...]), dot(fc_rows, spread_fc[...]), 0.0))
    normed_rows = (xhat * vectors[0:1] + vectors[2:3]).astype(BF)
    normed[...] = normed_rows

    def joint_tiles(start, count):
        tiles = [weights[0][t // 6, t % 6].reshape(WIDTH, 128) for t in range(start, start + count)]
        return jnp.concatenate(tiles, axis=1)

    for pair in range(9):
        kind, offset = pair // 3, (pair % 3) * 256
        out = dot(normed_rows, joint_tiles(2 * pair, 2))
        if kind != 1:
            out = out + vectors[3 + kind // 2 : 4 + kind // 2, offset : offset + 256]
        out = flip(out.astype(BF))
        for head in range(4):
            qkv_t[offset // 64 + head, 64 * kind : 64 * kind + 64, :] = out[64 * head : 64 * head + 64]
    to_heads(0, qkv_t, landed)
    second.ring()
    to_heads_received(0, qkv_t, landed)

    @pl.when(is_head)
    def _():
        order_heads(landed, ordered, natural)
        for step in range(4):
            attend(step, ordered, natural, out_t, log_total)

    second.pass_on()

    @pl.when(is_head)
    def _():
        for step in range(4, 2048 // TILE):
            attend(step, ordered, natural, out_t, log_total)
        for block in range(16):
            att_blocks[block] = position_block(lambda t: out_t[:, columns_of(t)], block).astype(BF)

    from_heads(1, att_blocks, att_t)
    second.last()
    second.finish()
    from_heads_received(1, att_blocks, att_t)

    rows_t = att_t[...].reshape(WIDTH, 128)
    mat_out = joint_tiles(18, 6)
    middle = x[0] + dot(flip(rows_t), mat_out) + vectors[5:6]
    xhat, factor = normalize(middle)
    normed_two = (xhat * vectors[1:2] + vectors[6:7]).astype(BF)
    normed_t = flip(normed_two)
    loads[1].wait()
    gradient = cotangent[0]
    d_two = gradient.astype(BF)
    d_norm = jnp.zeros((128, WIDTH), F32)
    twin_waits = {}
    for chunk in range(4):
        tile = lambda half, t: weights[1][chunk, 2 * t + half].reshape(WIDTH, 128)
        mat_fc = jnp.concatenate([tile(0, t) for t in range(6)], axis=1)
        mat_proj = jnp.concatenate([tile(1, t) for t in range(6)], axis=1)
        span = slice(WIDTH * chunk, WIDTH * chunk + WIDTH)
        pre = dot(normed_two, mat_fc) + hidden_bias[:, span]
        root = 0.7978845608028654
        inner = jnp.tanh(root * (pre + 0.044715 * (pre * pre * pre)))
        activated = (0.5 * pre * (1.0 + inner)).astype(BF)
        slope = 0.5 * (1.0 + inner) + 0.5 * pre * (1.0 - inner * inner) * (
            root * (1.0 + 3 * 0.044715 * (pre * pre))
        )
        update = dot(activated, mat_proj)
        final[...] = update if chunk == 0 else final[...] + update
        d_pre = (dot_right_t(d_two, mat_proj) * slope).astype(BF)
        grad_hidden[:, span] = sum_rows(d_pre.astype(F32))
        update = dot_right_t(d_pre, mat_fc)
        input_grad[...] = update if chunk == 0 else input_grad[...] + update
        grad_fc = dot(normed_t, d_pre).astype(BF)
        grad_proj = dot_left_t(activated, d_two).astype(BF)
        for t in range(6):
            grads[1][chunk, 2 * t] = grad_fc[:, columns_of(t)].reshape(2, 4, 2, 48, 128)
            grads[1][chunk, 2 * t + 1] = grad_proj[:, columns_of(t)].reshape(2, 4, 2, 48, 128)
        key = mail.send(grads[1].at[chunk, pl.ds(6 * (1 - core), 6)], sums[1].at[chunk], twin)
        twin_waits[1, chunk] = key
    final[...] = middle + final[...] + vectors[7:8]
    stores[0].start()
    d_norm = input_grad[...]
    d_mid = gradient + norm_back(d_norm, xhat, factor, vectors[1:2])
    d_middle[...] = d_mid
    d_one = d_mid.astype(BF)
    d_att_t[...] = dot_right_t(mat_out, d_one).astype(BF).reshape(HEADS, 64, 128)
    to_heads_sent(0, qkv_t, landed)
    to_heads(2, d_att_t, landed_back)
    def add_twin(kind, chunk):
        mail.receive(twin_waits[kind, chunk], sums[kind].at[chunk])
        count = 3 * (kind + 1)
        added(sums[kind].at[chunk], grads[kind].at[chunk, pl.ds(count * core, count)])

    back_second = Reduce(mail, sums, landing, FORWARD, at, core)
    for chunk in range(4):
        add_twin(1, chunk)
    back_second.ring()
    grad_out = dot(rows_t, d_one).astype(BF)
    for t in range(6):
        grads[0][3, t] = grad_out[:, columns_of(t)].reshape(2, 4, 2, 48, 128)
    twin_waits[0, 3] = mail.send(grads[0].at[3, pl.ds(3 * (1 - core), 3)], sums[0].at[3], twin)
    grad_vectors[...] = jnp.zeros_like(grad_vectors)
    grad_vectors[1:2] = sum_rows(d_norm * xhat)
    grad_vectors[5:6] = sum_rows(d_one.astype(F32))
    grad_vectors[6:7] = sum_rows(d_norm)
    grad_vectors[7:8] = sum_rows(d_two.astype(F32))

    add_twin(0, 3)

    to_heads_received(2, d_att_t, landed_back)

    @pl.when(is_head)
    def _():
        order_back(landed_back, ordered, d_out, values_natural)
        for step in range(5):
            attend_back(step, ordered, natural, values_natural, out_t, log_total, d_out, d_t, d_keys)

    back_second.pass_on()

    @pl.when(is_head)
    def _():
        for step in range(5, 2048 // TILE):
            attend_back(step, ordered, natural, values_natural, out_t, log_total, d_out, d_t, d_keys)
        for tile in range(16):
            d_t[64:192, columns_of(tile)] = d_keys[columns_of(tile), :].T.astype(BF)
        for block in range(16):
            d_blocks[block] = position_block(lambda t: d_t[:, columns_of(t)].astype(F32), block).astype(BF)

    from_heads_sent(1, att_blocks, att_t)
    from_heads(3, d_blocks, d_rows)
    back_second.collect_ring()
    back_second.straight(1)
    from_heads_received(3, d_blocks, d_rows)

    for head in range(HEADS):
        rows = flip(d_rows[head])
        for kind in range(3):
            offset = WIDTH * kind + 64 * head
            d_qkv[:, offset : offset + 64] = rows[:, 64 * kind : 64 * kind + 64]
    normed_t = flip(normed[...])
    for pair in range(9):
        out = dot(normed_t, d_qkv[:, 256 * pair : 256 * pair + 256]).astype(BF)
        for t in range(2):
            tile = 2 * pair + t
            grads[0][tile // 6, tile % 6] = out[:, columns_of(t)].reshape(2, 4, 2, 48, 128)
        if pair % 3 == 2:
            chunk = pair // 3
            source = grads[0].at[chunk, pl.ds(3 * (1 - core), 3)]
            twin_waits[0, chunk] = mail.send(source, sums[0].at[chunk], twin)
    back_second.collect(1)
    back_second.straight(2)
    d_norm = jnp.zeros((128, WIDTH), F32)
    for pair in range(9):
        d_norm = d_norm + dot_right_t(d_qkv[:, 256 * pair : 256 * pair + 256], joint_tiles(2 * pair, 2))
    back_first = Reduce(mail, sums, landing, ATTENTION, at, core)
    for chunk in range(3):
        add_twin(0, chunk)
    back_first.ring()
    xhat, factor = normalize(x[0])
    input_grad[...] = d_middle[...] + norm_back(d_norm, xhat, factor, vectors[0:1])
    stores[1].start()
    kinds = lambda kind: sum_rows(d_qkv[:, WIDTH * kind : WIDTH * kind + WIDTH].astype(F32))
    row = lax.broadcasted_iota(jnp.int32, (16, WIDTH), 0)
    found = grad_vectors[...]
    for which, value in ((0, sum_rows(d_norm * xhat)), (2, sum_rows(d_norm)), (3, kinds(0)), (4, kinds(2))):
        found = jnp.where(row == which, value, found)
    small = []
    for group in range(8):
        wide = jnp.where(width_mask(16 * group), jnp.broadcast_to(found[None], (16, 16, WIDTH)), 0.0)
        small.append(dot_right_t(wide.astype(BF).reshape(256, WIDTH), spread[...]).reshape(16, 16, 128))
    small = jnp.concatenate(small, axis=0)
    wide = jnp.where(hidden_mask(columns[...]), jnp.broadcast_to(grad_hidden[...], (128, HIDDEN)), 0.0)
    hidden = dot_right_t(wide.astype(BF), spread_fc[...])
    eighth = lax.broadcasted_iota(jnp.int32, (128, 16, 128), 1) == 8
    small = jnp.where(eighth, hidden[:, None, :], small)
    grads[2][...] = small.astype(BF).reshape(SHAPES[2])
    every = {axis: ALL for axis in AXES}
    key = mail.send(view(grads, (2, 0), every, 1 - core), sums[2], twin)

    back_second.collect(2)
    mine = [view(sums, sub, at, None) for sub in FORWARD]
    rows = jnp.concatenate([mine[t][0] for t in range(3)], axis=1)
    last_fc[...] = dot_left_t(place_q[...], rows).astype(BF).reshape(8, 16, 384)
    rows = jnp.concatenate([mine[t][1] for t in range(3)], axis=1)
    last_p[...] = dot_left_t(place_p[...], rows).astype(BF).reshape(2, 32, 384)
    waits = group_sends(last_fc, back_fc) + pair_sends(last_p, back_p)
    mail.receive(key, sums[2])
    added(sums[2], view(grads, (2, 0), every, core))
    back_small = Reduce(mail, sums, landing, SMALL, at, core)
    back_small.straight(0)

    back_first.pass_on()
    back_small.collect(0)
    back_small.straight(1)
    back_first.collect_ring()
    back_first.straight(1)
    back_small.collect(1)
    back_small.straight(2)
    receive(waits)
    for group in range(8):
        pad_fc[:, 384 * group : 384 * group + 384] = back_fc[group].astype(F32)[:8]
    reorder(pad_fc, np.argsort(hidden_order()), lambda t, value: out_fc.__setitem__((ALL, columns_of(t)), value))
    stores[3].start()
    for half in range(2):
        out_p[:, 384 * half : 384 * half + 384] = back_p[half].astype(F32)[:24]
    stores[4].start()
    back_first.collect(1)
    back_first.straight(2)
    back_small.collect(2)
    out_v[...] = view(sums, (2, 0), at, None)[...].astype(F32)
    stores[5].start()
    back_first.collect(2)
    rows = jnp.concatenate([view(sums, sub, at, None)[0] for sub in ATTENTION], axis=1)
    last_q[...] = dot_left_t(place_q[...], rows).astype(BF).reshape(8, 16, 384)
    receive(group_sends(last_q, back_q))
    for group in range(8):
        out_q[:, 384 * group : 384 * group + 384] = back_q[group].astype(F32)[:8]
    stores[2].start()

    mail.finish()
    to_heads_sent(2, d_att_t, landed_back)
    from_heads_sent(3, d_blocks, d_rows)
    for store in stores:
        store.wait()


def place_rows(groups, rows, padded):
    found = np.zeros((groups * rows, groups * padded), np.float32)
    for group in range(groups):
        for row in range(rows):
            found[group * rows + row, group * padded + row] = 1
    return found


def spread_matrix(entries, each):
    found = np.zeros((128, len(entries)), np.float32)
    found[entries % each, np.arange(len(entries))] = 1
    return found


def local(tokens, cotangent, w_qkv, w_out, w_fc, w_proj, gains, biases, fc_bias):
    order = hidden_order()
    placing = np.concatenate([place_rows(8, 6, 16), place_rows(2, 24, 32)], axis=1)
    spreads = np.concatenate([spread_matrix(np.arange(WIDTH), 6), spread_matrix(order, 24)], axis=1)
    given = (tokens, cotangent, w_qkv, w_out, w_fc, w_proj, gains, biases, fc_bias)
    given += (jnp.asarray(placing, BF), jnp.asarray(spreads, BF), jnp.asarray(order.reshape(1, HIDDEN), jnp.int32))
    results = ((128, WIDTH), (128, WIDTH), (8, HIDDEN), (8, HIDDEN), (24, WIDTH), (16, 128))
    scratch = [VMEM(item.shape, item.dtype) for item in given]
    scratch += [VMEM(shape, F32) for shape in results]
    scratch += [VMEM(shape, BF) for shape in SHAPES + SHAPES + SUMS + tuple(landing_shapes().values())]
    scratch += [
        VMEM((16, 2 * HIDDEN), F32),
        VMEM((8, HIDDEN), F32),
        VMEM((32, WIDTH), F32),
        VMEM((16, 128), F32),
        VMEM((8, 16, WIDTH), BF),
        VMEM((2, 32, 384), BF),
        pltpu.SemaphoreType.DMA((12,)),
        pltpu.SemaphoreType.DMA((6,)),
        VMEM((8, 16, WIDTH), BF),
        VMEM((2, 32, 384), BF),
        VMEM((8, 16, 384), BF),
        VMEM((8, 16, 384), BF),
        VMEM((2, 32, 384), BF),
        VMEM((8, 16, 384), BF),
        VMEM((8, 16, 384), BF),
        VMEM((2, 32, 384), BF),
        VMEM((128, WIDTH), BF),
        VMEM((16, WIDTH), F32),
        VMEM((1, HIDDEN), F32),
        VMEM((HEADS, 192, 128), BF),
        VMEM((192, 2048), BF),
        VMEM((192, 2048), BF),
        VMEM((2048, 128), BF),
        VMEM((64, 2048), F32),
        VMEM((8, 2048), F32),
        VMEM((16, 64, 128), BF),
        VMEM((HEADS, 64, 128), BF),
        VMEM((128, WIDTH), F32),
        VMEM((HEADS, 64, 128), BF),
        VMEM((64, 2048), BF),
        VMEM((64, 2048), BF),
        VMEM((2048, 128), BF),
        VMEM((192, 2048), BF),
        VMEM((2048, 128), F32),
        VMEM((16, 192, 128), BF),
        VMEM((HEADS, 192, 128), BF),
        VMEM((128, 3 * WIDTH), BF),
        VMEM((16, WIDTH), F32),
        VMEM((1, HIDDEN), F32),
        pltpu.SemaphoreType.DMA((IN_FLIGHT,)),
        pltpu.SemaphoreType.DMA((COPIES,)),
        pltpu.SemaphoreType.DMA((2, 16)),
        pltpu.SemaphoreType.DMA((2, 16)),
        pltpu.SemaphoreType.DMA((4,)),
    ]
    stay = pl.BlockSpec(memory_space=pl.ANY)
    found = pl.pallas_call(
        layer_kernel,
        out_shape=[jax.ShapeDtypeStruct(shape, F32) for shape in results],
        in_specs=[stay] * 12,
        out_specs=[stay] * 6,
        scratch_shapes=scratch,
        compiler_params=pltpu.CompilerParams(
            collective_id=0, has_side_effects=True, vmem_limit_bytes=VMEM_LIMIT * MEGA
        ),
        name="layer",
    )(*given)
    shapes = (
        (128, WIDTH), (128, WIDTH), (6, 1, 3 * WIDTH), (6, 1, WIDTH), (6, 1, HIDDEN), (24, WIDTH),
        (2, 6), (6, 1, 6), (1, 24),
    )
    parts = [shapes[i] for i in (2, 3, 4, 6, 7, 8)]
    final, input_grad, qkv, out, fc, proj, d_gains, d_biases, d_fc_bias = pl.pallas_call(
        results_kernel,
        out_shape=[jax.ShapeDtypeStruct(shape, F32) for shape in shapes],
        in_specs=[stay] * 6,
        out_specs=[stay] * 9,
        scratch_shapes=[VMEM(shape, F32) for shape in list(results) + parts]
        + [pltpu.SemaphoreType.DMA((6,)), pltpu.SemaphoreType.DMA((9,))],
        compiler_params=pltpu.CompilerParams(vmem_limit_bytes=VMEM_LIMIT * MEGA),
        name="results",
    )(*found)
    rows_first = lambda value: jnp.transpose(value, (1, 0, 2))
    return (
        final[None],
        input_grad[None],
        rows_first(qkv),
        rows_first(out),
        rows_first(fc),
        proj[None],
        d_gains[None],
        rows_first(d_biases),
        d_fc_bias,
    )


VMEM_LIMIT = 63


def solution(mesh):
    rows = P("dp", "ctx", None)
    weight = P(None, ("dp", "ctx"), None)
    vector = P(None, None, ("dp", "ctx"))
    tail = (weight,) * 4 + (vector, vector, P(None, ("dp", "ctx")))
    return jax.shard_map(
        local, mesh=mesh, in_specs=(rows, rows) + tail, out_specs=(rows, rows) + tail, check_vma=False
    )
```
